32 devices in a mesh: groups: 2 (over y), lanes: 4 (over z), heads: 2 (over x), rep: 2 (over core).
Axes of the slice: x: 2, y: 2, z: 4, core: 2. Of those that a mesh axis runs over, the one named last changes fastest.
Arguments:
- queries: bfloat16 [4096, 2048], P(('groups', 'lanes'), ('heads', 'rep')), parts along dimension 0, may hold values from -6 to 6
- span_states: bfloat16 [4096, 896], P(('groups', 'lanes')), parts along dimension 0, may hold values from -6 to 6
- store: bfloat16 [128, 128, 896], P(('groups', 'lanes'), ('heads', 'rep')), parts along dimension 0, may hold values from -480 to 480
- entry_ids: int32 [64, 2], P(('groups', 'lanes')), parts along dimension 0, may hold values from 0 to 15
- owners: int32 [64, 2], P(('groups', 'lanes')), parts along dimension 0, may hold values from 0 to 3, as said below
- w_key: bfloat16 [896, 2048], P(None, ('heads', 'rep')), may hold values from -0.1875 to 0.1875
- w_value: bfloat16 [896, 2048], P(None, ('heads', 'rep')), may hold values from -0.1875 to 0.1875
- w_out: bfloat16 [2048, 4096], P(('heads', 'rep')), may hold values from -0.125 to 0.125
Outputs:
- attended: bfloat16 [4096, 4096], P(('groups', 'lanes', 'heads', 'rep')), parts along dimension 0
The draws below stay inside these ranges and needn't reach their ends.
There are 2 independent parts, one for each index of `groups`. The reference program is written for one: setup_inputs(seed, part) draws one part's arguments, and reference() takes and returns one part's arrays. A program takes and returns all parts, laid end to end along the dimension named above; an argument that names none is the same for every part. Nothing has to cross between parts.
Inputs may be any that keep to these rules, and one draw needn't show every extreme that they name: Among the 16 neighbours of one lane's spans at most 4 have the same owner, the 2 owners of a span differ, and in every draw one owner holds 4 neighbours of every lane.
All inputs are finite; a program needn't handle non-finite values.
Results may differ from the reference program's by a relative error of at most 0.014.
The reference program's roundings to bfloat16 on the way count: a program that leaves them out, or rounds other values in their place, can miss the bound.
Values may be sent and summed in bfloat16 or wider, within the bound.
No kernel may reach another device: no remote copies, remote signals or barrier semaphores. Data moves between devices by JAX's collectives and lax.ppermute only.
A program may use at most 128 MiB of HBM per device.

```python
import jax
import jax.numpy as jnp
from jax import lax

D = 4096
H = 16
HD = 128
E = 896
ENCODER_HEAD_DIM = 128
CL = 64
K = 2
NT = 128
CHD = 8
ENT_DEV = 16
SPANS = 32
TOKENS = 2048
ENTRIES = 64
CAP = 4
N_LANES = 4
N_HEADS = 2
N_REP = 2


def lane_permutation(lane_key):
    return jax.random.permutation(lane_key, N_LANES - 1)


def span_reordering(lane_key):
    return jax.random.permutation(lane_key, CHD)


def draw_owners(key, part):
    base = jax.random.fold_in(key, 7)
    hot_key, perm_key, row_key = jax.random.split(base, 3)
    hottest = jax.random.randint(hot_key, (), 0, N_LANES).astype(jnp.int32)
    others = jax.vmap(lane_permutation)(jax.random.split(perm_key, N_LANES)).astype(jnp.int32)
    others = others + (others >= hottest).astype(jnp.int32)
    position = jnp.arange(K * CHD, dtype=jnp.int32)
    group_index = jnp.maximum(position - CAP, 0) // CAP
    picked = jnp.take(others, group_index, axis=1)
    layout_plan = jnp.where(position[None, :] < CAP, hottest, picked).reshape(N_LANES, K, CHD)
    shuffle = jax.vmap(span_reordering)(jax.random.split(row_key, N_LANES)).astype(jnp.int32)
    shuffled = jnp.take_along_axis(layout_plan, shuffle[:, None, :], axis=2)
    return jnp.transpose(shuffled, (0, 2, 1)).reshape(SPANS, K).astype(jnp.int32)


def draw_store(key, part):
    base = jax.random.fold_in(key, 3)
    value_key = jax.random.fold_in(base, 0)
    values = jnp.clip(jax.random.normal(value_key, (ENTRIES, NT, E), jnp.float32), -6.0, 6.0)
    return values.astype(jnp.bfloat16)


def plant(drawn, stream_key, least, top_value):
    longest = drawn.shape.index(max(drawn.shape))
    spots = []
    for shift in (0, 1):
        where = [jax.random.randint(jax.random.fold_in(stream_key, axis), (), 0, length) for axis, length in enumerate(drawn.shape)]
        where[longest] = (where[longest] + shift) % drawn.shape[longest]
        spots.append(tuple(where))
    return drawn.at[spots[0]].set(least).at[spots[1]].set(top_value)


def block_scale(rng, extent, shards, smallest, high):
    def one(dim, blocks):
        steps = jax.random.uniform(jax.random.fold_in(jax.random.fold_in(rng, 6), dim), (blocks,), jnp.float32, smallest / len(shards), high / len(shards))
        return jnp.repeat(jnp.exp(steps), extent[dim] // blocks).reshape((-1,) + (1,) * (len(extent) - dim - 1))

    level = one(*shards[0])
    for cut in shards[1:]:
        level = level * one(*cut)
    return level


def gaussian(key, shape, scale, bound, cuts=(), kind=jnp.bfloat16):
    values = jax.random.normal(key, shape, jnp.float32) * scale
    if len(cuts) > 0:
        values = block_scale(key, shape, cuts, -0.22, 0.18) * values
    return jnp.clip(values, min=-bound, max=bound).astype(kind)


def setup_inputs(seed: int = 0, part: int = 0) -> dict:
    seeds = jax.random.split(jax.random.key(seed), 9)
    part_keys = jax.random.split(jax.random.fold_in(seeds[8], part), 9)
    return {
        "queries": gaussian(part_keys[0], (TOKENS, H * HD), 1.0, 6.0, ((0, 4), (1, 4))),
        "span_states": gaussian(part_keys[1], (TOKENS, E), 1.0, 6.0, ((0, 4),)),
        "store": draw_store(jax.random.fold_in(jax.random.fold_in(seeds[8], part), 71), part),
        "entry_ids": plant(jax.random.randint(part_keys[3], (SPANS, K), 0, ENT_DEV), jax.random.fold_in(part_keys[3], 1), 0, ENT_DEV - 1).astype(jnp.int32),
        "owners": draw_owners(jax.random.fold_in(jax.random.fold_in(seeds[8], part), 71), part),
        "w_key": gaussian(seeds[5], (E, H * HD), E ** -0.5, 0.1875, ((1, 4),)),
        "w_value": gaussian(seeds[6], (E, H * HD), E ** -0.5, 0.1875, ((1, 4),)),
        "w_out": gaussian(seeds[7], (H * HD, D), (H * HD) ** -0.5, 0.125, ((0, 4),)),
    }


def reference(queries, span_states, store, entry_ids, owners, w_key, w_value, w_out):
    global_rows = (owners * ENT_DEV + entry_ids).astype(jnp.int32)
    enc_heads = E // ENCODER_HEAD_DIM

    def one_span(span_item):
        query_rows, state_rows, chosen = span_item
        tokens = jnp.take(store, chosen, axis=0).reshape(K * NT, E).astype(jnp.float32)
        states = state_rows.astype(jnp.float32)
        token_head_rows = tokens.reshape(K * NT, enc_heads, ENCODER_HEAD_DIM)
        head_states = states.reshape(CL, enc_heads, ENCODER_HEAD_DIM)
        score_logits = jnp.einsum("qil,bil->iqb", token_head_rows, head_states) * (ENCODER_HEAD_DIM ** -0.5)
        attention_result = lax.optimization_barrier(jax.nn.softmax(score_logits, axis=-1).astype(jnp.bfloat16))
        attention_result = attention_result.astype(jnp.float32)
        mixed_input = jnp.einsum("cni,icx->ncx", attention_result, head_states)
        encoded = (tokens + mixed_input.reshape(K * NT, E)).astype(jnp.bfloat16)
        key_rows = jnp.dot(encoded, w_key, preferred_element_type=jnp.float32).astype(jnp.bfloat16)
        value_rows = jnp.dot(encoded, w_value, preferred_element_type=jnp.float32).astype(jnp.bfloat16)
        query_heads = query_rows.astype(jnp.float32).reshape(CL, H, HD)
        key_heads = key_rows.astype(jnp.float32).reshape(K * NT, H, HD)
        value_heads = value_rows.astype(jnp.float32).reshape(K * NT, H, HD)
        scores = jnp.einsum("qhd,khd->hqk", query_heads, key_heads) * (HD ** -0.5)
        softmax_rows = lax.optimization_barrier(jax.nn.softmax(scores, axis=-1).astype(jnp.bfloat16))
        softmax_rows = softmax_rows.astype(jnp.float32)
        result = jnp.einsum("hqk,khd->qhd", softmax_rows, value_heads)
        return result.reshape(CL, H * HD).astype(jnp.bfloat16)

    heads_out = lax.map(one_span, (queries.reshape(SPANS, CL, H * HD), span_states.reshape(SPANS, CL, E), global_rows))
    heads_out = heads_out.reshape(TOKENS, H * HD)
    groups = N_HEADS * N_REP
    group_width = (H * HD) // groups
    pieces = jnp.transpose(heads_out.reshape(TOKENS, groups, group_width), (1, 0, 2))
    weights = w_out.reshape(groups, group_width, D)

    def add_group(running, operands):
        partial_value = jnp.dot(operands[0], operands[1], preferred_element_type=jnp.float32).astype(jnp.bfloat16)
        partial_value = lax.optimization_barrier(partial_value)
        return running + partial_value.astype(jnp.float32), None

    running, unused = lax.scan(add_group, jnp.zeros((TOKENS, D), jnp.float32), (pieces, weights))
    return running.astype(jnp.bfloat16)
```

```python
import functools

import jax
import jax.numpy as jnp
from jax import lax
from jax.experimental import pallas as pl
from jax.experimental.pallas import tpu as pltpu
from jax.sharding import PartitionSpec as P

HD = 128
ENCODER_HEAD_DIM = 128
F32 = jnp.float32
BF16 = jnp.bfloat16
LATER_GROUPS = 3
FIRST_COLS = 1024

VMEM = pl.BlockSpec(memory_space=pltpu.VMEM)
SMEM = pl.BlockSpec(memory_space=pltpu.SMEM)
ANY = pl.BlockSpec(memory_space=pl.ANY)


def params(mib):
    return pltpu.CompilerParams(vmem_limit_bytes=mib * 2**20)


def cost(flops, bytes_accessed):
    return pl.CostEstimate(flops=int(flops), bytes_accessed=int(bytes_accessed), transcendentals=0)


def apart(n, a, b):
    if n & (n - 1) == 0:
        return a ^ b
    return lax.rem(b - a + n, n)


def lane_pairs(n, d, reply):
    if n & (n - 1) == 0:
        return [(i, i ^ d) for i in range(n)]
    return [(i, (i - d if reply else i + d) % n) for i in range(n)]


def shift_pairs(n, s):
    return [(i, (i + s) % n) for i in range(n)]


def dot_t(a, b):
    return lax.dot_general(a, b, (((1,), (1,)), ((), ())), preferred_element_type=F32)


def dot(a, b):
    return jnp.dot(a, b, preferred_element_type=F32)


def plan_kernel(n_lanes, cap, owners_ref, entries_ref, want_ref, req_ref, slot_ref, count_ref):
    lane = lax.axis_index("lanes")
    fanout, spans = owners_ref.shape
    for i in range(n_lanes):
        count_ref[i] = 0
    for i in range(n_lanes * cap):
        want_ref[i] = 0
        req_ref[i] = 0
    for j in range(fanout * spans):
        d = apart(n_lanes, lane, owners_ref[j % fanout, j // fanout])
        rank = count_ref[d]
        count_ref[d] = rank + 1
        slot = d * cap + rank
        want_ref[slot] = entries_ref[j % fanout, j // fanout]
        req_ref[slot] = j
        slot_ref[j] = slot


def plan(owners, entry_ids, n_lanes, cap):
    requests = owners.size
    table = jax.ShapeDtypeStruct((n_lanes * cap,), jnp.int32)
    return pl.pallas_call(
        functools.partial(plan_kernel, n_lanes, cap),
        out_shape=(table, table, jax.ShapeDtypeStruct((requests,), jnp.int32)),
        in_specs=[SMEM, SMEM],
        out_specs=(SMEM, SMEM, SMEM),
        scratch_shapes=[pltpu.SMEM((n_lanes,), jnp.int32)],
        name="plan",
    )(owners.T, entry_ids.T)


def fetch_kernel(n_lanes, cap, *refs):
    others = n_lanes - 1
    asked, store_ref, outs, sem = refs[:others], refs[others], refs[others + 1 : -1], refs[-1]
    copies = []
    for d in range(1, n_lanes):
        for s in range(cap):
            entry = asked[d - 1][d * cap + s]
            copies.append(
                pltpu.make_async_copy(store_ref.at[entry], outs[d - 1].at[s], sem.at[(d - 1) * cap + s])
            )
    for copy in copies:
        copy.start()
    for copy in copies:
        copy.wait()


def fetch(asked, store, n_lanes, cap):
    block = jax.ShapeDtypeStruct((cap,) + store.shape[1:], store.dtype)
    others = n_lanes - 1
    return pl.pallas_call(
        functools.partial(fetch_kernel, n_lanes, cap),
        out_shape=[block] * others,
        in_specs=[SMEM] * others + [ANY],
        out_specs=[ANY] * others,
        scratch_shapes=[pltpu.SemaphoreType.DMA((others * cap,))],
        cost_estimate=cost(0, 2 * others * cap * store[0].size * 2),
        name="fetch",
    )(*asked, store)


def encode_slot(tokens, states):
    pieces = []
    for h in range(tokens.shape[1] // ENCODER_HEAD_DIM):
        cols = slice(h * ENCODER_HEAD_DIM, (h + 1) * ENCODER_HEAD_DIM)
        token, state = tokens[:, cols], states[:, cols]
        logits = dot_t(token, state) * ENCODER_HEAD_DIM ** (-0.5)
        weights = jnp.exp(logits - jnp.max(logits, axis=1, keepdims=True))
        weights = weights / jnp.sum(weights, axis=1, keepdims=True)
        mixed = dot(weights.astype(BF16), state)
        pieces.append((token.astype(F32) + mixed).astype(BF16))
    return jnp.concatenate(pieces, axis=1)


def encode_kernel(first, cap, fanout, span_len, req_ref, states_ref, *refs):
    blocks, out_ref = refs[:-1], refs[-1]
    for i, block in enumerate(blocks):
        for s in range(cap):
            span = lax.div(req_ref[(first + i) * cap + s], fanout)
            rows = pl.ds(pl.multiple_of(span * span_len, span_len), span_len)
            out_ref[i * cap + s] = encode_slot(block[s], states_ref[rows, :])


def encode_local_kernel(cap, fanout, span_len, req_ref, want_ref, states_ref, store_ref, out_ref, tokens_ref, sem):
    copies = [
        pltpu.make_async_copy(store_ref.at[want_ref[s]], tokens_ref.at[s], sem.at[s]) for s in range(cap)
    ]
    for copy in copies:
        copy.start()
    for s, copy in enumerate(copies):
        span = lax.div(req_ref[s], fanout)
        rows = pl.ds(pl.multiple_of(span * span_len, span_len), span_len)
        copy.wait()
        out_ref[s] = encode_slot(tokens_ref[s], states_ref[rows, :])


def encode_cost(slots, tokens, span_len, width):
    return cost(4 * slots * tokens * span_len * width, 4 * slots * tokens * width + 1024 * width)


def encode_local(plans, span_states, store, cap, fanout, span_len):
    want, req, _ = plans
    shape = (cap,) + store.shape[1:]
    return pl.pallas_call(
        functools.partial(encode_local_kernel, cap, fanout, span_len),
        out_shape=jax.ShapeDtypeStruct(shape, BF16),
        in_specs=[SMEM, SMEM, VMEM, ANY],
        out_specs=VMEM,
        scratch_shapes=[pltpu.VMEM(shape, BF16), pltpu.SemaphoreType.DMA((cap,))],
        compiler_params=params(16),
        cost_estimate=encode_cost(cap, store.shape[1], span_len, store.shape[2]),
        name="encode_local",
    )(req, want, span_states, store)


def encode(plans, span_states, blocks, first, cap, fanout, span_len):
    req = plans[1]
    _, tokens, width = blocks[0].shape
    slots = len(blocks) * cap
    return pl.pallas_call(
        functools.partial(encode_kernel, first, cap, fanout, span_len),
        out_shape=jax.ShapeDtypeStruct((slots, tokens, width), BF16),
        in_specs=[SMEM, VMEM] + [VMEM] * len(blocks),
        out_specs=VMEM,
        compiler_params=params(16),
        cost_estimate=encode_cost(slots, tokens, span_len, width),
        name="encode",
    )(req, span_states, *blocks)


def project_into(kv_ref, first, pieces, wk_ref, wv_ref):
    slots, tokens, width = pieces[0].shape
    rows = jnp.concatenate([piece[...].reshape(slots * tokens, width) for piece in pieces], axis=0)
    cols = wk_ref.shape[1]
    for side, weight in enumerate((wk_ref, wv_ref)):
        made = dot(rows, weight[...]).astype(BF16)
        for p in range(len(pieces)):
            part = made[p * slots * tokens : (p + 1) * slots * tokens]
            kv_ref[first : first + slots, p, :, side * cols : (side + 1) * cols] = part.reshape(
                slots, tokens, cols
            )


def project_kernel(n_pieces, *refs):
    pieces, (wk_ref, wv_ref, kv_ref) = refs[:n_pieces], refs[n_pieces:]
    project_into(kv_ref, 0, pieces, wk_ref, wv_ref)


def project_cost(pieces, w_key):
    rows = len(pieces) * pieces[0].shape[0] * pieces[0].shape[1]
    width, cols = w_key.shape
    return 4 * rows * width * cols, 2 * rows * (width + 2 * cols) + 4 * width * cols


def project(pieces, w_key, w_value):
    slots, tokens, _ = pieces[0].shape
    shape = (slots, len(pieces), tokens, 2 * w_key.shape[1])
    return pl.pallas_call(
        functools.partial(project_kernel, len(pieces)),
        out_shape=jax.ShapeDtypeStruct(shape, BF16),
        in_specs=[VMEM] * (len(pieces) + 2),
        out_specs=VMEM,
        compiler_params=params(32),
        cost_estimate=cost(*project_cost(pieces, w_key)),
        name="project",
    )(*pieces, w_key, w_value)


def attend_kernel(firsts, n_pieces, n_heads, n_rep, fanout, spans, slot_ref, q_ref, *refs):
    n_ready = len(firsts) - 1
    ready, refs = refs[:n_ready], refs[n_ready:]
    pieces, refs = refs[:n_pieces], refs[n_pieces:]
    wk_ref, wv_ref = refs[:2]
    outs = refs[2 : 2 + n_rep]
    kv_ref, sem = refs[2 + n_rep :]
    copies = [
        pltpu.make_async_copy(ref, kv_ref.at[pl.ds(first, ref.shape[0])], sem.at[i])
        for i, (ref, first) in enumerate(zip(ready, firsts))
    ]
    for copy in copies:
        copy.start()
    project_into(kv_ref, firsts[-1], pieces, wk_ref, wv_ref)
    for copy in copies:
        copy.wait()
    heads_at, rep_at = lax.axis_index("heads"), lax.axis_index("rep")
    cols_all = wk_ref.shape[1]
    span_len = q_ref.shape[0] // spans
    block = spans // (n_heads * n_rep)
    tokens = kv_ref.shape[1] * kv_ref.shape[2]
    for t in reversed(range(n_heads)):
        for s in range(n_rep):
            owner = lax.rem(heads_at + t, n_heads) * n_rep + lax.rem(rep_at + s, n_rep)
            for i in range(block):
                span = owner * block + i
                slots = [slot_ref[span * fanout + k] for k in range(fanout)]
                rows = pl.ds(pl.multiple_of(span * span_len, span_len), span_len)
                for h in range(cols_all // HD):
                    key_cols = slice(h * HD, (h + 1) * HD)
                    value_cols = slice(cols_all + h * HD, cols_all + (h + 1) * HD)
                    query = q_ref[rows, key_cols]
                    keys = [kv_ref[slot, :, :, key_cols].reshape(tokens, HD) for slot in slots]
                    values = [kv_ref[slot, :, :, value_cols].reshape(tokens, HD) for slot in slots]
                    logits = [dot_t(query, key) * HD ** (-0.5) for key in keys]
                    top = functools.reduce(
                        jnp.maximum, [jnp.max(part, axis=1, keepdims=True) for part in logits]
                    )
                    weights = [jnp.exp(part - top) for part in logits]
                    total = sum(jnp.sum(part, axis=1, keepdims=True) for part in weights)
                    mixed = sum(dot(part.astype(BF16), value) for part, value in zip(weights, values))
                    outs[s][t, i * span_len : (i + 1) * span_len, key_cols] = (mixed / total).astype(BF16)


def attend(plans, queries, ready, pieces, w_key, w_value, n_heads, n_rep, fanout, spans):
    firsts = [0]
    for kv in ready:
        firsts.append(firsts[-1] + kv.shape[0])
    slots, tokens, _ = pieces[0].shape
    cols = w_key.shape[1]
    rows = queries.shape[0] // (n_heads * n_rep)
    flops, moved = project_cost(pieces, w_key)
    all_slots = firsts[-1] + slots
    kv_shape = (all_slots, len(pieces), tokens, 2 * cols)
    return pl.pallas_call(
        functools.partial(attend_kernel, firsts, len(pieces), n_heads, n_rep, fanout, spans),
        out_shape=[jax.ShapeDtypeStruct((n_heads, rows, cols), BF16)] * n_rep,
        in_specs=[SMEM, VMEM] + [ANY] * len(ready) + [VMEM] * (len(pieces) + 2),
        out_specs=[VMEM] * n_rep,
        scratch_shapes=[pltpu.VMEM(kv_shape, BF16), pltpu.SemaphoreType.DMA((max(1, len(ready)),))],
        compiler_params=params(40),
        cost_estimate=cost(
            flops + 4 * queries.size * fanout * len(pieces) * tokens,
            moved + 2 * all_slots * len(pieces) * tokens * 2 * cols + 4 * queries.size,
        ),
        name="attend",
    )(plans[2], queries, *ready, *pieces, w_key, w_value)


def out_kernel(n_rep, *refs):
    mixed, weights, out_ref = refs[:n_rep], refs[n_rep:-1], refs[-1]
    out_ref[...] = sum(dot(a[0], w[...]) for a, w in zip(mixed, weights)).astype(BF16)


def out_project(mixed, weights, t, start, stop, tile):
    _, rows, depth = mixed[0].shape
    base = start // tile
    return pl.pallas_call(
        functools.partial(out_kernel, len(mixed)),
        grid=((stop - start) // tile,),
        out_shape=jax.ShapeDtypeStruct((rows, stop - start), BF16),
        in_specs=[pl.BlockSpec((1, rows, depth), lambda j: (t, 0, 0))] * len(mixed)
        + [pl.BlockSpec((depth, tile), lambda j: (0, base + j))] * len(mixed),
        out_specs=pl.BlockSpec((rows, tile), lambda j: (0, j)),
        compiler_params=params(16),
        cost_estimate=cost(
            2 * len(mixed) * rows * depth * (stop - start), 2 * len(mixed) * depth * (stop - start)
        ),
        name="out_project",
    )(*mixed, *weights)


def shards(queries, span_states, store, entry_ids, owners, w_key, w_value, w_out):
    n_lanes, n_heads, n_rep = (lax.axis_size(name) for name in ("lanes", "heads", "rep"))
    spans, fanout = entry_ids.shape
    requests = spans * fanout
    cap = max(2, (requests + n_lanes - 1) // n_lanes)
    span_len = queries.shape[0] // spans

    plans = plan(owners, entry_ids, n_lanes, cap)
    asked = [lax.ppermute(plans[0], "lanes", lane_pairs(n_lanes, d, False)) for d in range(1, n_lanes)]
    w_outs = [w_out] + [lax.ppermute(w_out, "rep", shift_pairs(n_rep, s)) for s in range(1, n_rep)]

    def gather(encoded):
        pieces = [encoded]
        pieces += [lax.ppermute(encoded, "heads", shift_pairs(n_heads, s)) for s in range(1, n_heads)]
        return pieces + [
            lax.ppermute(piece, "rep", shift_pairs(n_rep, s)) for piece in pieces for s in range(1, n_rep)
        ]

    groups = [gather(encode_local(plans, span_states, store, cap, fanout, span_len))]
    fetched = fetch(asked, store, n_lanes, cap)
    arrived = [
        lax.ppermute(fetched[d - 1], "lanes", lane_pairs(n_lanes, d, True)) for d in range(1, n_lanes)
    ]
    size = -(-(n_lanes - 1) // LATER_GROUPS)
    for first in range(1, n_lanes, size):
        blocks = arrived[first - 1 : first - 1 + size]
        groups.append(gather(encode(plans, span_states, blocks, first, cap, fanout, span_len)))
    ready = [project(pieces, w_key, w_value) for pieces in groups[:-1]]
    mixed = attend(plans, queries, ready, groups[-1], w_key, w_value, n_heads, n_rep, fanout, spans)
    mixed = [mixed[0]] + [lax.ppermute(mixed[s], "rep", shift_pairs(n_rep, s)) for s in range(1, n_rep)]

    width = w_out.shape[1]
    tile = min(FIRST_COLS, width)
    cuts = [0, tile, width] if tile < width else [0, width]
    received = []
    for t in range(1, n_heads):
        parts = []
        for start, stop in zip(cuts, cuts[1:]):
            partial = out_project(mixed, w_outs, t, start, stop, tile)
            parts.append(lax.ppermute(partial, "heads", shift_pairs(n_heads, t)))
        received.append(jnp.concatenate(parts, axis=1))
    total = out_project(mixed, w_outs, 0, 0, width, tile).astype(F32)
    for part in received:
        total = total + part.astype(F32)
    return total.astype(BF16)


def solution(mesh):
    return jax.shard_map(
        shards,
        mesh=mesh,
        in_specs=(
            P(("groups", "lanes"), ("heads", "rep")),
            P(("groups", "lanes"), None),
            P(("groups", "lanes"), ("heads", "rep"), None),
            P(("groups", "lanes"), None),
            P(("groups", "lanes"), None),
            P(None, ("heads", "rep")),
            P(None, ("heads", "rep")),
            P(("heads", "rep"), None),
        ),
        out_specs=P(("groups", "lanes", "heads", "rep"), None),
        check_vma=False,
    )
```

```python
import functools

import jax
import jax.numpy as jnp
from jax import lax
from jax.experimental import pallas as pl
from jax.experimental.pallas import tpu as pltpu
from jax.sharding import PartitionSpec as P

HD = 128
ENCODER_HEAD_DIM = 128
F32 = jnp.float32
BF16 = jnp.bfloat16
GROUPS = 4
FIRST_COLS = 1024

VMEM = pl.BlockSpec(memory_space=pltpu.VMEM)
SMEM = pl.BlockSpec(memory_space=pltpu.SMEM)
ANY = pl.BlockSpec(memory_space=pl.ANY)


def params(mib):
    return pltpu.CompilerParams(vmem_limit_bytes=mib * 2**20)


def cost(flops, bytes_accessed):
    return pl.CostEstimate(flops=int(flops), bytes_accessed=int(bytes_accessed), transcendentals=0)


def apart(n, a, b):
    if n & (n - 1) == 0:
        return a ^ b
    return lax.rem(b - a + n, n)


def lane_pairs(n, d, reply):
    if n & (n - 1) == 0:
        return [(i, i ^ d) for i in range(n)]
    return [(i, (i - d if reply else i + d) % n) for i in range(n)]


def shift_pairs(n, s):
    return [(i, (i + s) % n) for i in range(n)]


def dot_t(a, b):
    return lax.dot_general(a, b, (((1,), (1,)), ((), ())), preferred_element_type=F32)


def dot(a, b):
    return jnp.dot(a, b, preferred_element_type=F32)


def fetch_kernel(n_lanes, cap, own_ref, *refs):
    asked, store_ref, refs = refs[: n_lanes - 1], refs[n_lanes - 1], refs[n_lanes:]
    blocks, (req_ref, slot_ref, pick_ref, count_ref) = refs[:n_lanes], refs[n_lanes:]
    lane = lax.axis_index("lanes")
    fanout, spans = own_ref.shape[0] // 2, own_ref.shape[1]
    requests = [(j // fanout, j % fanout) for j in range(fanout * spans)]
    for i in range(n_lanes):
        count_ref[i] = 0
    for i in range(n_lanes * cap):
        pick_ref[i] = 0
        req_ref[i] = 0
    for j, (span, k) in enumerate(requests):
        d = apart(n_lanes, lane, own_ref[k, span])
        rank = count_ref[d]
        count_ref[d] = rank + 1
        slot = d * cap + rank
        pick_ref[slot] = own_ref[fanout + k, span]
        req_ref[slot] = j
        slot_ref[j] = slot
    for d in range(1, n_lanes):
        place = d * cap
        for span, k in requests:
            pick_ref[place] = asked[d - 1][fanout + k, span]
            place = place + (asked[d - 1][k, span] == lane).astype(jnp.int32)
    for d in list(range(1, n_lanes)) + [0]:
        for s in range(cap):
            blocks[d][s] = store_ref[pick_ref[d * cap + s]]


def fetch(own, asked, store, n_lanes, cap):
    block = jax.ShapeDtypeStruct((cap,) + store.shape[1:], store.dtype)
    requests = own.size // 2
    tables = (
        jax.ShapeDtypeStruct((n_lanes * cap,), jnp.int32),
        jax.ShapeDtypeStruct((requests,), jnp.int32),
    )
    return pl.pallas_call(
        functools.partial(fetch_kernel, n_lanes, cap),
        out_shape=[block] * n_lanes + list(tables),
        in_specs=[SMEM] * n_lanes + [VMEM],
        out_specs=[VMEM] * n_lanes + [SMEM, SMEM],
        scratch_shapes=[pltpu.SMEM((n_lanes * cap + 1,), jnp.int32), pltpu.SMEM((n_lanes,), jnp.int32)],
        compiler_params=params(16),
        cost_estimate=cost(0, 2 * store.size + 2 * n_lanes * cap * store[0].size),
        name="fetch",
    )(own, *asked, store)


def encode_pairs(width):
    step = 2 * ENCODER_HEAD_DIM
    return [(start, min(start + step, width)) for start in range(0, width, step)]


def spread(states, start, stop):
    part = states[:, start:stop]
    heads = (stop - start) // ENCODER_HEAD_DIM
    if heads == 1:
        return part
    rows = jnp.concatenate([part] * heads, axis=0)
    return jnp.where(own_cells(rows.shape, part.shape[0]), rows, jnp.zeros_like(rows))


def own_cells(shape, keys):
    row = lax.broadcasted_iota(jnp.int32, shape, 0)
    col = lax.broadcasted_iota(jnp.int32, shape, 1)
    return (row >= keys) == (col >= ENCODER_HEAD_DIM)


def softmax_top(logits, keys):
    if logits.shape[1] == keys:
        return jnp.max(logits, axis=1, keepdims=True)
    first = lax.broadcasted_iota(jnp.int32, logits.shape, 1) < keys
    low = jnp.max(jnp.where(first, logits, -jnp.inf), axis=1, keepdims=True)
    high = jnp.max(jnp.where(first, -jnp.inf, logits), axis=1, keepdims=True)
    return jnp.where(first, low, high)


def encode_kernel(first, cap, fanout, span_len, req_ref, states_ref, *refs):
    blocks, out_ref = refs[:-1], refs[-1]
    scale = ENCODER_HEAD_DIM ** (-0.5)
    runs = encode_pairs(states_ref.shape[1])
    for i, block in enumerate(blocks):
        units = []
        for s in range(cap):
            span = lax.div(req_ref[(first + i) * cap + s], fanout)
            states = states_ref[pl.ds(pl.multiple_of(span * span_len, span_len), span_len), :]
            units += [(s, start, stop, spread(states, start, stop)) for start, stop in runs]
        logits = [dot_t(block[s, :, start:stop], keys) for s, start, stop, keys in units]
        tops = [softmax_top(part, span_len) for part in logits]
        weights = [jnp.exp((part - top) * scale).astype(BF16) for part, top in zip(logits, tops)]
        mixed = [dot(part, keys) for part, (_, _, _, keys) in zip(weights, units)]
        sums = []
        for part, (_, start, stop, keys) in zip(weights, units):
            ones = jnp.ones(keys.shape, BF16)
            if stop - start > ENCODER_HEAD_DIM:
                ones = jnp.where(own_cells(keys.shape, span_len), ones, jnp.zeros_like(ones))
            sums.append(dot(part, ones))
        for (s, start, stop, _), top, bottom in zip(units, mixed, sums):
            token = block[s, :, start:stop].astype(F32)
            out_ref[i * cap + s, :, start:stop] = (token + top / bottom).astype(BF16)


def encode(req, span_states, blocks, first, cap, fanout, span_len):
    _, tokens, width = blocks[0].shape
    slots = len(blocks) * cap
    return pl.pallas_call(
        functools.partial(encode_kernel, first, cap, fanout, span_len),
        out_shape=jax.ShapeDtypeStruct((slots, tokens, width), BF16),
        in_specs=[SMEM, VMEM] + [VMEM] * len(blocks),
        out_specs=VMEM,
        compiler_params=params(16),
        cost_estimate=cost(16 * slots * tokens * span_len * width, 4 * slots * tokens * width),
        name="encode",
    )(req, span_states, *blocks)


def project_into(kv_ref, first, pieces, wk_ref, wv_ref):
    slots, tokens, width = pieces[0].shape
    rows = jnp.concatenate([piece[...].reshape(slots * tokens, width) for piece in pieces], axis=0)
    cols = wk_ref.shape[1]
    for side, weight in enumerate((wk_ref, wv_ref)):
        made = dot(rows, weight[...]).astype(BF16)
        for p in range(len(pieces)):
            part = made[p * slots * tokens : (p + 1) * slots * tokens]
            kv_ref[first : first + slots, p, :, side * cols : (side + 1) * cols] = part.reshape(
                slots, tokens, cols
            )


def project_kernel(n_pieces, *refs):
    pieces, (wk_ref, wv_ref, kv_ref) = refs[:n_pieces], refs[n_pieces:]
    project_into(kv_ref, 0, pieces, wk_ref, wv_ref)


def project_cost(pieces, w_key):
    rows = len(pieces) * pieces[0].shape[0] * pieces[0].shape[1]
    width, cols = w_key.shape
    return 4 * rows * width * cols, 2 * rows * (width + 2 * cols) + 4 * width * cols


def project(pieces, w_key, w_value):
    slots, tokens, _ = pieces[0].shape
    shape = (slots, len(pieces), tokens, 2 * w_key.shape[1])
    return pl.pallas_call(
        functools.partial(project_kernel, len(pieces)),
        out_shape=jax.ShapeDtypeStruct(shape, BF16),
        in_specs=[VMEM] * (len(pieces) + 2),
        out_specs=VMEM,
        compiler_params=params(32),
        cost_estimate=cost(*project_cost(pieces, w_key)),
        name="project",
    )(*pieces, w_key, w_value)


def attend_kernel(firsts, n_pieces, n_heads, n_rep, turns, fanout, spans, slot_ref, q_ref, *refs):
    n_ready = len(firsts) - 1
    ready, refs = refs[:n_ready], refs[n_ready:]
    pieces, refs = refs[:n_pieces], refs[n_pieces:]
    wk_ref, wv_ref = refs[:2]
    outs = refs[2 : 2 + n_rep]
    kv_ref, sem = refs[2 + n_rep :]
    copies = [
        pltpu.make_async_copy(ref, kv_ref.at[pl.ds(first, ref.shape[0])], sem.at[i])
        for i, (ref, first) in enumerate(zip(ready, firsts))
    ]
    for copy in copies:
        copy.start()
    project_into(kv_ref, firsts[-1], pieces, wk_ref, wv_ref)
    for copy in copies:
        copy.wait()
    heads_at, rep_at = lax.axis_index("heads"), lax.axis_index("rep")
    cols = wk_ref.shape[1]
    span_len = q_ref.shape[0] // spans
    block = spans // (n_heads * n_rep)
    tokens = kv_ref.shape[1] * kv_ref.shape[2]
    heads = [slice(h * HD, (h + 1) * HD) for h in range(cols // HD)]
    for at, t in enumerate(turns):
        for s in range(n_rep):
            owner = lax.rem(heads_at + t, n_heads) * n_rep + lax.rem(rep_at + s, n_rep)
            for i in range(block):
                span = owner * block + i
                slots = [slot_ref[span * fanout + k] for k in range(fanout)]
                rows = pl.ds(pl.multiple_of(span * span_len, span_len), span_len)

                def side(lanes):
                    return jnp.concatenate(
                        [kv_ref[slot, :, :, lanes].reshape(tokens, HD) for slot in slots], axis=0
                    )

                logits = [dot_t(q_ref[rows, lanes], side(lanes)) for lanes in heads]
                tops = [jnp.max(part, axis=1, keepdims=True) for part in logits]
                weights = [jnp.exp((part - top) * HD ** (-0.5)) for part, top in zip(logits, tops)]
                scales = [1.0 / jnp.sum(part, axis=1, keepdims=True) for part in weights]
                mixed = [
                    dot(part.astype(BF16), side(slice(cols + lanes.start, cols + lanes.stop)))
                    for part, lanes in zip(weights, heads)
                ]
                for part, scale, lanes in zip(mixed, scales, heads):
                    outs[s][at, i * span_len : (i + 1) * span_len, lanes] = (part * scale).astype(BF16)


def attend(slot, queries, ready, pieces, w_key, w_value, n_heads, n_rep, turns, fanout, spans):
    firsts = [0]
    for kv in ready:
        firsts.append(firsts[-1] + kv.shape[0])
    slots, tokens, _ = pieces[0].shape
    cols = w_key.shape[1]
    rows = queries.shape[0] // (n_heads * n_rep)
    flops, moved = project_cost(pieces, w_key)
    all_slots = firsts[-1] + slots
    kv_shape = (all_slots, len(pieces), tokens, 2 * cols)
    return pl.pallas_call(
        functools.partial(attend_kernel, firsts, len(pieces), n_heads, n_rep, turns, fanout, spans),
        out_shape=[jax.ShapeDtypeStruct((len(turns), rows, cols), BF16)] * n_rep,
        in_specs=[SMEM, VMEM] + [ANY] * len(ready) + [VMEM] * (len(pieces) + 2),
        out_specs=[VMEM] * n_rep,
        scratch_shapes=[pltpu.VMEM(kv_shape, BF16), pltpu.SemaphoreType.DMA((max(1, len(ready)),))],
        compiler_params=params(40),
        cost_estimate=cost(
            flops + 4 * queries.size * fanout * len(pieces) * tokens,
            moved + 2 * all_slots * len(pieces) * tokens * 2 * cols + 4 * queries.size,
        ),
        name="attend",
    )(slot, queries, *ready, *pieces, w_key, w_value)


def out_kernel(n_rep, *refs):
    mixed, weights, out_ref = refs[:n_rep], refs[n_rep:-1], refs[-1]
    out_ref[...] = sum(dot(a[0], w[...]) for a, w in zip(mixed, weights)).astype(BF16)


def out_project(mixed, weights, t, start, stop, tile):
    _, rows, depth = mixed[0].shape
    base = start // tile
    return pl.pallas_call(
        functools.partial(out_kernel, len(mixed)),
        grid=((stop - start) // tile,),
        out_shape=jax.ShapeDtypeStruct((rows, stop - start), BF16),
        in_specs=[pl.BlockSpec((1, rows, depth), lambda j: (t, 0, 0))] * len(mixed)
        + [pl.BlockSpec((depth, tile), lambda j: (0, base + j))] * len(mixed),
        out_specs=pl.BlockSpec((rows, tile), lambda j: (0, j)),
        compiler_params=params(16),
        cost_estimate=cost(
            2 * len(mixed) * rows * depth * (stop - start), 2 * len(mixed) * depth * (stop - start)
        ),
        name="out_project",
    )(*mixed, *weights)


def shards(queries, span_states, store, entry_ids, owners, w_key, w_value, w_out):
    n_lanes, n_heads, n_rep = (lax.axis_size(name) for name in ("lanes", "heads", "rep"))
    spans, fanout = entry_ids.shape
    requests = spans * fanout
    cap = max(2, (requests + n_lanes - 1) // n_lanes)
    span_len = queries.shape[0] // spans

    def over_rep(array):
        return [array] + [lax.ppermute(array, "rep", shift_pairs(n_rep, s)) for s in range(1, n_rep)]

    own = jnp.concatenate([owners.T, entry_ids.T], axis=0)
    asked = [lax.ppermute(own, "lanes", lane_pairs(n_lanes, d, False)) for d in range(1, n_lanes)]
    *blocks, req, slot = fetch(own, asked, store, n_lanes, cap)
    arrived = [blocks[0]]
    for d in range(1, n_lanes):
        arrived.append(lax.ppermute(blocks[d], "lanes", lane_pairs(n_lanes, d, True)))

    def gather(encoded):
        pieces = [encoded]
        pieces += [lax.ppermute(encoded, "heads", shift_pairs(n_heads, s)) for s in range(1, n_heads)]
        return [part for piece in pieces for part in over_rep(piece)]

    size = -(-n_lanes // GROUPS)
    groups = []
    for first in range(0, n_lanes, size):
        encoded = encode(req, span_states, arrived[first : first + size], first, cap, fanout, span_len)
        groups.append(gather(encoded))
    ready = [project(pieces, w_key, w_value) for pieces in groups[:-1]]

    def mix(turns, q):
        outs = attend(slot, q, ready, groups[-1], w_key, w_value, n_heads, n_rep, turns, fanout, spans)
        return [outs[0]] + [
            lax.ppermute(outs[s], "rep", shift_pairs(n_rep, s)) for s in range(1, n_rep)
        ]

    w_out_here, req = lax.optimization_barrier((w_out, req))
    w_outs = over_rep(w_out_here)
    width = w_out.shape[1]
    tile = min(FIRST_COLS, width)
    cuts = [0, tile, width] if tile < width else [0, width]
    mixed = mix(list(range(1, n_heads)), queries)
    received = []
    for t in range(1, n_heads):
        parts = []
        for start, stop in zip(cuts, cuts[1:]):
            partial = out_project(mixed, w_outs, t - 1, start, stop, tile)
            partial, mixed = lax.optimization_barrier((partial, mixed))
            parts.append(lax.ppermute(partial, "heads", shift_pairs(n_heads, t)))
        received.append(jnp.concatenate(parts, axis=1))
    queries, mixed = lax.optimization_barrier((queries, mixed))
    total = out_project(mix([0], queries), w_outs, 0, 0, width, tile).astype(F32)
    for part in received:
        total = total + part.astype(F32)
    return total.astype(BF16)


def solution(mesh):
    return jax.shard_map(
        shards,
        mesh=mesh,
        in_specs=(
            P(("groups", "lanes"), ("heads", "rep")),
            P(("groups", "lanes"), None),
            P(("groups", "lanes"), ("heads", "rep"), None),
            P(("groups", "lanes"), None),
            P(("groups", "lanes"), None),
            P(None, ("heads", "rep")),
            P(None, ("heads", "rep")),
            P(("heads", "rep"), None),
        ),
        out_specs=P(("groups", "lanes", "heads", "rep"), None),
        check_vma=False,
    )
```

```python
import functools

import jax
import jax.numpy as jnp
from jax import lax
from jax.experimental import pallas as pl
from jax.experimental.pallas import tpu as pltpu
from jax.sharding import PartitionSpec as P

HD = 128
ENCODER_HEAD_DIM = 128
F32 = jnp.float32
BF16 = jnp.bfloat16
COL_TILE = 512

VMEM = pl.BlockSpec(memory_space=pltpu.VMEM)
SMEM = pl.BlockSpec(memory_space=pltpu.SMEM)
ANY = pl.BlockSpec(memory_space=pl.ANY)


def params(mib):
    return pltpu.CompilerParams(vmem_limit_bytes=mib * 2**20)


SMALL = pl.CostEstimate(flops=1024, bytes_accessed=1024, transcendentals=0)


def apart(n, a, b):
    if n & (n - 1) == 0:
        return a ^ b
    return lax.rem(b - a + n, n)


def lane_pairs(n, d, reply):
    if n & (n - 1) == 0:
        return [(i, i ^ d) for i in range(n)]
    return [(i, (i - d if reply else i + d) % n) for i in range(n)]


def shift_pairs(n, s):
    return [(i, (i + s) % n) for i in range(n)]


def dot_t(a, b):
    return lax.dot_general(a, b, (((1,), (1,)), ((), ())), preferred_element_type=F32)


def dot(a, b):
    return jnp.dot(a, b, preferred_element_type=F32)


def fetch_kernel(n_lanes, cap, *refs):
    others = n_lanes - 1
    asked, store_ref, refs = refs[:others], refs[others], refs[others + 1 :]
    blocks, (pick_ref, sem) = refs[:others], refs[others:]
    lane = lax.axis_index("lanes")
    fanout, spans = asked[0].shape[0] // 2, asked[0].shape[1]
    for i in range(others * cap):
        pick_ref[i] = 0
    copies = []
    for d in range(others):
        place = d * cap
        for span in range(spans):
            for k in range(fanout):
                pick_ref[place] = asked[d][fanout + k, span]
                place = place + (asked[d][k, span] == lane).astype(jnp.int32)
        for s in range(cap):
            slot = d * cap + s
            copies.append(
                pltpu.make_async_copy(store_ref.at[pick_ref[slot]], blocks[d].at[s], sem.at[slot])
            )
            copies[-1].start()
    for copy in copies:
        copy.wait()


def fetch(asked, store, n_lanes, cap):
    block = jax.ShapeDtypeStruct((cap,) + store.shape[1:], store.dtype)
    others = n_lanes - 1
    return pl.pallas_call(
        functools.partial(fetch_kernel, n_lanes, cap),
        out_shape=[block] * others,
        in_specs=[SMEM] * others + [ANY],
        out_specs=[VMEM] * others,
        scratch_shapes=[
            pltpu.SMEM((others * cap + 1,), jnp.int32),
            pltpu.SemaphoreType.DMA((others * cap,)),
        ],
        compiler_params=params(16),
        cost_estimate=SMALL,
        name="fetch",
    )(*asked, store)


def encode_pairs(width):
    step = 2 * ENCODER_HEAD_DIM
    return [(start, min(start + step, width)) for start in range(0, width, step)]


def spread(states, start, stop):
    part = states[:, start:stop]
    heads = (stop - start) // ENCODER_HEAD_DIM
    if heads == 1:
        return part
    rows = jnp.concatenate([part] * heads, axis=0)
    return jnp.where(own_cells(rows.shape, part.shape[0]), rows, jnp.zeros_like(rows))


def own_cells(shape, keys):
    row = lax.broadcasted_iota(jnp.int32, shape, 0)
    col = lax.broadcasted_iota(jnp.int32, shape, 1)
    return (row >= keys) == (col >= ENCODER_HEAD_DIM)


def softmax_top(logits, keys):
    if logits.shape[1] == keys:
        return jnp.max(logits, axis=1, keepdims=True)
    first = lax.broadcasted_iota(jnp.int32, logits.shape, 1) < keys
    low = jnp.max(jnp.where(first, logits, -jnp.inf), axis=1, keepdims=True)
    high = jnp.max(jnp.where(first, -jnp.inf, logits), axis=1, keepdims=True)
    return jnp.where(first, low, high)


def encode_block(block, out_ref, first, req_ref, states_ref, fanout, span_len):
    scale = ENCODER_HEAD_DIM ** (-0.5)
    runs = encode_pairs(states_ref.shape[1])
    units = []
    for s in range(block.shape[0]):
        span = lax.div(req_ref[first + s], fanout)
        states = states_ref[pl.ds(pl.multiple_of(span * span_len, span_len), span_len), :]
        units += [(s, start, stop, spread(states, start, stop)) for start, stop in runs]
    logits = [dot_t(block[s, :, start:stop], keys) for s, start, stop, keys in units]
    tops = [softmax_top(part, span_len) for part in logits]
    weights = [jnp.exp((part - top) * scale).astype(BF16) for part, top in zip(logits, tops)]
    mixed = [dot(part, keys) for part, (_, _, _, keys) in zip(weights, units)]
    sums = []
    for part, (_, start, stop, keys) in zip(weights, units):
        ones = jnp.ones(keys.shape, BF16)
        if stop - start > ENCODER_HEAD_DIM:
            ones = jnp.where(own_cells(keys.shape, span_len), ones, jnp.zeros_like(ones))
        sums.append(dot(part, ones))
    for (s, start, stop, _), top, bottom in zip(units, mixed, sums):
        token = block[s, :, start:stop].astype(F32)
        out_ref[s, :, start:stop] = (token + top / bottom).astype(BF16)


def encode_kernel(first, cap, fanout, span_len, req_ref, states_ref, *refs):
    blocks, out_ref = refs[:-1], refs[-1]
    for i, block in enumerate(blocks):
        out = out_ref.at[i * cap : (i + 1) * cap]
        encode_block(block, out, (first + i) * cap, req_ref, states_ref, fanout, span_len)


def encode(req, span_states, blocks, first, fanout, span_len):
    cap, tokens, width = blocks[0].shape
    return pl.pallas_call(
        functools.partial(encode_kernel, first, cap, fanout, span_len),
        out_shape=jax.ShapeDtypeStruct((len(blocks) * cap, tokens, width), BF16),
        in_specs=[SMEM, VMEM] + [VMEM] * len(blocks),
        out_specs=VMEM,
        compiler_params=params(16),
        cost_estimate=SMALL,
        name="encode",
    )(req, span_states, *blocks)


def encode_local_kernel(n_lanes, cap, span_len, own_ref, states_ref, store_ref, *refs):
    out_ref, req_ref, slot_ref, pick_ref, count_ref, tokens_ref, sem = refs
    lane = lax.axis_index("lanes")
    fanout, spans = own_ref.shape[0] // 2, own_ref.shape[1]
    for i in range(n_lanes):
        count_ref[i] = 0
    for i in range(n_lanes * cap):
        pick_ref[i] = 0
        req_ref[i] = 0
    for j in range(fanout * spans):
        span, k = j // fanout, j % fanout
        d = apart(n_lanes, lane, own_ref[k, span])
        rank = count_ref[d]
        count_ref[d] = rank + 1
        slot = d * cap + rank
        pick_ref[slot] = own_ref[fanout + k, span]
        req_ref[slot] = j
        slot_ref[j] = slot
    copies = [
        pltpu.make_async_copy(store_ref.at[pick_ref[s]], tokens_ref.at[s], sem.at[s]) for s in range(cap)
    ]
    for copy in copies:
        copy.start()
    for copy in copies:
        copy.wait()
    encode_block(tokens_ref, out_ref, 0, req_ref, states_ref, fanout, span_len)


def encode_local(own, span_states, store, n_lanes, cap, span_len):
    block = (cap,) + store.shape[1:]
    return pl.pallas_call(
        functools.partial(encode_local_kernel, n_lanes, cap, span_len),
        out_shape=(
            jax.ShapeDtypeStruct(block, BF16),
            jax.ShapeDtypeStruct((n_lanes * cap,), jnp.int32),
            jax.ShapeDtypeStruct((own.size // 2,), jnp.int32),
        ),
        in_specs=[SMEM, VMEM, ANY],
        out_specs=(VMEM, SMEM, SMEM),
        scratch_shapes=[
            pltpu.SMEM((n_lanes * cap,), jnp.int32),
            pltpu.SMEM((n_lanes,), jnp.int32),
            pltpu.VMEM(block, BF16),
            pltpu.SemaphoreType.DMA((cap,)),
        ],
        compiler_params=params(16),
        cost_estimate=SMALL,
        name="encode_local",
    )(own, span_states, store)


def project_into(kv_ref, first, pieces, wk_ref, wv_ref):
    n, slots, tokens, width = pieces[0].shape
    rows = jnp.concatenate([piece[...].reshape(n * slots * tokens, width) for piece in pieces], axis=0)
    cols = wk_ref.shape[1]
    for side, weight in enumerate((wk_ref, wv_ref)):
        made = dot(rows, weight[...]).astype(BF16)
        for p in range(n * len(pieces)):
            part = made[p * slots * tokens : (p + 1) * slots * tokens]
            kv_ref[first : first + slots, p, :, side * cols : (side + 1) * cols] = part.reshape(
                slots, tokens, cols
            )


def project_kernel(n_pieces, *refs):
    pieces, (wk_ref, wv_ref, kv_ref) = refs[:n_pieces], refs[n_pieces:]
    project_into(kv_ref, 0, pieces, wk_ref, wv_ref)


def project(pieces, w_key, w_value):
    n, slots, tokens, _ = pieces[0].shape
    shape = (slots, n * len(pieces), tokens, 2 * w_key.shape[1])
    return pl.pallas_call(
        functools.partial(project_kernel, len(pieces)),
        out_shape=jax.ShapeDtypeStruct(shape, BF16),
        in_specs=[VMEM] * (len(pieces) + 2),
        out_specs=VMEM,
        compiler_params=params(32),
        cost_estimate=SMALL,
        name="project",
    )(*pieces, w_key, w_value)


def attend_kernel(firsts, n_pieces, n_heads, n_rep, turns, fanout, spans, slot_ref, q_ref, *refs):
    n_ready = len(firsts) - 1
    ready, refs = refs[:n_ready], refs[n_ready:]
    pieces, refs = refs[:n_pieces], refs[n_pieces:]
    wk_ref, wv_ref = refs[:2]
    outs = refs[2 : 2 + n_rep]
    kv_ref, sem = refs[2 + n_rep :]
    copies = [
        pltpu.make_async_copy(ref, kv_ref.at[pl.ds(first, ref.shape[0])], sem.at[i])
        for i, (ref, first) in enumerate(zip(ready, firsts))
    ]
    for copy in copies:
        copy.start()
    project_into(kv_ref, firsts[-1], pieces, wk_ref, wv_ref)
    for copy in copies:
        copy.wait()
    heads_at, rep_at = lax.axis_index("heads"), lax.axis_index("rep")
    cols = wk_ref.shape[1]
    span_len = q_ref.shape[0] // spans
    block = spans // (n_heads * n_rep)
    tokens = kv_ref.shape[1] * kv_ref.shape[2]
    heads = [slice(h * HD, (h + 1) * HD) for h in range(cols // HD)]
    for at, t in enumerate(turns):
        for s in range(n_rep):
            owner = lax.rem(heads_at + t, n_heads) * n_rep + lax.rem(rep_at + s, n_rep)
            for i in range(block):
                span = owner * block + i
                slots = [slot_ref[span * fanout + k] for k in range(fanout)]
                rows = pl.ds(pl.multiple_of(span * span_len, span_len), span_len)

                def side(lanes):
                    return jnp.concatenate(
                        [kv_ref[slot, :, :, lanes].reshape(tokens, HD) for slot in slots], axis=0
                    )

                logits = [dot_t(q_ref[rows, lanes], side(lanes)) for lanes in heads]
                tops = [jnp.max(part, axis=1, keepdims=True) for part in logits]
                weights = [jnp.exp((part - top) * HD ** (-0.5)) for part, top in zip(logits, tops)]
                scales = [1.0 / jnp.sum(part, axis=1, keepdims=True) for part in weights]
                mixed = [
                    dot(part.astype(BF16), side(slice(cols + lanes.start, cols + lanes.stop)))
                    for part, lanes in zip(weights, heads)
                ]
                for part, scale, lanes in zip(mixed, scales, heads):
                    outs[s][at, i * span_len : (i + 1) * span_len, lanes] = (part * scale).astype(BF16)


def attend(slot, queries, ready, pieces, w_key, w_value, n_heads, n_rep, turns, fanout, spans):
    firsts = [0]
    for kv in ready:
        firsts.append(firsts[-1] + kv.shape[0])
    n, slots, tokens, _ = pieces[0].shape
    cols = w_key.shape[1]
    rows = queries.shape[0] // (n_heads * n_rep)
    kv_shape = (firsts[-1] + slots, n * len(pieces), tokens, 2 * cols)
    return pl.pallas_call(
        functools.partial(attend_kernel, firsts, len(pieces), n_heads, n_rep, turns, fanout, spans),
        out_shape=[jax.ShapeDtypeStruct((len(turns), rows, cols), BF16)] * n_rep,
        in_specs=[SMEM, VMEM] + [ANY] * len(ready) + [VMEM] * (len(pieces) + 2),
        out_specs=[VMEM] * n_rep,
        scratch_shapes=[pltpu.VMEM(kv_shape, BF16), pltpu.SemaphoreType.DMA((max(1, len(ready)),))],
        compiler_params=params(40),
        cost_estimate=SMALL,
        name="attend",
    )(slot, queries, *ready, *pieces, w_key, w_value)


def out_kernel(n_rep, *refs):
    mixed, weights, out_ref = refs[:n_rep], refs[n_rep:-1], refs[-1]
    out_ref[...] = sum(dot(a[0], w[...]) for a, w in zip(mixed, weights)).astype(BF16)


def out_project(mixed, weights, t, start, stop, tile):
    _, rows, depth = mixed[0].shape
    base = start // tile
    return pl.pallas_call(
        functools.partial(out_kernel, len(mixed)),
        grid=((stop - start) // tile,),
        out_shape=jax.ShapeDtypeStruct((rows, stop - start), BF16),
        in_specs=[pl.BlockSpec((1, rows, depth), lambda j: (t, 0, 0))] * len(mixed)
        + [pl.BlockSpec((depth, tile), lambda j: (0, base + j))] * len(mixed),
        out_specs=pl.BlockSpec((rows, tile), lambda j: (0, j)),
        compiler_params=params(16),
        cost_estimate=SMALL,
        name="out_project",
    )(*mixed, *weights)


def after(values, *earlier):
    return lax.optimization_barrier((values, earlier))[0]


def shards(queries, span_states, store, entry_ids, owners, w_key, w_value, w_out):
    n_lanes, n_heads, n_rep = (lax.axis_size(name) for name in ("lanes", "heads", "rep"))
    spans, fanout = entry_ids.shape
    requests = spans * fanout
    cap = max(2, (requests + n_lanes - 1) // n_lanes)
    span_len = queries.shape[0] // spans

    def over_heads(array):
        return [array] + [lax.ppermute(array, "heads", shift_pairs(n_heads, s)) for s in range(1, n_heads)]

    def over_rep(array):
        return [array] + [lax.ppermute(array, "rep", shift_pairs(n_rep, s)) for s in range(1, n_rep)]

    own = jnp.concatenate([owners.T, entry_ids.T], axis=0)
    asked = [lax.ppermute(own, "lanes", lane_pairs(n_lanes, d, False)) for d in range(1, n_lanes)]
    w_outs = over_rep(w_out)
    encoded, req, slot = encode_local(own, span_states, store, n_lanes, cap, span_len)
    asked = after(asked, req, w_outs)
    blocks = [None] + list(fetch(asked, store, n_lanes, cap))

    def send(distances, *earlier):
        ready = after([blocks[d] for d in distances], *earlier)
        return [
            lax.ppermute(block, "lanes", lane_pairs(n_lanes, d, True))
            for block, d in zip(ready, distances)
        ]

    cut = 1 + (2 * (n_lanes - 1) + 2) // 3
    parts = [list(range(1, cut)), list(range(cut, n_lanes))]
    parts = [part for part in parts if part]

    crossed = over_heads(encoded)
    arrived = send(parts[0]) if parts else []
    stacked, kvs = jnp.stack(crossed), []
    for i, part in enumerate(parts):
        later = parts[i + 1] if i + 1 < len(parts) else []
        next_arrived = send(later, arrived) if later else []
        encoded = encode(req, span_states, after(arrived, stacked, kvs), part[0], fanout, span_len)
        crossed = over_heads(encoded)
        kvs.append(project(after(over_rep(stacked), encoded), w_key, w_value))
        stacked = jnp.stack(after(crossed, kvs))
        arrived = next_arrived
    pieces = over_rep(stacked)

    def mix(turns, q):
        outs = attend(slot, q, kvs, pieces, w_key, w_value, n_heads, n_rep, turns, fanout, spans)
        return [outs[0]] + [
            lax.ppermute(outs[s], "rep", shift_pairs(n_rep, s)) for s in range(1, n_rep)
        ]

    width = w_out.shape[1]
    tile = min(COL_TILE, width)
    cuts = sorted({0, width // 2 // tile * tile, width - tile, width})
    mixed = mix(list(range(1, n_heads)), queries)
    received = []
    for t in range(1, n_heads):
        sent = []
        for start, stop in zip(cuts, cuts[1:]):
            partial = out_project(mixed, w_outs, t - 1, start, stop, tile)
            partial, mixed = lax.optimization_barrier((partial, mixed))
            sent.append(lax.ppermute(partial, "heads", shift_pairs(n_heads, t)))
        received.append(jnp.concatenate(sent, axis=1))
    total = out_project(mix([0], after(queries, mixed)), w_outs, 0, 0, width, tile).astype(F32)
    for part in received:
        total = total + part.astype(F32)
    return total.astype(BF16)


def solution(mesh):
    return jax.shard_map(
        shards,
        mesh=mesh,
        in_specs=(
            P(("groups", "lanes"), ("heads", "rep")),
            P(("groups", "lanes"), None),
            P(("groups", "lanes"), ("heads", "rep"), None),
            P(("groups", "lanes"), None),
            P(("groups", "lanes"), None),
            P(None, ("heads", "rep")),
            P(None, ("heads", "rep")),
            P(("heads", "rep"), None),
        ),
        out_specs=P(("groups", "lanes", "heads", "rep"), None),
        check_vma=False,
    )
```

```python
import functools

import jax
import jax.numpy as jnp
from jax import lax
from jax.experimental import pallas as pl
from jax.experimental.pallas import tpu as pltpu
from jax.sharding import PartitionSpec as P

HD = 128
ENCODER_HEAD_DIM = 128
F32 = jnp.float32
BF16 = jnp.bfloat16
COL_TILE = 512

VMEM = pl.BlockSpec(memory_space=pltpu.VMEM)
SMEM = pl.BlockSpec(memory_space=pltpu.SMEM)
ANY = pl.BlockSpec(memory_space=pl.ANY)


def params(mib):
    return pltpu.CompilerParams(vmem_limit_bytes=mib * 2**20)


def cost(gflops):
    return pl.CostEstimate(flops=int(gflops * 10**9), bytes_accessed=1024, transcendentals=0)


def apart(n, a, b):
    if n & (n - 1) == 0:
        return a ^ b
    return lax.rem(b - a + n, n)


def lane_pairs(n, d, reply):
    if n & (n - 1) == 0:
        return [(i, i ^ d) for i in range(n)]
    return [(i, (i - d if reply else i + d) % n) for i in range(n)]


def shift_pairs(n, s):
    return [(i, (i + s) % n) for i in range(n)]


def dot_t(a, b):
    return lax.dot_general(a, b, (((1,), (1,)), ((), ())), preferred_element_type=F32)


def dot(a, b):
    return jnp.dot(a, b, preferred_element_type=F32)


def fetch_kernel(n_lanes, cap, *refs):
    others = n_lanes - 1
    asked, store_ref, refs = refs[:others], refs[others], refs[others + 1 :]
    blocks, (pick_ref, sem) = refs[:others], refs[others:]
    lane = lax.axis_index("lanes")
    fanout, spans = asked[0].shape[0] // 2, asked[0].shape[1]
    for i in range(others * cap):
        pick_ref[i] = 0
    copies = []
    for d in range(others):
        place = d * cap
        for span in range(spans):
            for k in range(fanout):
                pick_ref[place] = asked[d][fanout + k, span]
                place = place + (asked[d][k, span] == lane).astype(jnp.int32)
        for s in range(cap):
            slot = d * cap + s
            copies.append(
                pltpu.make_async_copy(store_ref.at[pick_ref[slot]], blocks[d].at[s], sem.at[slot])
            )
            copies[-1].start()
    for copy in copies:
        copy.wait()


def fetch(asked, store, n_lanes, cap):
    block = jax.ShapeDtypeStruct((cap,) + store.shape[1:], store.dtype)
    others = n_lanes - 1
    return pl.pallas_call(
        functools.partial(fetch_kernel, n_lanes, cap),
        out_shape=[block] * others,
        in_specs=[SMEM] * others + [ANY],
        out_specs=[VMEM] * others,
        scratch_shapes=[
            pltpu.SMEM((others * cap + 1,), jnp.int32),
            pltpu.SemaphoreType.DMA((others * cap,)),
        ],
        compiler_params=params(16),
        cost_estimate=cost(10),
        name="fetch",
    )(*asked, store)


def encode_pairs(width):
    step = 2 * ENCODER_HEAD_DIM
    return [(start, min(start + step, width)) for start in range(0, width, step)]


def spread(states, start, stop):
    part = states[:, start:stop]
    heads = (stop - start) // ENCODER_HEAD_DIM
    if heads == 1:
        return part
    rows = jnp.concatenate([part] * heads, axis=0)
    return jnp.where(own_cells(rows.shape, part.shape[0]), rows, jnp.zeros_like(rows))


def own_cells(shape, keys):
    row = lax.broadcasted_iota(jnp.int32, shape, 0)
    col = lax.broadcasted_iota(jnp.int32, shape, 1)
    return (row >= keys) == (col >= ENCODER_HEAD_DIM)


def softmax_top(logits, keys):
    if logits.shape[1] == keys:
        return jnp.max(logits, axis=1, keepdims=True)
    first = lax.broadcasted_iota(jnp.int32, logits.shape, 1) < keys
    low = jnp.max(jnp.where(first, logits, -jnp.inf), axis=1, keepdims=True)
    high = jnp.max(jnp.where(first, -jnp.inf, logits), axis=1, keepdims=True)
    return jnp.where(first, low, high)


def encode_block(block, out_ref, first, req_ref, states_ref, fanout, span_len):
    scale = ENCODER_HEAD_DIM ** (-0.5)
    runs = encode_pairs(states_ref.shape[1])
    units = []
    for s in range(block.shape[0]):
        span = lax.div(req_ref[first + s], fanout)
        states = states_ref[pl.ds(pl.multiple_of(span * span_len, span_len), span_len), :]
        units += [(s, start, stop, spread(states, start, stop)) for start, stop in runs]
    logits = [dot_t(block[s, :, start:stop], keys) for s, start, stop, keys in units]
    tops = [softmax_top(part, span_len) for part in logits]
    weights = [jnp.exp((part - top) * scale).astype(BF16) for part, top in zip(logits, tops)]
    mixed = [dot(part, keys) for part, (_, _, _, keys) in zip(weights, units)]
    sums = []
    for part, (_, start, stop, keys) in zip(weights, units):
        ones = jnp.ones(keys.shape, BF16)
        if stop - start > ENCODER_HEAD_DIM:
            ones = jnp.where(own_cells(keys.shape, span_len), ones, jnp.zeros_like(ones))
        sums.append(dot(part, ones))
    for (s, start, stop, _), top, bottom in zip(units, mixed, sums):
        token = block[s, :, start:stop].astype(F32)
        out_ref[s, :, start:stop] = (token + top / bottom).astype(BF16)


def encode_kernel(first, cap, fanout, span_len, req_ref, states_ref, *refs):
    blocks, out_ref = refs[:-1], refs[-1]
    for i, block in enumerate(blocks):
        out = out_ref.at[i * cap : (i + 1) * cap]
        encode_block(block, out, (first + i) * cap, req_ref, states_ref, fanout, span_len)


def encode(req, span_states, blocks, first, fanout, span_len):
    cap, tokens, width = blocks[0].shape
    return pl.pallas_call(
        functools.partial(encode_kernel, first, cap, fanout, span_len),
        out_shape=jax.ShapeDtypeStruct((len(blocks) * cap, tokens, width), BF16),
        in_specs=[SMEM, VMEM] + [VMEM] * len(blocks),
        out_specs=VMEM,
        compiler_params=params(16),
        cost_estimate=cost(10),
        name="encode",
    )(req, span_states, *blocks)


def encode_local_kernel(n_lanes, cap, span_len, own_ref, states_ref, store_ref, *refs):
    out_ref, req_ref, slot_ref, pick_ref, count_ref, tokens_ref, sem = refs
    lane = lax.axis_index("lanes")
    fanout, spans = own_ref.shape[0] // 2, own_ref.shape[1]
    for i in range(n_lanes):
        count_ref[i] = 0
    for i in range(n_lanes * cap):
        pick_ref[i] = 0
        req_ref[i] = 0
    for j in range(fanout * spans):
        span, k = j // fanout, j % fanout
        d = apart(n_lanes, lane, own_ref[k, span])
        rank = count_ref[d]
        count_ref[d] = rank + 1
        slot = d * cap + rank
        pick_ref[slot] = own_ref[fanout + k, span]
        req_ref[slot] = j
        slot_ref[j] = slot
    copies = [
        pltpu.make_async_copy(store_ref.at[pick_ref[s]], tokens_ref.at[s], sem.at[s]) for s in range(cap)
    ]
    for copy in copies:
        copy.start()
    for copy in copies:
        copy.wait()
    encode_block(tokens_ref, out_ref, 0, req_ref, states_ref, fanout, span_len)


def encode_local(own, span_states, store, n_lanes, cap, span_len):
    block = (cap,) + store.shape[1:]
    return pl.pallas_call(
        functools.partial(encode_local_kernel, n_lanes, cap, span_len),
        out_shape=(
            jax.ShapeDtypeStruct(block, BF16),
            jax.ShapeDtypeStruct((n_lanes * cap,), jnp.int32),
            jax.ShapeDtypeStruct((own.size // 2,), jnp.int32),
        ),
        in_specs=[SMEM, VMEM, ANY],
        out_specs=(VMEM, SMEM, SMEM),
        scratch_shapes=[
            pltpu.SMEM((n_lanes * cap,), jnp.int32),
            pltpu.SMEM((n_lanes,), jnp.int32),
            pltpu.VMEM(block, BF16),
            pltpu.SemaphoreType.DMA((cap,)),
        ],
        compiler_params=params(16),
        cost_estimate=cost(10),
        name="encode_local",
    )(own, span_states, store)


def project_into(kv_ref, first, pieces, wk_ref, wv_ref):
    n, slots, tokens, width = pieces[0].shape
    rows = jnp.concatenate([piece[...].reshape(n * slots * tokens, width) for piece in pieces], axis=0)
    cols = wk_ref.shape[1]
    for side, weight in enumerate((wk_ref, wv_ref)):
        made = dot(rows, weight[...]).astype(BF16)
        for p in range(n * len(pieces)):
            part = made[p * slots * tokens : (p + 1) * slots * tokens]
            kv_ref[first : first + slots, p, :, side * cols : (side + 1) * cols] = part.reshape(
                slots, tokens, cols
            )


def project_kernel(n_pieces, *refs):
    pieces, (wk_ref, wv_ref, kv_ref) = refs[:n_pieces], refs[n_pieces:]
    project_into(kv_ref, 0, pieces, wk_ref, wv_ref)


def project(pieces, w_key, w_value):
    n, slots, tokens, _ = pieces[0].shape
    shape = (slots, n * len(pieces), tokens, 2 * w_key.shape[1])
    return pl.pallas_call(
        functools.partial(project_kernel, len(pieces)),
        out_shape=jax.ShapeDtypeStruct(shape, BF16),
        in_specs=[VMEM] * (len(pieces) + 2),
        out_specs=VMEM,
        compiler_params=params(32),
        cost_estimate=cost(0.1),
        name="project",
    )(*pieces, w_key, w_value)


def attend_kernel(firsts, n_pieces, n_heads, n_rep, turns, fanout, spans, slot_ref, q_ref, *refs):
    n_ready = len(firsts) - 1
    ready, refs = refs[:n_ready], refs[n_ready:]
    pieces, refs = refs[:n_pieces], refs[n_pieces:]
    wk_ref, wv_ref = refs[:2]
    outs = refs[2 : 2 + n_rep]
    kv_ref, sem = refs[2 + n_rep :]
    copies = [
        pltpu.make_async_copy(ref, kv_ref.at[pl.ds(first, ref.shape[0])], sem.at[i])
        for i, (ref, first) in enumerate(zip(ready, firsts))
    ]
    for copy in copies:
        copy.start()
    project_into(kv_ref, firsts[-1], pieces, wk_ref, wv_ref)
    for copy in copies:
        copy.wait()
    heads_at, rep_at = lax.axis_index("heads"), lax.axis_index("rep")
    cols = wk_ref.shape[1]
    span_len = q_ref.shape[0] // spans
    block = spans // (n_heads * n_rep)
    tokens = kv_ref.shape[1] * kv_ref.shape[2]
    heads = [slice(h * HD, (h + 1) * HD) for h in range(cols // HD)]
    for at, t in enumerate(turns):
        for s in range(n_rep):
            owner = lax.rem(heads_at + t, n_heads) * n_rep + lax.rem(rep_at + s, n_rep)
            for i in range(block):
                span = owner * block + i
                slots = [slot_ref[span * fanout + k] for k in range(fanout)]
                rows = pl.ds(pl.multiple_of(span * span_len, span_len), span_len)

                def side(lanes):
                    return jnp.concatenate(
                        [kv_ref[slot, :, :, lanes].reshape(tokens, HD) for slot in slots], axis=0
                    )

                logits = [dot_t(q_ref[rows, lanes], side(lanes)) for lanes in heads]
                tops = [jnp.max(part, axis=1, keepdims=True) for part in logits]
                weights = [jnp.exp((part - top) * HD ** (-0.5)) for part, top in zip(logits, tops)]
                scales = [1.0 / jnp.sum(part, axis=1, keepdims=True) for part in weights]
                mixed = [
                    dot(part.astype(BF16), side(slice(cols + lanes.start, cols + lanes.stop)))
                    for part, lanes in zip(weights, heads)
                ]
                for part, scale, lanes in zip(mixed, scales, heads):
                    outs[s][at, i * span_len : (i + 1) * span_len, lanes] = (part * scale).astype(BF16)


def attend(slot, queries, ready, pieces, w_key, w_value, n_heads, n_rep, turns, fanout, spans):
    firsts = [0]
    for kv in ready:
        firsts.append(firsts[-1] + kv.shape[0])
    n, slots, tokens, _ = pieces[0].shape
    cols = w_key.shape[1]
    rows = queries.shape[0] // (n_heads * n_rep)
    kv_shape = (firsts[-1] + slots, n * len(pieces), tokens, 2 * cols)
    return pl.pallas_call(
        functools.partial(attend_kernel, firsts, len(pieces), n_heads, n_rep, turns, fanout, spans),
        out_shape=[jax.ShapeDtypeStruct((len(turns), rows, cols), BF16)] * n_rep,
        in_specs=[SMEM, VMEM] + [ANY] * len(ready) + [VMEM] * (len(pieces) + 2),
        out_specs=[VMEM] * n_rep,
        scratch_shapes=[pltpu.VMEM(kv_shape, BF16), pltpu.SemaphoreType.DMA((max(1, len(ready)),))],
        compiler_params=params(40),
        cost_estimate=cost(0.001),
        name="attend",
    )(slot, queries, *ready, *pieces, w_key, w_value)


def out_kernel(n_rep, *refs):
    mixed, weights, out_ref = refs[:n_rep], refs[n_rep:-1], refs[-1]
    out_ref[...] = sum(dot(a[0], w[...]) for a, w in zip(mixed, weights)).astype(BF16)


def out_project(mixed, weights, t, start, stop, tile):
    _, rows, depth = mixed[0].shape
    base = start // tile
    return pl.pallas_call(
        functools.partial(out_kernel, len(mixed)),
        grid=((stop - start) // tile,),
        out_shape=jax.ShapeDtypeStruct((rows, stop - start), BF16),
        in_specs=[pl.BlockSpec((1, rows, depth), lambda j: (t, 0, 0))] * len(mixed)
        + [pl.BlockSpec((depth, tile), lambda j: (0, base + j))] * len(mixed),
        out_specs=pl.BlockSpec((rows, tile), lambda j: (0, j)),
        compiler_params=params(16),
        cost_estimate=cost(0.001),
        name="out_project",
    )(*mixed, *weights)


def after(values, *earlier):
    return lax.optimization_barrier((values, earlier))[0]


def shards(queries, span_states, store, entry_ids, owners, w_key, w_value, w_out):
    n_lanes, n_heads, n_rep = (lax.axis_size(name) for name in ("lanes", "heads", "rep"))
    spans, fanout = entry_ids.shape
    requests = spans * fanout
    cap = max(2, (requests + n_lanes - 1) // n_lanes)
    span_len = queries.shape[0] // spans

    def over_heads(array):
        return [array] + [lax.ppermute(array, "heads", shift_pairs(n_heads, s)) for s in range(1, n_heads)]

    def over_rep(array):
        return [array] + [lax.ppermute(array, "rep", shift_pairs(n_rep, s)) for s in range(1, n_rep)]

    own = jnp.concatenate([owners.T, entry_ids.T], axis=0)
    asked = [lax.ppermute(own, "lanes", lane_pairs(n_lanes, d, False)) for d in range(1, n_lanes)]
    w_outs = over_rep(w_out)
    encoded, req, slot = encode_local(own, span_states, store, n_lanes, cap, span_len)
    asked = after(asked, req, w_outs)
    blocks = [None] + list(fetch(asked, store, n_lanes, cap))

    def send(distances, *earlier):
        ready = after([blocks[d] for d in distances], *earlier)
        return [
            lax.ppermute(block, "lanes", lane_pairs(n_lanes, d, True))
            for block, d in zip(ready, distances)
        ]

    cut = 1 + (2 * (n_lanes - 1) + 2) // 3
    parts = [list(range(1, cut)), list(range(cut, n_lanes))]
    parts = [part for part in parts if part]

    crossed = over_heads(encoded)
    arrived = send(parts[0]) if parts else []
    stacked, kvs = jnp.stack(after(crossed, blocks[1:])), []
    for i, part in enumerate(parts):
        later = parts[i + 1] if i + 1 < len(parts) else []
        next_arrived = send(later, arrived) if later else []
        encoded = encode(req, span_states, after(arrived, stacked, kvs), part[0], fanout, span_len)
        if i:
            stacked = jnp.stack(after(crossed, encoded))
        kvs.append(project(after(over_rep(stacked), encoded), w_key, w_value))
        crossed, arrived = over_heads(encoded), next_arrived
    pieces = over_rep(jnp.stack(after(crossed, kvs)) if parts else stacked)

    def mix(turns, q):
        outs = attend(slot, q, kvs, pieces, w_key, w_value, n_heads, n_rep, turns, fanout, spans)
        return [outs[0]] + [
            lax.ppermute(outs[s], "rep", shift_pairs(n_rep, s)) for s in range(1, n_rep)
        ]

    width = w_out.shape[1]
    tile = min(COL_TILE, width)
    cuts = sorted({0, width // 2 // tile * tile, width - tile, width})
    mixed = mix(list(range(1, n_heads)), queries)
    received, partials = [], []
    for t in range(1, n_heads):
        sent = []
        for start, stop in zip(cuts, cuts[1:]):
            partial = out_project(mixed, w_outs, t - 1, start, stop, tile)
            partial, mixed = lax.optimization_barrier((partial, mixed))
            partials.append(partial)
            sent.append(lax.ppermute(partial, "heads", shift_pairs(n_heads, t)))
        received.append(jnp.concatenate(sent, axis=1))
    total = out_project(mix([0], after(queries, partials)), w_outs, 0, 0, width, tile).astype(F32)
    for part in received:
        total = total + part.astype(F32)
    return total.astype(BF16)


def solution(mesh):
    return jax.shard_map(
        shards,
        mesh=mesh,
        in_specs=(
            P(("groups", "lanes"), ("heads", "rep")),
            P(("groups", "lanes"), None),
            P(("groups", "lanes"), ("heads", "rep"), None),
            P(("groups", "lanes"), None),
            P(("groups", "lanes"), None),
            P(None, ("heads", "rep")),
            P(None, ("heads", "rep")),
            P(("heads", "rep"), None),
        ),
        out_specs=P(("groups", "lanes", "heads", "rep"), None),
        check_vma=False,
    )
```

```python
import functools

import jax
import jax.numpy as jnp
from jax import lax
from jax.experimental import pallas as pl
from jax.experimental.pallas import tpu as pltpu
from jax.sharding import PartitionSpec as P

HD = 128
ENCODER_HEAD_DIM = 128
F32 = jnp.float32
BF16 = jnp.bfloat16
LATER_GROUPS = 4
COL_TILE = 256

VMEM = pl.BlockSpec(memory_space=pltpu.VMEM)
SMEM = pl.BlockSpec(memory_space=pltpu.SMEM)
ANY = pl.BlockSpec(memory_space=pl.ANY)


def params(mib):
    return pltpu.CompilerParams(vmem_limit_bytes=mib * 2**20)


def cost(gflops):
    return pl.CostEstimate(flops=int(gflops * 10**9), bytes_accessed=1024, transcendentals=0)


def apart(n, a, b):
    if n & (n - 1) == 0:
        return a ^ b
    return lax.rem(b - a + n, n)


def lane_pairs(n, d, reply):
    if n & (n - 1) == 0:
        return [(i, i ^ d) for i in range(n)]
    return [(i, (i - d if reply else i + d) % n) for i in range(n)]


def shift_pairs(n, s):
    return [(i, (i + s) % n) for i in range(n)]


def dot_t(a, b):
    return lax.dot_general(a, b, (((1,), (1,)), ((), ())), preferred_element_type=F32)


def dot(a, b):
    return jnp.dot(a, b, preferred_element_type=F32)


def plan_kernel(n_lanes, cap, own_ref, req_ref, slot_ref, pick_ref, count_ref):
    lane = lax.axis_index("lanes")
    fanout, spans = own_ref.shape[0] // 2, own_ref.shape[1]
    for i in range(n_lanes):
        count_ref[i] = 0
    for i in range(n_lanes * cap):
        pick_ref[i] = 0
        req_ref[i] = 0
    for j in range(fanout * spans):
        span, k = j // fanout, j % fanout
        d = apart(n_lanes, lane, own_ref[k, span])
        rank = count_ref[d]
        count_ref[d] = rank + 1
        slot = d * cap + rank
        pick_ref[slot] = own_ref[fanout + k, span]
        req_ref[slot] = j
        slot_ref[j] = slot


def plan(own, n_lanes, cap):
    table = jax.ShapeDtypeStruct((n_lanes * cap,), jnp.int32)
    return pl.pallas_call(
        functools.partial(plan_kernel, n_lanes, cap),
        out_shape=(table, jax.ShapeDtypeStruct((own.size // 2,), jnp.int32), table),
        in_specs=[SMEM],
        out_specs=(SMEM, SMEM, SMEM),
        scratch_shapes=[pltpu.SMEM((n_lanes,), jnp.int32)],
        compiler_params=params(16),
        cost_estimate=cost(10),
        name="plan",
    )(own)


def fetch_kernel(items, cap, *refs):
    others = items[-1][0]
    asked, store_ref, refs = refs[:others], refs[others], refs[others + 1 :]
    blocks, pick_ref = refs[:-1], refs[-1]
    lane = lax.axis_index("lanes")
    fanout, spans = asked[0].shape[0] // 2, asked[0].shape[1]
    for i in range(others * cap):
        pick_ref[i] = 0
    for d in range(others):
        place = d * cap
        for span in range(spans):
            for k in range(fanout):
                pick_ref[place] = asked[d][fanout + k, span]
                place = place + (asked[d][k, span] == lane).astype(jnp.int32)
    for block, (d, low, high) in zip(blocks, items):
        for s in range(low, high):
            block[s - low] = store_ref[pick_ref[(d - 1) * cap + s]]


def fetch(asked, store, items, cap):
    others = len(asked)
    return pl.pallas_call(
        functools.partial(fetch_kernel, items, cap),
        out_shape=[
            jax.ShapeDtypeStruct((high - low,) + store.shape[1:], store.dtype) for _, low, high in items
        ],
        in_specs=[SMEM] * others + [VMEM],
        out_specs=[VMEM] * len(items),
        scratch_shapes=[pltpu.SMEM((others * cap + 1,), jnp.int32)],
        compiler_params=params(16),
        cost_estimate=cost(10),
        name="fetch",
    )(*asked, store)


def encode_pairs(width):
    step = 2 * ENCODER_HEAD_DIM
    return [(start, min(start + step, width)) for start in range(0, width, step)]


def spread(states, start, stop):
    part = states[:, start:stop]
    heads = (stop - start) // ENCODER_HEAD_DIM
    if heads == 1:
        return part
    rows = jnp.concatenate([part] * heads, axis=0)
    return jnp.where(own_cells(rows.shape, part.shape[0]), rows, jnp.zeros_like(rows))


def own_cells(shape, keys):
    row = lax.broadcasted_iota(jnp.int32, shape, 0)
    col = lax.broadcasted_iota(jnp.int32, shape, 1)
    return (row >= keys) == (col >= ENCODER_HEAD_DIM)


def softmax_top(logits, keys):
    if logits.shape[1] == keys:
        return jnp.max(logits, axis=1, keepdims=True)
    first = lax.broadcasted_iota(jnp.int32, logits.shape, 1) < keys
    low = jnp.max(jnp.where(first, logits, -jnp.inf), axis=1, keepdims=True)
    high = jnp.max(jnp.where(first, -jnp.inf, logits), axis=1, keepdims=True)
    return jnp.where(first, low, high)


def encode_block(block, out_ref, first, req_ref, states_ref, fanout, span_len):
    scale = ENCODER_HEAD_DIM ** (-0.5)
    runs = encode_pairs(states_ref.shape[1])
    units = []
    for s in range(block.shape[0]):
        span = lax.div(req_ref[first + s], fanout)
        states = states_ref[pl.ds(pl.multiple_of(span * span_len, span_len), span_len), :]
        units += [(s, start, stop, spread(states, start, stop)) for start, stop in runs]
    logits = [dot_t(block[s, :, start:stop], keys) for s, start, stop, keys in units]
    tops = [softmax_top(part, span_len) for part in logits]
    weights = [jnp.exp((part - top) * scale).astype(BF16) for part, top in zip(logits, tops)]
    mixed = [dot(part, keys) for part, (_, _, _, keys) in zip(weights, units)]
    sums = []
    for part, (_, start, stop, keys) in zip(weights, units):
        ones = jnp.ones(keys.shape, BF16)
        if stop - start > ENCODER_HEAD_DIM:
            ones = jnp.where(own_cells(keys.shape, span_len), ones, jnp.zeros_like(ones))
        sums.append(dot(part, ones))
    for (s, start, stop, _), top, bottom in zip(units, mixed, sums):
        token = block[s, :, start:stop].astype(F32)
        out_ref[s, :, start:stop] = (token + top / bottom).astype(BF16)


def encode_kernel(first, fanout, span_len, req_ref, states_ref, *refs):
    blocks, out_ref = refs[:-1], refs[-1]
    at = 0
    for block in blocks:
        stop = at + block.shape[0]
        encode_block(block, out_ref.at[at:stop], first + at, req_ref, states_ref, fanout, span_len)
        at = stop


def encode(req, span_states, blocks, first, fanout, span_len):
    slots = sum(block.shape[0] for block in blocks)
    return pl.pallas_call(
        functools.partial(encode_kernel, first, fanout, span_len),
        out_shape=jax.ShapeDtypeStruct((slots,) + blocks[0].shape[1:], BF16),
        in_specs=[SMEM, VMEM] + [VMEM] * len(blocks),
        out_specs=VMEM,
        compiler_params=params(16),
        cost_estimate=cost(10),
        name="encode",
    )(req, span_states, *blocks)


def encode_local_kernel(fanout, span_len, req_ref, pick_ref, states_ref, store_ref, out_ref, tokens_ref):
    for s in range(out_ref.shape[0]):
        tokens_ref[s] = store_ref[pick_ref[s]]
    encode_block(tokens_ref, out_ref, 0, req_ref, states_ref, fanout, span_len)


def encode_local(req, pick, span_states, store, cap, fanout, span_len):
    block = (cap,) + store.shape[1:]
    return pl.pallas_call(
        functools.partial(encode_local_kernel, fanout, span_len),
        out_shape=jax.ShapeDtypeStruct(block, BF16),
        in_specs=[SMEM, SMEM, VMEM, VMEM],
        out_specs=VMEM,
        scratch_shapes=[pltpu.VMEM(block, BF16)],
        compiler_params=params(16),
        cost_estimate=cost(10),
        name="encode_local",
    )(req, pick, span_states, store)


def project_into(kv_ref, first, pieces, wk_ref, wv_ref):
    n, slots, tokens, width = pieces[0].shape
    rows = jnp.concatenate([piece[...].reshape(n * slots * tokens, width) for piece in pieces], axis=0)
    cols = wk_ref.shape[1]
    for side, weight in enumerate((wk_ref, wv_ref)):
        made = dot(rows, weight[...]).astype(BF16)
        for p in range(n * len(pieces)):
            part = made[p * slots * tokens : (p + 1) * slots * tokens]
            kv_ref[first : first + slots, p, :, side * cols : (side + 1) * cols] = part.reshape(
                slots, tokens, cols
            )


def project_kernel(n_pieces, *refs):
    pieces, (wk_ref, wv_ref, kv_ref) = refs[:n_pieces], refs[n_pieces:]
    project_into(kv_ref, 0, pieces, wk_ref, wv_ref)


def project(pieces, w_key, w_value):
    n, slots, tokens, _ = pieces[0].shape
    shape = (slots, n * len(pieces), tokens, 2 * w_key.shape[1])
    return pl.pallas_call(
        functools.partial(project_kernel, len(pieces)),
        out_shape=jax.ShapeDtypeStruct(shape, BF16),
        in_specs=[VMEM] * (len(pieces) + 2),
        out_specs=VMEM,
        compiler_params=params(32),
        cost_estimate=cost(0.1),
        name="project",
    )(*pieces, w_key, w_value)


def attend_kernel(firsts, n_pieces, n_heads, n_rep, turns, fanout, spans, slot_ref, q_ref, *refs):
    n_ready = len(firsts) - 1
    ready, refs = refs[:n_ready], refs[n_ready:]
    pieces, refs = refs[:n_pieces], refs[n_pieces:]
    wk_ref, wv_ref = refs[:2]
    outs = refs[2 : 2 + n_rep]
    kv_ref, sem = refs[2 + n_rep :]
    copies = [
        pltpu.make_async_copy(ref, kv_ref.at[pl.ds(first, ref.shape[0])], sem.at[i])
        for i, (ref, first) in enumerate(zip(ready, firsts))
    ]
    for copy in copies:
        copy.start()
    project_into(kv_ref, firsts[-1], pieces, wk_ref, wv_ref)
    for copy in copies:
        copy.wait()
    heads_at, rep_at = lax.axis_index("heads"), lax.axis_index("rep")
    cols = wk_ref.shape[1]
    span_len = q_ref.shape[0] // spans
    block = spans // (n_heads * n_rep)
    tokens = kv_ref.shape[1] * kv_ref.shape[2]
    heads = [slice(h * HD, (h + 1) * HD) for h in range(cols // HD)]
    for at, t in enumerate(turns):
        for s in range(n_rep):
            owner = lax.rem(heads_at + t, n_heads) * n_rep + lax.rem(rep_at + s, n_rep)
            for i in range(block):
                span = owner * block + i
                slots = [slot_ref[span * fanout + k] for k in range(fanout)]
                rows = pl.ds(pl.multiple_of(span * span_len, span_len), span_len)

                def side(lanes):
                    return jnp.concatenate(
                        [kv_ref[slot, :, :, lanes].reshape(tokens, HD) for slot in slots], axis=0
                    )

                logits = [dot_t(q_ref[rows, lanes], side(lanes)) for lanes in heads]
                tops = [jnp.max(part, axis=1, keepdims=True) for part in logits]
                weights = [jnp.exp((part - top) * HD ** (-0.5)) for part, top in zip(logits, tops)]
                scales = [1.0 / jnp.sum(part, axis=1, keepdims=True) for part in weights]
                mixed = [
                    dot(part.astype(BF16), side(slice(cols + lanes.start, cols + lanes.stop)))
                    for part, lanes in zip(weights, heads)
                ]
                for part, scale, lanes in zip(mixed, scales, heads):
                    outs[s][at, i * span_len : (i + 1) * span_len, lanes] = (part * scale).astype(BF16)


def attend(slot, queries, ready, pieces, w_key, w_value, n_heads, n_rep, turns, fanout, spans):
    firsts = [0]
    for kv in ready:
        firsts.append(firsts[-1] + kv.shape[0])
    n, slots, tokens, _ = pieces[0].shape
    cols = w_key.shape[1]
    rows = queries.shape[0] // (n_heads * n_rep)
    kv_shape = (firsts[-1] + slots, n * len(pieces), tokens, 2 * cols)
    return pl.pallas_call(
        functools.partial(attend_kernel, firsts, len(pieces), n_heads, n_rep, turns, fanout, spans),
        out_shape=[jax.ShapeDtypeStruct((len(turns), rows, cols), BF16)] * n_rep,
        in_specs=[SMEM, VMEM] + [ANY] * len(ready) + [VMEM] * (len(pieces) + 2),
        out_specs=[VMEM] * n_rep,
        scratch_shapes=[pltpu.VMEM(kv_shape, BF16), pltpu.SemaphoreType.DMA((max(1, len(ready)),))],
        compiler_params=params(40),
        cost_estimate=cost(0.001),
        name="attend",
    )(slot, queries, *ready, *pieces, w_key, w_value)


def out_kernel(n_rep, *refs):
    mixed, weights, out_ref = refs[:n_rep], refs[n_rep:-1], refs[-1]
    out_ref[...] = sum(dot(a[0], w[...]) for a, w in zip(mixed, weights)).astype(BF16)


def out_project(mixed, weights, t, start, stop, tile):
    _, rows, depth = mixed[0].shape
    base = start // tile
    return pl.pallas_call(
        functools.partial(out_kernel, len(mixed)),
        grid=((stop - start) // tile,),
        out_shape=jax.ShapeDtypeStruct((rows, stop - start), BF16),
        in_specs=[pl.BlockSpec((1, rows, depth), lambda j: (t, 0, 0))] * len(mixed)
        + [pl.BlockSpec((depth, tile), lambda j: (0, base + j))] * len(mixed),
        out_specs=pl.BlockSpec((rows, tile), lambda j: (0, j)),
        compiler_params=params(16),
        cost_estimate=cost(0.001),
        name="out_project",
    )(*mixed, *weights)


def after(values, *earlier):
    return lax.optimization_barrier((values, earlier))[0]


def shards(queries, span_states, store, entry_ids, owners, w_key, w_value, w_out):
    n_lanes, n_heads, n_rep = (lax.axis_size(name) for name in ("lanes", "heads", "rep"))
    spans, fanout = entry_ids.shape
    requests = spans * fanout
    cap = max(2, (requests + n_lanes - 1) // n_lanes)
    span_len = queries.shape[0] // spans

    def over_heads(array):
        return [array] + [lax.ppermute(array, "heads", shift_pairs(n_heads, s)) for s in range(1, n_heads)]

    def over_rep(array):
        return [array] + [lax.ppermute(array, "rep", shift_pairs(n_rep, s)) for s in range(1, n_rep)]

    items = [(d, 0, cap) for d in range(1, n_lanes - 1)]
    items += [(n_lanes - 1, 0, cap // 2), (n_lanes - 1, cap // 2, cap)]
    size = -(-len(items) // LATER_GROUPS)
    parts = [range(i, min(i + size, len(items))) for i in range(0, len(items), size)]

    own = jnp.concatenate([owners.T, entry_ids.T], axis=0)
    asked = [lax.ppermute(own, "lanes", lane_pairs(n_lanes, d, False)) for d in range(1, n_lanes)]
    w_outs = over_rep(w_out)
    req, slot, pick = plan(own, n_lanes, cap)
    encoded = encode_local(req, pick, span_states, store, cap, fanout, span_len)
    blocks = fetch(after(asked, w_outs, encoded), store, items, cap)

    def send(part, *earlier):
        ready = after([blocks[i] for i in part], *earlier)
        return [
            lax.ppermute(block, "lanes", lane_pairs(n_lanes, items[i][0], True))
            for block, i in zip(ready, part)
        ]

    crossed, pieces, kvs = [over_heads(encoded)], [], []
    arrived = [None] + [send(part) for part in parts[:2]]
    last = blocks
    for i, part in enumerate(parts, 1):
        if i + 2 <= len(parts):
            arrived.append(send(parts[i + 1], arrived[i], last))
        first = items[part[0]][0] * cap + items[part[0]][1]
        encoded = encode(req, span_states, after(arrived[i], last), first, fanout, span_len)
        crossed.append(over_heads(encoded))
        last = encoded
        if i >= 2:
            last = project(after(pieces[i - 2], last), w_key, w_value)
            kvs.append(last)
        if i < len(parts):
            last = jnp.stack(after(crossed[i - 1], last))
            pieces.append(over_rep(last))
    ends = [jnp.concatenate(pair, axis=0) for pair in zip(*after(crossed[-2:], kvs))]
    pieces = over_rep(jnp.stack(ends))

    def mix(turns, q):
        outs = attend(slot, q, kvs, pieces, w_key, w_value, n_heads, n_rep, turns, fanout, spans)
        return [outs[0]] + [
            lax.ppermute(outs[s], "rep", shift_pairs(n_rep, s)) for s in range(1, n_rep)
        ]

    width = w_out.shape[1]
    tile = min(COL_TILE, width)
    cuts = [width // tile * part // 16 * tile for part in (0, 6, 11, 14)] + [width]
    mixed = mix(list(range(1, n_heads)), queries)
    received, partials = [], []
    for t in range(1, n_heads):
        sent = []
        for start, stop in zip(cuts, cuts[1:]):
            partial = out_project(mixed, w_outs, t - 1, start, stop, tile)
            partial, mixed = lax.optimization_barrier((partial, mixed))
            partials.append(partial)
            sent.append(lax.ppermute(partial, "heads", shift_pairs(n_heads, t)))
        received.append(jnp.concatenate(sent, axis=1))
    total = out_project(mix([0], after(queries, partials)), w_outs, 0, 0, width, tile).astype(F32)
    for part in received:
        total = total + part.astype(F32)
    return total.astype(BF16)


def solution(mesh):
    return jax.shard_map(
        shards,
        mesh=mesh,
        in_specs=(
            P(("groups", "lanes"), ("heads", "rep")),
            P(("groups", "lanes"), None),
            P(("groups", "lanes"), ("heads", "rep"), None),
            P(("groups", "lanes"), None),
            P(("groups", "lanes"), None),
            P(None, ("heads", "rep")),
            P(None, ("heads", "rep")),
            P(("heads", "rep"), None),
        ),
        out_specs=P(("groups", "lanes", "heads", "rep"), None),
        check_vma=False,
    )
```

```python
import functools

import jax
import jax.numpy as jnp
from jax import lax
from jax.experimental import pallas as pl
from jax.experimental.pallas import tpu as pltpu
from jax.sharding import PartitionSpec as P

HD = 128
ENCODER_HEAD_DIM = 128
F32 = jnp.float32
BF16 = jnp.bfloat16
LATER_GROUPS = 3
COL_TILE = 256
ENCODE_COST = (None, 0.1, 10, 10, 10)

VMEM = pl.BlockSpec(memory_space=pltpu.VMEM)
SMEM = pl.BlockSpec(memory_space=pltpu.SMEM)
ANY = pl.BlockSpec(memory_space=pl.ANY)


def params(mib):
    return pltpu.CompilerParams(vmem_limit_bytes=mib * 2**20)


def cost(gflops):
    return pl.CostEstimate(flops=int(gflops * 10**9), bytes_accessed=1024, transcendentals=0)


def apart(n, a, b):
    if n & (n - 1) == 0:
        return a ^ b
    return lax.rem(b - a + n, n)


def lane_pairs(n, d, reply):
    if n & (n - 1) == 0:
        return [(i, i ^ d) for i in range(n)]
    return [(i, (i - d if reply else i + d) % n) for i in range(n)]


def shift_pairs(n, s):
    return [(i, (i + s) % n) for i in range(n)]


def dot_t(a, b):
    return lax.dot_general(a, b, (((1,), (1,)), ((), ())), preferred_element_type=F32)


def dot(a, b):
    return jnp.dot(a, b, preferred_element_type=F32)


def plan_kernel(n_lanes, cap, own_ref, req_ref, slot_ref, pick_ref, count_ref):
    lane = lax.axis_index("lanes")
    fanout, spans = own_ref.shape[0] // 2, own_ref.shape[1]
    for i in range(n_lanes):
        count_ref[i] = 0
    for i in range(n_lanes * cap):
        pick_ref[i] = 0
        req_ref[i] = 0
    for j in range(fanout * spans):
        span, k = j // fanout, j % fanout
        d = apart(n_lanes, lane, own_ref[k, span])
        rank = count_ref[d]
        count_ref[d] = rank + 1
        slot = d * cap + rank
        pick_ref[slot] = own_ref[fanout + k, span]
        req_ref[slot] = j
        slot_ref[j] = slot


def plan(own, n_lanes, cap):
    table = jax.ShapeDtypeStruct((n_lanes * cap,), jnp.int32)
    return pl.pallas_call(
        functools.partial(plan_kernel, n_lanes, cap),
        out_shape=(table, jax.ShapeDtypeStruct((own.size // 2,), jnp.int32), table),
        in_specs=[SMEM],
        out_specs=(SMEM, SMEM, SMEM),
        scratch_shapes=[pltpu.SMEM((n_lanes,), jnp.int32)],
        compiler_params=params(16),
        cost_estimate=cost(10),
        name="plan",
    )(own)


def fetch_kernel(items, cap, *refs):
    others = items[-1][0]
    asked, store_ref, refs = refs[:others], refs[others], refs[others + 1 :]
    blocks, pick_ref = refs[:-1], refs[-1]
    lane = lax.axis_index("lanes")
    fanout, spans = asked[0].shape[0] // 2, asked[0].shape[1]
    for i in range(others * cap):
        pick_ref[i] = 0
    for d in range(others):
        place = d * cap
        for span in range(spans):
            for k in range(fanout):
                pick_ref[place] = asked[d][fanout + k, span]
                place = place + (asked[d][k, span] == lane).astype(jnp.int32)
    for block, (d, low, high) in zip(blocks, items):
        for s in range(low, high):
            block[s - low] = store_ref[pick_ref[(d - 1) * cap + s]]


def fetch(asked, store, items, cap):
    others = len(asked)
    return pl.pallas_call(
        functools.partial(fetch_kernel, items, cap),
        out_shape=[
            jax.ShapeDtypeStruct((high - low,) + store.shape[1:], store.dtype) for _, low, high in items
        ],
        in_specs=[SMEM] * others + [VMEM],
        out_specs=[VMEM] * len(items),
        scratch_shapes=[pltpu.SMEM((others * cap + 1,), jnp.int32)],
        compiler_params=params(16),
        cost_estimate=cost(10),
        name="fetch",
    )(*asked, store)


def encode_pairs(width):
    step = 2 * ENCODER_HEAD_DIM
    return [(start, min(start + step, width)) for start in range(0, width, step)]


def spread(states, start, stop):
    part = states[:, start:stop]
    heads = (stop - start) // ENCODER_HEAD_DIM
    if heads == 1:
        return part
    rows = jnp.concatenate([part] * heads, axis=0)
    return jnp.where(own_cells(rows.shape, part.shape[0]), rows, jnp.zeros_like(rows))


def own_cells(shape, keys):
    row = lax.broadcasted_iota(jnp.int32, shape, 0)
    col = lax.broadcasted_iota(jnp.int32, shape, 1)
    return (row >= keys) == (col >= ENCODER_HEAD_DIM)


def softmax_top(logits, keys):
    if logits.shape[1] == keys:
        return jnp.max(logits, axis=1, keepdims=True)
    first = lax.broadcasted_iota(jnp.int32, logits.shape, 1) < keys
    low = jnp.max(jnp.where(first, logits, -jnp.inf), axis=1, keepdims=True)
    high = jnp.max(jnp.where(first, -jnp.inf, logits), axis=1, keepdims=True)
    return jnp.where(first, low, high)


def encode_block(block, out_ref, first, req_ref, states_ref, fanout, span_len):
    scale = ENCODER_HEAD_DIM ** (-0.5)
    runs = encode_pairs(states_ref.shape[1])
    units = []
    for s in range(block.shape[0]):
        span = lax.div(req_ref[first + s], fanout)
        states = states_ref[pl.ds(pl.multiple_of(span * span_len, span_len), span_len), :]
        units += [(s, start, stop, spread(states, start, stop)) for start, stop in runs]
    logits = [dot_t(block[s, :, start:stop], keys) for s, start, stop, keys in units]
    tops = [softmax_top(part, span_len) for part in logits]
    weights = [jnp.exp((part - top) * scale).astype(BF16) for part, top in zip(logits, tops)]
    mixed = [dot(part, keys) for part, (_, _, _, keys) in zip(weights, units)]
    sums = []
    for part, (_, start, stop, keys) in zip(weights, units):
        ones = jnp.ones(keys.shape, BF16)
        if stop - start > ENCODER_HEAD_DIM:
            ones = jnp.where(own_cells(keys.shape, span_len), ones, jnp.zeros_like(ones))
        sums.append(dot(part, ones))
    for (s, start, stop, _), top, bottom in zip(units, mixed, sums):
        token = block[s, :, start:stop].astype(F32)
        out_ref[s, :, start:stop] = (token + top / bottom).astype(BF16)


def encode_kernel(first, fanout, span_len, req_ref, states_ref, *refs):
    blocks, out_ref = refs[:-1], refs[-1]
    at = 0
    for block in blocks:
        stop = at + block.shape[0]
        encode_block(block, out_ref.at[at:stop], first + at, req_ref, states_ref, fanout, span_len)
        at = stop


def encode(req, span_states, blocks, first, fanout, span_len, gflops):
    slots = sum(block.shape[0] for block in blocks)
    return pl.pallas_call(
        functools.partial(encode_kernel, first, fanout, span_len),
        out_shape=jax.ShapeDtypeStruct((slots,) + blocks[0].shape[1:], BF16),
        in_specs=[SMEM, VMEM] + [VMEM] * len(blocks),
        out_specs=VMEM,
        compiler_params=params(16),
        cost_estimate=cost(gflops),
        name="encode",
    )(req, span_states, *blocks)


def encode_local_kernel(fanout, span_len, req_ref, pick_ref, states_ref, store_ref, out_ref, tokens_ref):
    for s in range(out_ref.shape[0]):
        tokens_ref[s] = store_ref[pick_ref[s]]
    encode_block(tokens_ref, out_ref, 0, req_ref, states_ref, fanout, span_len)


def encode_local(req, pick, span_states, store, cap, fanout, span_len):
    block = (cap,) + store.shape[1:]
    return pl.pallas_call(
        functools.partial(encode_local_kernel, fanout, span_len),
        out_shape=jax.ShapeDtypeStruct(block, BF16),
        in_specs=[SMEM, SMEM, VMEM, VMEM],
        out_specs=VMEM,
        scratch_shapes=[pltpu.VMEM(block, BF16)],
        compiler_params=params(16),
        cost_estimate=cost(10),
        name="encode_local",
    )(req, pick, span_states, store)


def project_into(kv_ref, first, pieces, wk_ref, wv_ref):
    n, slots, tokens, width = pieces[0].shape
    rows = jnp.concatenate([piece[...].reshape(n * slots * tokens, width) for piece in pieces], axis=0)
    cols = wk_ref.shape[1]
    for side, weight in enumerate((wk_ref, wv_ref)):
        made = dot(rows, weight[...]).astype(BF16)
        for p in range(n * len(pieces)):
            part = made[p * slots * tokens : (p + 1) * slots * tokens]
            kv_ref[first : first + slots, p, :, side * cols : (side + 1) * cols] = part.reshape(
                slots, tokens, cols
            )


def project_kernel(n_pieces, *refs):
    pieces, (wk_ref, wv_ref, kv_ref) = refs[:n_pieces], refs[n_pieces:]
    project_into(kv_ref, 0, pieces, wk_ref, wv_ref)


def project(pieces, w_key, w_value):
    n, slots, tokens, _ = pieces[0].shape
    shape = (slots, n * len(pieces), tokens, 2 * w_key.shape[1])
    return pl.pallas_call(
        functools.partial(project_kernel, len(pieces)),
        out_shape=jax.ShapeDtypeStruct(shape, BF16),
        in_specs=[VMEM] * (len(pieces) + 2),
        out_specs=VMEM,
        compiler_params=params(32),
        cost_estimate=cost(0.1),
        name="project",
    )(*pieces, w_key, w_value)


def attend_kernel(firsts, n_pieces, n_heads, n_rep, turns, fanout, spans, slot_ref, q_ref, *refs):
    n_ready = len(firsts) - 1
    ready, refs = refs[:n_ready], refs[n_ready:]
    pieces, refs = refs[:n_pieces], refs[n_pieces:]
    wk_ref, wv_ref = refs[:2]
    outs = refs[2 : 2 + n_rep]
    kv_ref, sem = refs[2 + n_rep :]
    copies = [
        pltpu.make_async_copy(ref, kv_ref.at[pl.ds(first, ref.shape[0])], sem.at[i])
        for i, (ref, first) in enumerate(zip(ready, firsts))
    ]
    for copy in copies:
        copy.start()
    project_into(kv_ref, firsts[-1], pieces, wk_ref, wv_ref)
    for copy in copies:
        copy.wait()
    heads_at, rep_at = lax.axis_index("heads"), lax.axis_index("rep")
    cols = wk_ref.shape[1]
    span_len = q_ref.shape[0] // spans
    block = spans // (n_heads * n_rep)
    tokens = kv_ref.shape[1] * kv_ref.shape[2]
    heads = [slice(h * HD, (h + 1) * HD) for h in range(cols // HD)]
    for at, t in enumerate(turns):
        for s in range(n_rep):
            owner = lax.rem(heads_at + t, n_heads) * n_rep + lax.rem(rep_at + s, n_rep)
            for i in range(block):
                span = owner * block + i
                slots = [slot_ref[span * fanout + k] for k in range(fanout)]
                rows = pl.ds(pl.multiple_of(span * span_len, span_len), span_len)

                def side(lanes):
                    return jnp.concatenate(
                        [kv_ref[slot, :, :, lanes].reshape(tokens, HD) for slot in slots], axis=0
                    )

                logits = [dot_t(q_ref[rows, lanes], side(lanes)) for lanes in heads]
                tops = [jnp.max(part, axis=1, keepdims=True) for part in logits]
                weights = [jnp.exp((part - top) * HD ** (-0.5)) for part, top in zip(logits, tops)]
                scales = [1.0 / jnp.sum(part, axis=1, keepdims=True) for part in weights]
                mixed = [
                    dot(part.astype(BF16), side(slice(cols + lanes.start, cols + lanes.stop)))
                    for part, lanes in zip(weights, heads)
                ]
                for part, scale, lanes in zip(mixed, scales, heads):
                    outs[s][at, i * span_len : (i + 1) * span_len, lanes] = (part * scale).astype(BF16)


def attend(slot, queries, ready, pieces, w_key, w_value, n_heads, n_rep, turns, fanout, spans):
    firsts = [0]
    for kv in ready:
        firsts.append(firsts[-1] + kv.shape[0])
    n, slots, tokens, _ = pieces[0].shape
    cols = w_key.shape[1]
    rows = queries.shape[0] // (n_heads * n_rep)
    kv_shape = (firsts[-1] + slots, n * len(pieces), tokens, 2 * cols)
    return pl.pallas_call(
        functools.partial(attend_kernel, firsts, len(pieces), n_heads, n_rep, turns, fanout, spans),
        out_shape=[jax.ShapeDtypeStruct((len(turns), rows, cols), BF16)] * n_rep,
        in_specs=[SMEM, VMEM] + [ANY] * len(ready) + [VMEM] * (len(pieces) + 2),
        out_specs=[VMEM] * n_rep,
        scratch_shapes=[pltpu.VMEM(kv_shape, BF16), pltpu.SemaphoreType.DMA((max(1, len(ready)),))],
        compiler_params=params(40),
        cost_estimate=cost(0.001),
        name="attend",
    )(slot, queries, *ready, *pieces, w_key, w_value)


def out_kernel(n_rep, *refs):
    mixed, weights, out_ref = refs[:n_rep], refs[n_rep:-1], refs[-1]
    out_ref[...] = sum(dot(a[0], w[...]) for a, w in zip(mixed, weights)).astype(BF16)


def out_project(mixed, weights, t, start, stop, tile):
    _, rows, depth = mixed[0].shape
    base = start // tile
    return pl.pallas_call(
        functools.partial(out_kernel, len(mixed)),
        grid=((stop - start) // tile,),
        out_shape=jax.ShapeDtypeStruct((rows, stop - start), BF16),
        in_specs=[pl.BlockSpec((1, rows, depth), lambda j: (t, 0, 0))] * len(mixed)
        + [pl.BlockSpec((depth, tile), lambda j: (0, base + j))] * len(mixed),
        out_specs=pl.BlockSpec((rows, tile), lambda j: (0, j)),
        compiler_params=params(16),
        cost_estimate=cost(0.001),
        name="out_project",
    )(*mixed, *weights)


def after(values, *earlier):
    return lax.optimization_barrier((values, earlier))[0]


def shards(queries, span_states, store, entry_ids, owners, w_key, w_value, w_out):
    n_lanes, n_heads, n_rep = (lax.axis_size(name) for name in ("lanes", "heads", "rep"))
    spans, fanout = entry_ids.shape
    requests = spans * fanout
    cap = max(2, (requests + n_lanes - 1) // n_lanes)
    span_len = queries.shape[0] // spans

    def over_heads(array):
        return [array] + [lax.ppermute(array, "heads", shift_pairs(n_heads, s)) for s in range(1, n_heads)]

    def over_rep(array):
        return [array] + [lax.ppermute(array, "rep", shift_pairs(n_rep, s)) for s in range(1, n_rep)]

    items = []
    for d in range(1, n_lanes):
        cuts = (0, cap // 2, cap) if d in (1, n_lanes - 1) else (0, cap)
        items += [(d, low, high) for low, high in zip(cuts, cuts[1:])]
    size = max(1, -(-(len(items) - 2) // LATER_GROUPS))
    cuts = [0] + list(range(2, len(items), size)) + [len(items)]
    parts = [range(low, high) for low, high in zip(cuts, cuts[1:])]

    own = jnp.concatenate([owners.T, entry_ids.T], axis=0)
    asked = [lax.ppermute(own, "lanes", lane_pairs(n_lanes, d, False)) for d in range(1, n_lanes)]
    w_outs = over_rep(w_out)
    req, slot, pick = plan(own, n_lanes, cap)
    encoded = encode_local(req, pick, span_states, store, cap, fanout, span_len)
    blocks = fetch(after(asked, w_outs, encoded), store, items, cap)

    def send(part, *earlier):
        ready = after([blocks[i] for i in part], *earlier)
        return [
            lax.ppermute(block, "lanes", lane_pairs(n_lanes, items[i][0], True))
            for block, i in zip(ready, part)
        ]

    crossed, pieces, kvs = [over_heads(encoded)], [], []
    arrived = [None] + [send(part) for part in parts[:2]]
    last = blocks
    for i, part in enumerate(parts, 1):
        if i + 2 <= len(parts):
            arrived.append(send(parts[i + 1], arrived[i], last))
        first = items[part[0]][0] * cap + items[part[0]][1]
        encoded = encode(req, span_states, after(arrived[i], last), first, fanout, span_len, ENCODE_COST[i])
        crossed.append(over_heads(encoded))
        last = encoded
        if i >= 2:
            last = project(after(pieces[i - 2], last), w_key, w_value)
            kvs.append(last)
        if i < len(parts):
            last = jnp.stack(after(crossed[i - 1], last))
            pieces.append(over_rep(last))
    ends = [jnp.concatenate(pair, axis=0) for pair in zip(*after(crossed[-2:], kvs))]
    pieces = over_rep(jnp.stack(ends))

    def mix(turns, q):
        outs = attend(slot, q, kvs, pieces, w_key, w_value, n_heads, n_rep, turns, fanout, spans)
        return [outs[0]] + [
            lax.ppermute(outs[s], "rep", shift_pairs(n_rep, s)) for s in range(1, n_rep)
        ]

    width = w_out.shape[1]
    tile = min(COL_TILE, width)
    cuts = [width // tile * part // 16 * tile for part in (0, 6, 11, 14)] + [width]
    mixed = mix(list(range(1, n_heads)), queries)
    received, partials = [], []
    for t in range(1, n_heads):
        sent = []
        for start, stop in zip(cuts, cuts[1:]):
            partial = out_project(mixed, w_outs, t - 1, start, stop, tile)
            partial, mixed = lax.optimization_barrier((partial, mixed))
            partials.append(partial)
            sent.append(lax.ppermute(partial, "heads", shift_pairs(n_heads, t)))
        received.append(jnp.concatenate(sent, axis=1))
    total = out_project(mix([0], after(queries, partials)), w_outs, 0, 0, width, tile).astype(F32)
    for part in received:
        total = total + part.astype(F32)
    return total.astype(BF16)


def solution(mesh):
    return jax.shard_map(
        shards,
        mesh=mesh,
        in_specs=(
            P(("groups", "lanes"), ("heads", "rep")),
            P(("groups", "lanes"), None),
            P(("groups", "lanes"), ("heads", "rep"), None),
            P(("groups", "lanes"), None),
            P(("groups", "lanes"), None),
            P(None, ("heads", "rep")),
            P(None, ("heads", "rep")),
            P(("heads", "rep"), None),
        ),
        out_specs=P(("groups", "lanes", "heads", "rep"), None),
        check_vma=False,
    )
```

```python
import functools

import jax
import jax.numpy as jnp
from jax import lax
from jax.experimental import pallas as pl
from jax.experimental.pallas import tpu as pltpu
from jax.sharding import PartitionSpec as P

HD = 128
ENCODER_HEAD_DIM = 128
F32 = jnp.float32
BF16 = jnp.bfloat16
LATER_GROUPS = 2
COL_TILE = 512
ENCODE_COST = (None, 0.1, 10, 10)

VMEM = pl.BlockSpec(memory_space=pltpu.VMEM)
SMEM = pl.BlockSpec(memory_space=pltpu.SMEM)
ANY = pl.BlockSpec(memory_space=pl.ANY)


def params(mib):
    return pltpu.CompilerParams(vmem_limit_bytes=mib * 2**20)


def cost(gflops):
    return pl.CostEstimate(flops=int(gflops * 10**9), bytes_accessed=1024, transcendentals=0)


def apart(n, a, b):
    if n & (n - 1) == 0:
        return a ^ b
    return lax.rem(b - a + n, n)


def lane_pairs(n, d, reply):
    if n & (n - 1) == 0:
        return [(i, i ^ d) for i in range(n)]
    return [(i, (i - d if reply else i + d) % n) for i in range(n)]


def shift_pairs(n, s):
    return [(i, (i + s) % n) for i in range(n)]


def dot_t(a, b):
    return lax.dot_general(a, b, (((1,), (1,)), ((), ())), preferred_element_type=F32)


def dot(a, b):
    return jnp.dot(a, b, preferred_element_type=F32)


def plan_kernel(order, cap, own_ref, req_ref, slot_ref, pick_ref, next_ref):
    n_lanes = len(order)
    lane = lax.axis_index("lanes")
    fanout, spans = own_ref.shape[0] // 2, own_ref.shape[1]
    for i, d in enumerate(order):
        next_ref[d] = i * cap
    for i in range(n_lanes * cap):
        pick_ref[i] = 0
        req_ref[i] = 0
    for j in range(fanout * spans):
        span, k = j // fanout, j % fanout
        d = apart(n_lanes, lane, own_ref[k, span])
        slot = next_ref[d]
        next_ref[d] = slot + 1
        pick_ref[slot] = own_ref[fanout + k, span]
        req_ref[slot] = j
        slot_ref[j] = slot


def plan(own, order, cap):
    table = jax.ShapeDtypeStruct((len(order) * cap,), jnp.int32)
    return pl.pallas_call(
        functools.partial(plan_kernel, order, cap),
        out_shape=(table, jax.ShapeDtypeStruct((own.size // 2,), jnp.int32), table),
        in_specs=[SMEM],
        out_specs=(SMEM, SMEM, SMEM),
        scratch_shapes=[pltpu.SMEM((len(order),), jnp.int32)],
        compiler_params=params(16),
        cost_estimate=cost(10),
        name="plan",
    )(own)


def fetch_kernel(items, cap, *refs):
    others = max(d for d, _, _ in items)
    asked, store_ref, refs = refs[:others], refs[others], refs[others + 1 :]
    blocks, pick_ref = refs[:-1], refs[-1]
    lane = lax.axis_index("lanes")
    fanout, spans = asked[0].shape[0] // 2, asked[0].shape[1]
    for i in range(others * cap):
        pick_ref[i] = 0
    for d in range(others):
        place = d * cap
        for span in range(spans):
            for k in range(fanout):
                pick_ref[place] = asked[d][fanout + k, span]
                place = place + (asked[d][k, span] == lane).astype(jnp.int32)
    for block, (d, low, high) in zip(blocks, items):
        for s in range(low, high):
            block[s - low] = store_ref[pick_ref[(d - 1) * cap + s]]


def fetch(asked, store, items, cap):
    others = len(asked)
    return pl.pallas_call(
        functools.partial(fetch_kernel, items, cap),
        out_shape=[
            jax.ShapeDtypeStruct((high - low,) + store.shape[1:], store.dtype) for _, low, high in items
        ],
        in_specs=[SMEM] * others + [VMEM],
        out_specs=[VMEM] * len(items),
        scratch_shapes=[pltpu.SMEM((others * cap + 1,), jnp.int32)],
        compiler_params=params(16),
        cost_estimate=cost(10),
        name="fetch",
    )(*asked, store)


def encode_pairs(width):
    step = 2 * ENCODER_HEAD_DIM
    return [(start, min(start + step, width)) for start in range(0, width, step)]


def spread(states, start, stop):
    part = states[:, start:stop]
    heads = (stop - start) // ENCODER_HEAD_DIM
    if heads == 1:
        return part
    rows = jnp.concatenate([part] * heads, axis=0)
    return jnp.where(own_cells(rows.shape, part.shape[0]), rows, jnp.zeros_like(rows))


def own_cells(shape, keys):
    row = lax.broadcasted_iota(jnp.int32, shape, 0)
    col = lax.broadcasted_iota(jnp.int32, shape, 1)
    return (row >= keys) == (col >= ENCODER_HEAD_DIM)


def softmax_top(logits, keys):
    if logits.shape[1] == keys:
        return jnp.max(logits, axis=1, keepdims=True)
    first = lax.broadcasted_iota(jnp.int32, logits.shape, 1) < keys
    low = jnp.max(jnp.where(first, logits, -jnp.inf), axis=1, keepdims=True)
    high = jnp.max(jnp.where(first, -jnp.inf, logits), axis=1, keepdims=True)
    return jnp.where(first, low, high)


def encode_block(block, out_ref, first, req_ref, states_ref, fanout, span_len):
    scale = ENCODER_HEAD_DIM ** (-0.5)
    runs = encode_pairs(states_ref.shape[1])
    units = []
    for s in range(block.shape[0]):
        span = lax.div(req_ref[first + s], fanout)
        states = states_ref[pl.ds(pl.multiple_of(span * span_len, span_len), span_len), :]
        units += [(s, start, stop, spread(states, start, stop)) for start, stop in runs]
    logits = [dot_t(block[s, :, start:stop], keys) for s, start, stop, keys in units]
    tops = [softmax_top(part, span_len) for part in logits]
    weights = [jnp.exp((part - top) * scale).astype(BF16) for part, top in zip(logits, tops)]
    mixed = [dot(part, keys) for part, (_, _, _, keys) in zip(weights, units)]
    sums = []
    for part, (_, start, stop, keys) in zip(weights, units):
        ones = jnp.ones(keys.shape, BF16)
        if stop - start > ENCODER_HEAD_DIM:
            ones = jnp.where(own_cells(keys.shape, span_len), ones, jnp.zeros_like(ones))
        sums.append(dot(part, ones))
    for (s, start, stop, _), top, bottom in zip(units, mixed, sums):
        token = block[s, :, start:stop].astype(F32)
        out_ref[s, :, start:stop] = (token + top / bottom).astype(BF16)


def encode_kernel(first, fanout, span_len, req_ref, states_ref, *refs):
    blocks, out_ref = refs[:-1], refs[-1]
    at = 0
    for block in blocks:
        stop = at + block.shape[0]
        encode_block(block, out_ref.at[at:stop], first + at, req_ref, states_ref, fanout, span_len)
        at = stop


def encode(req, span_states, blocks, first, fanout, span_len, gflops):
    slots = sum(block.shape[0] for block in blocks)
    return pl.pallas_call(
        functools.partial(encode_kernel, first, fanout, span_len),
        out_shape=jax.ShapeDtypeStruct((slots,) + blocks[0].shape[1:], BF16),
        in_specs=[SMEM, VMEM] + [VMEM] * len(blocks),
        out_specs=VMEM,
        compiler_params=params(16),
        cost_estimate=cost(gflops),
        name="encode",
    )(req, span_states, *blocks)


def encode_local_kernel(fanout, span_len, req_ref, pick_ref, states_ref, store_ref, out_ref, tokens_ref):
    for s in range(out_ref.shape[0]):
        tokens_ref[s] = store_ref[pick_ref[s]]
    encode_block(tokens_ref, out_ref, 0, req_ref, states_ref, fanout, span_len)


def encode_local(req, pick, span_states, store, cap, fanout, span_len):
    block = (cap,) + store.shape[1:]
    return pl.pallas_call(
        functools.partial(encode_local_kernel, fanout, span_len),
        out_shape=jax.ShapeDtypeStruct(block, BF16),
        in_specs=[SMEM, SMEM, VMEM, VMEM],
        out_specs=VMEM,
        scratch_shapes=[pltpu.VMEM(block, BF16)],
        compiler_params=params(16),
        cost_estimate=cost(10),
        name="encode_local",
    )(req, pick, span_states, store)


def project_into(kv_ref, first, pieces, wk_ref, wv_ref):
    n, slots, tokens, width = pieces[0].shape
    rows = jnp.concatenate([piece[...].reshape(n * slots * tokens, width) for piece in pieces], axis=0)
    cols = wk_ref.shape[1]
    for side, weight in enumerate((wk_ref, wv_ref)):
        made = dot(rows, weight[...]).astype(BF16)
        for p in range(n * len(pieces)):
            part = made[p * slots * tokens : (p + 1) * slots * tokens]
            kv_ref[first : first + slots, p, :, side * cols : (side + 1) * cols] = part.reshape(
                slots, tokens, cols
            )


def project_kernel(n_pieces, *refs):
    pieces, (wk_ref, wv_ref, kv_ref) = refs[:n_pieces], refs[n_pieces:]
    project_into(kv_ref, 0, pieces, wk_ref, wv_ref)


def project(pieces, w_key, w_value):
    n, slots, tokens, _ = pieces[0].shape
    shape = (slots, n * len(pieces), tokens, 2 * w_key.shape[1])
    return pl.pallas_call(
        functools.partial(project_kernel, len(pieces)),
        out_shape=jax.ShapeDtypeStruct(shape, BF16),
        in_specs=[VMEM] * (len(pieces) + 2),
        out_specs=VMEM,
        compiler_params=params(32),
        cost_estimate=cost(10),
        name="project",
    )(*pieces, w_key, w_value)


def attend_kernel(firsts, n_pieces, n_heads, n_rep, turns, fanout, spans, slot_ref, q_ref, *refs):
    n_ready = len(firsts) - 1
    ready, refs = refs[:n_ready], refs[n_ready:]
    pieces, refs = refs[:n_pieces], refs[n_pieces:]
    wk_ref, wv_ref = refs[:2]
    outs = refs[2 : 2 + n_rep]
    kv_ref, sem = refs[2 + n_rep :]
    copies = [
        pltpu.make_async_copy(ref, kv_ref.at[pl.ds(first, ref.shape[0])], sem.at[i])
        for i, (ref, first) in enumerate(zip(ready, firsts))
    ]
    for copy in copies:
        copy.start()
    project_into(kv_ref, firsts[-1], pieces, wk_ref, wv_ref)
    for copy in copies:
        copy.wait()
    heads_at, rep_at = lax.axis_index("heads"), lax.axis_index("rep")
    cols = wk_ref.shape[1]
    span_len = q_ref.shape[0] // spans
    block = spans // (n_heads * n_rep)
    tokens = kv_ref.shape[1] * kv_ref.shape[2]
    heads = [slice(h * HD, (h + 1) * HD) for h in range(cols // HD)]
    for at, t in enumerate(turns):
        for s in range(n_rep):
            owner = lax.rem(heads_at + t, n_heads) * n_rep + lax.rem(rep_at + s, n_rep)
            for i in range(block):
                span = owner * block + i
                slots = [slot_ref[span * fanout + k] for k in range(fanout)]
                rows = pl.ds(pl.multiple_of(span * span_len, span_len), span_len)

                def side(lanes):
                    return jnp.concatenate(
                        [kv_ref[slot, :, :, lanes].reshape(tokens, HD) for slot in slots], axis=0
                    )

                logits = [dot_t(q_ref[rows, lanes], side(lanes)) for lanes in heads]
                tops = [jnp.max(part, axis=1, keepdims=True) for part in logits]
                weights = [jnp.exp((part - top) * HD ** (-0.5)) for part, top in zip(logits, tops)]
                scales = [1.0 / jnp.sum(part, axis=1, keepdims=True) for part in weights]
                mixed = [
                    dot(part.astype(BF16), side(slice(cols + lanes.start, cols + lanes.stop)))
                    for part, lanes in zip(weights, heads)
                ]
                for part, scale, lanes in zip(mixed, scales, heads):
                    outs[s][at, i * span_len : (i + 1) * span_len, lanes] = (part * scale).astype(BF16)


def attend(slot, queries, ready, pieces, w_key, w_value, n_heads, n_rep, turns, fanout, spans):
    firsts = [0]
    for kv in ready:
        firsts.append(firsts[-1] + kv.shape[0])
    n, slots, tokens, _ = pieces[0].shape
    cols = w_key.shape[1]
    rows = queries.shape[0] // (n_heads * n_rep)
    kv_shape = (firsts[-1] + slots, n * len(pieces), tokens, 2 * cols)
    return pl.pallas_call(
        functools.partial(attend_kernel, firsts, len(pieces), n_heads, n_rep, turns, fanout, spans),
        out_shape=[jax.ShapeDtypeStruct((len(turns), rows, cols), BF16)] * n_rep,
        in_specs=[SMEM, VMEM] + [ANY] * len(ready) + [VMEM] * (len(pieces) + 2),
        out_specs=[VMEM] * n_rep,
        scratch_shapes=[pltpu.VMEM(kv_shape, BF16), pltpu.SemaphoreType.DMA((max(1, len(ready)),))],
        compiler_params=params(40),
        cost_estimate=cost(0.001),
        name="attend",
    )(slot, queries, *ready, *pieces, w_key, w_value)


def out_kernel(n_rep, *refs):
    mixed, weights, out_ref = refs[:n_rep], refs[n_rep:-1], refs[-1]
    out_ref[...] = sum(dot(a[0], w[...]) for a, w in zip(mixed, weights)).astype(BF16)


def out_project(mixed, weights, t, start, stop, tile):
    _, rows, depth = mixed[0].shape
    base = start // tile
    return pl.pallas_call(
        functools.partial(out_kernel, len(mixed)),
        grid=((stop - start) // tile,),
        out_shape=jax.ShapeDtypeStruct((rows, stop - start), BF16),
        in_specs=[pl.BlockSpec((1, rows, depth), lambda j: (t, 0, 0))] * len(mixed)
        + [pl.BlockSpec((depth, tile), lambda j: (0, base + j))] * len(mixed),
        out_specs=pl.BlockSpec((rows, tile), lambda j: (0, j)),
        compiler_params=params(16),
        cost_estimate=cost(0.001),
        name="out_project",
    )(*mixed, *weights)


def after(values, *earlier):
    return lax.optimization_barrier((values, earlier))[0]


def shards(queries, span_states, store, entry_ids, owners, w_key, w_value, w_out):
    n_lanes, n_heads, n_rep = (lax.axis_size(name) for name in ("lanes", "heads", "rep"))
    spans, fanout = entry_ids.shape
    requests = spans * fanout
    cap = max(2, (requests + n_lanes - 1) // n_lanes)
    span_len = queries.shape[0] // spans

    def over_heads(array):
        return [array] + [lax.ppermute(array, "heads", shift_pairs(n_heads, s)) for s in range(1, n_heads)]

    def over_rep(array):
        return [array] + [lax.ppermute(array, "rep", shift_pairs(n_rep, s)) for s in range(1, n_rep)]

    order = list(range(n_lanes))
    items = []
    for d in order[1:]:
        cuts = (0, cap // 2, cap) if d == 1 else (0, cap)
        items += [(d, low, high) for low, high in zip(cuts, cuts[1:])]
    size = max(1, -(-(len(items) - 2) // LATER_GROUPS))
    cuts = [0] + list(range(2, len(items), size)) + [len(items)]
    parts = [range(low, high) for low, high in zip(cuts, cuts[1:])]

    own = jnp.concatenate([owners.T, entry_ids.T], axis=0)
    asked = [lax.ppermute(own, "lanes", lane_pairs(n_lanes, d, False)) for d in range(1, n_lanes)]
    w_outs = over_rep(w_out)
    req, slot, pick = plan(own, order, cap)
    encoded = encode_local(req, pick, span_states, store, cap, fanout, span_len)
    blocks = fetch(after(asked, w_outs, encoded), store, items, cap)

    def send(part, *earlier):
        ready = after([blocks[i] for i in part], *earlier)
        return [
            lax.ppermute(block, "lanes", lane_pairs(n_lanes, items[i][0], True))
            for block, i in zip(ready, part)
        ]

    crossed, pieces = [over_heads(encoded)], []
    arrived = [None] + [send(part) for part in parts[:2]]
    last = blocks
    for i, part in enumerate(parts, 1):
        if i + 2 <= len(parts):
            arrived.append(send(parts[i + 1], arrived[i], last))
        first = items[part[0]][0] * cap + items[part[0]][1]
        encoded = encode(
            req, span_states, after(arrived[i], last), first, fanout, span_len, ENCODE_COST[i]
        )
        crossed.append(over_heads(encoded))
        last = encoded
        while i > 1 and len(pieces) < i:
            last = jnp.stack(after(crossed[len(pieces)], last))
            pieces.append(over_rep(last))
    kvs = []
    while len(kvs) < len(pieces):
        last = project(after(pieces[len(kvs)], last), w_key, w_value)
        kvs.append(last)
    pieces = over_rep(jnp.stack(after(crossed[-1], kvs)))

    def mix(turns, q):
        outs = attend(slot, q, kvs, pieces, w_key, w_value, n_heads, n_rep, turns, fanout, spans)
        return [outs[0]] + [
            lax.ppermute(outs[s], "rep", shift_pairs(n_rep, s)) for s in range(1, n_rep)
        ]

    width = w_out.shape[1]
    tile = min(COL_TILE, width)
    cuts = [width // tile * part // 8 * tile for part in (0, 3, 5, 7)] + [width]
    mixed = mix(list(range(1, n_heads)), queries)
    received, partials = [], []
    for t in range(1, n_heads):
        sent = []
        for start, stop in zip(cuts, cuts[1:]):
            partial = out_project(mixed, w_outs, t - 1, start, stop, tile)
            partial, mixed = lax.optimization_barrier((partial, mixed))
            partials.append(partial)
            sent.append(lax.ppermute(partial, "heads", shift_pairs(n_heads, t)))
        received.append(jnp.concatenate(sent, axis=1))
    total = out_project(mix([0], after(queries, partials)), w_outs, 0, 0, width, tile).astype(F32)
    for part in received:
        total = total + part.astype(F32)
    return total.astype(BF16)


def solution(mesh):
    return jax.shard_map(
        shards,
        mesh=mesh,
        in_specs=(
            P(("groups", "lanes"), ("heads", "rep")),
            P(("groups", "lanes"), None),
            P(("groups", "lanes"), ("heads", "rep"), None),
            P(("groups", "lanes"), None),
            P(("groups", "lanes"), None),
            P(None, ("heads", "rep")),
            P(None, ("heads", "rep")),
            P(("heads", "rep"), None),
        ),
        out_specs=P(("groups", "lanes", "heads", "rep"), None),
        check_vma=False,
    )
```

```python
import functools

import jax
import jax.numpy as jnp
from jax import lax
from jax.experimental import pallas as pl
from jax.experimental.pallas import tpu as pltpu
from jax.sharding import PartitionSpec as P

HD = 128
ENCODER_HEAD_DIM = 128
F32 = jnp.float32
BF16 = jnp.bfloat16
LATER_GROUPS = 2
COL_TILE = 512
ENCODE_COST = (None, 0.1, 10, 10)

VMEM = pl.BlockSpec(memory_space=pltpu.VMEM)
SMEM = pl.BlockSpec(memory_space=pltpu.SMEM)
ANY = pl.BlockSpec(memory_space=pl.ANY)


def params(mib):
    return pltpu.CompilerParams(vmem_limit_bytes=mib * 2**20)


def cost(gflops):
    return pl.CostEstimate(flops=int(gflops * 10**9), bytes_accessed=1024, transcendentals=0)


def apart(n, a, b):
    if n & (n - 1) == 0:
        return a ^ b
    return lax.rem(b - a + n, n)


def lane_pairs(n, d, reply):
    if n & (n - 1) == 0:
        return [(i, i ^ d) for i in range(n)]
    return [(i, (i - d if reply else i + d) % n) for i in range(n)]


def shift_pairs(n, s):
    return [(i, (i + s) % n) for i in range(n)]


def dot_t(a, b):
    return lax.dot_general(a, b, (((1,), (1,)), ((), ())), preferred_element_type=F32)


def dot(a, b):
    return jnp.dot(a, b, preferred_element_type=F32)


def plan_kernel(order, cap, own_ref, req_ref, slot_ref, pick_ref, next_ref):
    n_lanes = len(order)
    lane = lax.axis_index("lanes")
    fanout, spans = own_ref.shape[0] // 2, own_ref.shape[1]
    for i, d in enumerate(order):
        next_ref[d] = i * cap
    for i in range(n_lanes * cap):
        pick_ref[i] = 0
        req_ref[i] = 0
    for j in range(fanout * spans):
        span, k = j // fanout, j % fanout
        d = apart(n_lanes, lane, own_ref[k, span])
        slot = next_ref[d]
        next_ref[d] = slot + 1
        pick_ref[slot] = own_ref[fanout + k, span]
        req_ref[slot] = j
        slot_ref[j] = slot


def plan(own, order, cap):
    table = jax.ShapeDtypeStruct((len(order) * cap,), jnp.int32)
    return pl.pallas_call(
        functools.partial(plan_kernel, order, cap),
        out_shape=(table, jax.ShapeDtypeStruct((own.size // 2,), jnp.int32), table),
        in_specs=[SMEM],
        out_specs=(SMEM, SMEM, SMEM),
        scratch_shapes=[pltpu.SMEM((len(order),), jnp.int32)],
        compiler_params=params(16),
        cost_estimate=cost(10),
        name="plan",
    )(own)


def fetch_kernel(items, cap, *refs):
    others = max(d for d, _, _ in items)
    asked, store_ref, refs = refs[:others], refs[others], refs[others + 1 :]
    blocks, pick_ref = refs[:-1], refs[-1]
    lane = lax.axis_index("lanes")
    fanout, spans = asked[0].shape[0] // 2, asked[0].shape[1]
    for i in range(others * cap):
        pick_ref[i] = 0
    for d in range(others):
        place = d * cap
        for span in range(spans):
            for k in range(fanout):
                pick_ref[place] = asked[d][fanout + k, span]
                place = place + (asked[d][k, span] == lane).astype(jnp.int32)
    for block, (d, low, high) in zip(blocks, items):
        for s in range(low, high):
            block[s - low] = store_ref[pick_ref[(d - 1) * cap + s]]


def fetch(asked, store, items, cap):
    others = len(asked)
    return pl.pallas_call(
        functools.partial(fetch_kernel, items, cap),
        out_shape=[
            jax.ShapeDtypeStruct((high - low,) + store.shape[1:], store.dtype) for _, low, high in items
        ],
        in_specs=[SMEM] * others + [VMEM],
        out_specs=[VMEM] * len(items),
        scratch_shapes=[pltpu.SMEM((others * cap + 1,), jnp.int32)],
        compiler_params=params(16),
        cost_estimate=cost(10),
        name="fetch",
    )(*asked, store)


def encode_pairs(width):
    step = 2 * ENCODER_HEAD_DIM
    return [(start, min(start + step, width)) for start in range(0, width, step)]


def spread(states, start, stop):
    part = states[:, start:stop]
    heads = (stop - start) // ENCODER_HEAD_DIM
    if heads == 1:
        return part
    rows = jnp.concatenate([part] * heads, axis=0)
    return jnp.where(own_cells(rows.shape, part.shape[0]), rows, jnp.zeros_like(rows))


def own_cells(shape, keys):
    row = lax.broadcasted_iota(jnp.int32, shape, 0)
    col = lax.broadcasted_iota(jnp.int32, shape, 1)
    return (row >= keys) == (col >= ENCODER_HEAD_DIM)


def softmax_top(logits, keys):
    if logits.shape[1] == keys:
        return jnp.max(logits, axis=1, keepdims=True)
    first = lax.broadcasted_iota(jnp.int32, logits.shape, 1) < keys
    low = jnp.max(jnp.where(first, logits, -jnp.inf), axis=1, keepdims=True)
    high = jnp.max(jnp.where(first, -jnp.inf, logits), axis=1, keepdims=True)
    return jnp.where(first, low, high)


def encode_block(block, out_ref, first, req_ref, states_ref, fanout, span_len):
    scale = ENCODER_HEAD_DIM ** (-0.5)
    runs = encode_pairs(states_ref.shape[1])
    units = []
    for s in range(block.shape[0]):
        span = lax.div(req_ref[first + s], fanout)
        states = states_ref[pl.ds(pl.multiple_of(span * span_len, span_len), span_len), :]
        units += [(s, start, stop, spread(states, start, stop)) for start, stop in runs]
    logits = [dot_t(block[s, :, start:stop], keys) for s, start, stop, keys in units]
    tops = [softmax_top(part, span_len) for part in logits]
    weights = [jnp.exp((part - top) * scale).astype(BF16) for part, top in zip(logits, tops)]
    mixed = [dot(part, keys) for part, (_, _, _, keys) in zip(weights, units)]
    sums = []
    for part, (_, start, stop, keys) in zip(weights, units):
        ones = jnp.ones(keys.shape, BF16)
        if stop - start > ENCODER_HEAD_DIM:
            ones = jnp.where(own_cells(keys.shape, span_len), ones, jnp.zeros_like(ones))
        sums.append(dot(part, ones))
    for (s, start, stop, _), top, bottom in zip(units, mixed, sums):
        token = block[s, :, start:stop].astype(F32)
        out_ref[s, :, start:stop] = (token + top / bottom).astype(BF16)


def encode_kernel(first, fanout, span_len, req_ref, states_ref, *refs):
    blocks, out_ref = refs[:-1], refs[-1]
    at = 0
    for block in blocks:
        stop = at + block.shape[0]
        encode_block(block, out_ref.at[at:stop], first + at, req_ref, states_ref, fanout, span_len)
        at = stop


def encode(req, span_states, blocks, first, fanout, span_len, gflops):
    slots = sum(block.shape[0] for block in blocks)
    return pl.pallas_call(
        functools.partial(encode_kernel, first, fanout, span_len),
        out_shape=jax.ShapeDtypeStruct((slots,) + blocks[0].shape[1:], BF16),
        in_specs=[SMEM, VMEM] + [VMEM] * len(blocks),
        out_specs=VMEM,
        compiler_params=params(16),
        cost_estimate=cost(gflops),
        name="encode",
    )(req, span_states, *blocks)


def encode_local_kernel(fanout, span_len, req_ref, pick_ref, states_ref, store_ref, out_ref, tokens_ref):
    for s in range(out_ref.shape[0]):
        tokens_ref[s] = store_ref[pick_ref[s]]
    encode_block(tokens_ref, out_ref, 0, req_ref, states_ref, fanout, span_len)


def encode_local(req, pick, span_states, store, cap, fanout, span_len):
    block = (cap,) + store.shape[1:]
    return pl.pallas_call(
        functools.partial(encode_local_kernel, fanout, span_len),
        out_shape=jax.ShapeDtypeStruct(block, BF16),
        in_specs=[SMEM, SMEM, VMEM, VMEM],
        out_specs=VMEM,
        scratch_shapes=[pltpu.VMEM(block, BF16)],
        compiler_params=params(16),
        cost_estimate=cost(10),
        name="encode_local",
    )(req, pick, span_states, store)


def project_into(kv_ref, first, pieces, wk_ref, wv_ref):
    n, slots, tokens, width = pieces[0].shape
    rows = jnp.concatenate([piece[...].reshape(n * slots * tokens, width) for piece in pieces], axis=0)
    cols = wk_ref.shape[1]
    for side, weight in enumerate((wk_ref, wv_ref)):
        made = dot(rows, weight[...]).astype(BF16)
        for p in range(n * len(pieces)):
            part = made[p * slots * tokens : (p + 1) * slots * tokens]
            kv_ref[first : first + slots, p, :, side * cols : (side + 1) * cols] = part.reshape(
                slots, tokens, cols
            )


def project_kernel(n_pieces, *refs):
    pieces, (wk_ref, wv_ref, kv_ref) = refs[:n_pieces], refs[n_pieces:]
    project_into(kv_ref, 0, pieces, wk_ref, wv_ref)


def project(pieces, w_key, w_value):
    n, slots, tokens, _ = pieces[0].shape
    shape = (slots, n * len(pieces), tokens, 2 * w_key.shape[1])
    return pl.pallas_call(
        functools.partial(project_kernel, len(pieces)),
        out_shape=jax.ShapeDtypeStruct(shape, BF16),
        in_specs=[VMEM] * (len(pieces) + 2),
        out_specs=VMEM,
        compiler_params=params(32),
        cost_estimate=cost(10),
        name="project",
    )(*pieces, w_key, w_value)


def attend_kernel(firsts, n_pieces, n_heads, n_rep, turns, fanout, spans, slot_ref, q_ref, *refs):
    n_ready = len(firsts) - 1
    ready, refs = refs[:n_ready], refs[n_ready:]
    pieces, refs = refs[:n_pieces], refs[n_pieces:]
    wk_ref, wv_ref = refs[:2]
    outs = refs[2 : 2 + n_rep]
    kv_ref, sem = refs[2 + n_rep :]
    copies = [
        pltpu.make_async_copy(ref, kv_ref.at[pl.ds(first, ref.shape[0])], sem.at[i])
        for i, (ref, first) in enumerate(zip(ready, firsts))
    ]
    for copy in copies:
        copy.start()
    project_into(kv_ref, firsts[-1], pieces, wk_ref, wv_ref)
    for copy in copies:
        copy.wait()
    heads_at, rep_at = lax.axis_index("heads"), lax.axis_index("rep")
    cols = wk_ref.shape[1]
    span_len = q_ref.shape[0] // spans
    block = spans // (n_heads * n_rep)
    tokens = kv_ref.shape[1] * kv_ref.shape[2]
    heads = [slice(h * HD, (h + 1) * HD) for h in range(cols // HD)]
    for at, t in enumerate(turns):
        for s in range(n_rep):
            owner = lax.rem(heads_at + t, n_heads) * n_rep + lax.rem(rep_at + s, n_rep)
            for i in range(block):
                span = owner * block + i
                slots = [slot_ref[span * fanout + k] for k in range(fanout)]
                rows = pl.ds(pl.multiple_of(span * span_len, span_len), span_len)

                def side(lanes):
                    return jnp.concatenate(
                        [kv_ref[slot, :, :, lanes].reshape(tokens, HD) for slot in slots], axis=0
                    )

                logits = [dot_t(q_ref[rows, lanes], side(lanes)) for lanes in heads]
                tops = [jnp.max(part, axis=1, keepdims=True) for part in logits]
                weights = [jnp.exp((part - top) * HD ** (-0.5)) for part, top in zip(logits, tops)]
                scales = [1.0 / jnp.sum(part, axis=1, keepdims=True) for part in weights]
                mixed = [
                    dot(part.astype(BF16), side(slice(cols + lanes.start, cols + lanes.stop)))
                    for part, lanes in zip(weights, heads)
                ]
                for part, scale, lanes in zip(mixed, scales, heads):
                    outs[s][at, i * span_len : (i + 1) * span_len, lanes] = (part * scale).astype(BF16)


def attend(slot, queries, ready, pieces, w_key, w_value, n_heads, n_rep, turns, fanout, spans):
    firsts = [0]
    for kv in ready:
        firsts.append(firsts[-1] + kv.shape[0])
    n, slots, tokens, _ = pieces[0].shape
    cols = w_key.shape[1]
    rows = queries.shape[0] // (n_heads * n_rep)
    kv_shape = (firsts[-1] + slots, n * len(pieces), tokens, 2 * cols)
    return pl.pallas_call(
        functools.partial(attend_kernel, firsts, len(pieces), n_heads, n_rep, turns, fanout, spans),
        out_shape=[jax.ShapeDtypeStruct((len(turns), rows, cols), BF16)] * n_rep,
        in_specs=[SMEM, VMEM] + [ANY] * len(ready) + [VMEM] * (len(pieces) + 2),
        out_specs=[VMEM] * n_rep,
        scratch_shapes=[pltpu.VMEM(kv_shape, BF16), pltpu.SemaphoreType.DMA((max(1, len(ready)),))],
        compiler_params=params(40),
        cost_estimate=cost(0.001),
        name="attend",
    )(slot, queries, *ready, *pieces, w_key, w_value)


def out_kernel(n_rep, n_received, *refs):
    mixed, weights, received = refs[:n_rep], refs[n_rep : 2 * n_rep], refs[2 * n_rep : 2 * n_rep + n_received]
    total = sum(dot(a[0], w[...]) for a, w in zip(mixed, weights))
    for part in received:
        total = total + part[...].astype(F32)
    refs[-1][...] = total.astype(BF16)


def out_project(mixed, weights, t, start, stop, tile, gflops, received=(), out=None, final=False):
    _, rows, depth = mixed[0].shape
    width = weights[0].shape[1]
    base = start // tile
    n = len(mixed)
    operands = [*mixed, *weights, *received] + ([] if out is None else [out])
    return pl.pallas_call(
        functools.partial(out_kernel, n, len(received)),
        grid=((stop - start) // tile,),
        out_shape=jax.ShapeDtypeStruct((rows, width if final else stop - start), BF16),
        in_specs=[pl.BlockSpec((1, rows, depth), lambda j: (t, 0, 0))] * n
        + [pl.BlockSpec((depth, tile), lambda j: (0, base + j))] * n
        + [pl.BlockSpec((rows, tile), lambda j: (0, j))] * len(received)
        + [ANY] * (out is not None),
        out_specs=pl.BlockSpec((rows, tile), lambda j: (0, (base if final else 0) + j)),
        input_output_aliases={} if out is None else {len(operands) - 1: 0},
        compiler_params=params(16),
        cost_estimate=cost(gflops),
        name="out_final" if final else "out_project",
    )(*operands)


def after(values, *earlier):
    return lax.optimization_barrier((values, earlier))[0]


def shards(queries, span_states, store, entry_ids, owners, w_key, w_value, w_out):
    n_lanes, n_heads, n_rep = (lax.axis_size(name) for name in ("lanes", "heads", "rep"))
    spans, fanout = entry_ids.shape
    requests = spans * fanout
    cap = max(2, (requests + n_lanes - 1) // n_lanes)
    span_len = queries.shape[0] // spans

    def over_heads(array):
        return [array] + [lax.ppermute(array, "heads", shift_pairs(n_heads, s)) for s in range(1, n_heads)]

    def over_rep(array):
        return [array] + [lax.ppermute(array, "rep", shift_pairs(n_rep, s)) for s in range(1, n_rep)]

    order = list(range(n_lanes))
    items = []
    for d in order[1:]:
        cuts = (0, cap // 2, cap) if d == 1 else (0, cap)
        items += [(d, low, high) for low, high in zip(cuts, cuts[1:])]
    size = max(1, -(-(len(items) - 2) // LATER_GROUPS))
    cuts = [0] + list(range(2, len(items), size)) + [len(items)]
    parts = [range(low, high) for low, high in zip(cuts, cuts[1:])]

    own = jnp.concatenate([owners.T, entry_ids.T], axis=0)
    asked = [lax.ppermute(own, "lanes", lane_pairs(n_lanes, d, False)) for d in range(1, n_lanes)]
    req, slot, pick = plan(own, order, cap)
    encoded = encode_local(req, pick, span_states, store, cap, fanout, span_len)
    blocks = fetch(after(asked, encoded), store, items, cap)

    def send(part, *earlier):
        ready = after([blocks[i] for i in part], *earlier)
        return [
            lax.ppermute(block, "lanes", lane_pairs(n_lanes, items[i][0], True))
            for block, i in zip(ready, part)
        ]

    crossed, pieces = [over_heads(encoded)], []
    arrived = [None] + [send(part) for part in parts[:2]]
    last = blocks
    for i, part in enumerate(parts, 1):
        if i + 2 <= len(parts):
            arrived.append(send(parts[i + 1], arrived[i], last))
        first = items[part[0]][0] * cap + items[part[0]][1]
        encoded = encode(
            req, span_states, after(arrived[i], last), first, fanout, span_len, ENCODE_COST[i]
        )
        crossed.append(over_heads(encoded))
        last = encoded
        while i > 1 and len(pieces) < i:
            last = jnp.stack(after(crossed[len(pieces)], last))
            pieces.append(over_rep(last))
    w_outs = over_rep(w_out)
    kvs, last = [], after(last, w_outs)
    while len(kvs) < len(pieces):
        last = project(after(pieces[len(kvs)], last), w_key, w_value)
        kvs.append(last)
    pieces = over_rep(jnp.stack(after(crossed[-1], kvs)))

    def mix(turns, q):
        outs = attend(slot, q, kvs, pieces, w_key, w_value, n_heads, n_rep, turns, fanout, spans)
        return [outs[0]] + [
            lax.ppermute(outs[s], "rep", shift_pairs(n_rep, s)) for s in range(1, n_rep)
        ]

    width = w_out.shape[1]
    tile = min(COL_TILE, width)
    cuts = [width // tile * part // 8 * tile for part in (0, 2, 4, 6, 7)] + [width]
    blocks = [(start, stop) for start, stop in zip(cuts, cuts[1:]) if stop > start]
    mixed = mix(list(range(1, n_heads)), queries)
    received, partials = [[] for _ in blocks], []
    for t in range(1, n_heads):
        for i, (start, stop) in enumerate(blocks):
            partial = out_project(mixed, w_outs, t - 1, start, stop, tile, 0.001)
            partial, mixed = lax.optimization_barrier((partial, mixed))
            partials.append(partial)
            received[i].append(lax.ppermute(partial, "heads", shift_pairs(n_heads, t)))
    mixed = mix([0], after(queries, partials))
    out = None
    for (start, stop), parts in zip(blocks, received):
        out = out_project(mixed, w_outs, 0, start, stop, tile, 0.2, parts, out, True)
    return out


def solution(mesh):
    return jax.shard_map(
        shards,
        mesh=mesh,
        in_specs=(
            P(("groups", "lanes"), ("heads", "rep")),
            P(("groups", "lanes"), None),
            P(("groups", "lanes"), ("heads", "rep"), None),
            P(("groups", "lanes"), None),
            P(("groups", "lanes"), None),
            P(None, ("heads", "rep")),
            P(None, ("heads", "rep")),
            P(("heads", "rep"), None),
        ),
        out_specs=P(("groups", "lanes", "heads", "rep"), None),
        check_vma=False,
    )
```

```python
import functools

import jax
import jax.numpy as jnp
from jax import lax
from jax.experimental import pallas as pl
from jax.experimental.pallas import tpu as pltpu
from jax.sharding import PartitionSpec as P

HD = 128
ENCODER_HEAD_DIM = 128
F32 = jnp.float32
BF16 = jnp.bfloat16
LATER_GROUPS = 2
COL_TILE = 512
ENCODE_COST = (None, 0.1, 10, 10)

VMEM = pl.BlockSpec(memory_space=pltpu.VMEM)
SMEM = pl.BlockSpec(memory_space=pltpu.SMEM)
ANY = pl.BlockSpec(memory_space=pl.ANY)


def params(mib):
    return pltpu.CompilerParams(vmem_limit_bytes=mib * 2**20)


def cost(gflops):
    return pl.CostEstimate(flops=int(gflops * 10**9), bytes_accessed=1024, transcendentals=0)


def apart(n, a, b):
    if n & (n - 1) == 0:
        return a ^ b
    return lax.rem(b - a + n, n)


def lane_pairs(n, d, reply):
    if n & (n - 1) == 0:
        return [(i, i ^ d) for i in range(n)]
    return [(i, (i - d if reply else i + d) % n) for i in range(n)]


def tables_of_lanes(own, n, meanwhile):
    if n & (n - 1):
        others = [lax.ppermute(own, "lanes", lane_pairs(n, d, False)) for d in range(1, n)]
        return jnp.concatenate([own] + others, axis=0)
    step, held = 1, own
    while step < n:
        other = lax.ppermute(held, "lanes", lane_pairs(n, step, False))
        held = jnp.concatenate(after([held, other], meanwhile if step == 1 else ()), axis=0)
        step *= 2
    return held


def shift_pairs(n, s):
    return [(i, (i + s) % n) for i in range(n)]


def dot_t(a, b):
    return lax.dot_general(a, b, (((1,), (1,)), ((), ())), preferred_element_type=F32)


def dot(a, b):
    return jnp.dot(a, b, preferred_element_type=F32)


def plan_kernel(order, cap, own_ref, req_ref, slot_ref, pick_ref, next_ref):
    n_lanes = len(order)
    lane = lax.axis_index("lanes")
    fanout, spans = own_ref.shape[0] // 2, own_ref.shape[1]
    for i, d in enumerate(order):
        next_ref[d] = i * cap
    for i in range(n_lanes * cap):
        pick_ref[i] = 0
        req_ref[i] = 0
    for j in range(fanout * spans):
        span, k = j // fanout, j % fanout
        d = apart(n_lanes, lane, own_ref[k, span])
        slot = next_ref[d]
        next_ref[d] = slot + 1
        pick_ref[slot] = own_ref[fanout + k, span]
        req_ref[slot] = j
        slot_ref[j] = slot


def plan(own, order, cap):
    table = jax.ShapeDtypeStruct((len(order) * cap,), jnp.int32)
    return pl.pallas_call(
        functools.partial(plan_kernel, order, cap),
        out_shape=(table, jax.ShapeDtypeStruct((own.size // 2,), jnp.int32), table),
        in_specs=[SMEM],
        out_specs=(SMEM, SMEM, SMEM),
        scratch_shapes=[pltpu.SMEM((len(order),), jnp.int32)],
        compiler_params=params(16),
        cost_estimate=cost(10),
        name="plan",
    )(own)


def fetch_kernel(items, cap, fanout, tables_ref, store_ref, *refs):
    blocks, pick_ref = refs[:-1], refs[-1]
    lane = lax.axis_index("lanes")
    spans = tables_ref.shape[1]
    others = tables_ref.shape[0] // (2 * fanout) - 1
    for i in range(others * cap):
        pick_ref[i] = 0
    for d in range(others):
        place, row = d * cap, (d + 1) * 2 * fanout
        for span in range(spans):
            for k in range(fanout):
                pick_ref[place] = tables_ref[row + fanout + k, span]
                place = place + (tables_ref[row + k, span] == lane).astype(jnp.int32)
    for block, (d, low, high) in zip(blocks, items):
        for s in range(low, high):
            block[s - low] = store_ref[pick_ref[(d - 1) * cap + s]]


def fetch(tables, store, items, cap, fanout):
    others = tables.shape[0] // (2 * fanout) - 1
    return pl.pallas_call(
        functools.partial(fetch_kernel, items, cap, fanout),
        out_shape=[
            jax.ShapeDtypeStruct((high - low,) + store.shape[1:], store.dtype) for _, low, high in items
        ],
        in_specs=[SMEM, VMEM],
        out_specs=[VMEM] * len(items),
        scratch_shapes=[pltpu.SMEM((others * cap + 1,), jnp.int32)],
        compiler_params=params(16),
        cost_estimate=cost(10),
        name="fetch",
    )(tables, store)


def encode_pairs(width):
    step = 2 * ENCODER_HEAD_DIM
    return [(start, min(start + step, width)) for start in range(0, width, step)]


def spread(states, start, stop):
    part = states[:, start:stop]
    heads = (stop - start) // ENCODER_HEAD_DIM
    if heads == 1:
        return part
    rows = jnp.concatenate([part] * heads, axis=0)
    return jnp.where(own_cells(rows.shape, part.shape[0]), rows, jnp.zeros_like(rows))


def own_cells(shape, keys):
    row = lax.broadcasted_iota(jnp.int32, shape, 0)
    col = lax.broadcasted_iota(jnp.int32, shape, 1)
    return (row >= keys) == (col >= ENCODER_HEAD_DIM)


def softmax_top(logits, keys):
    if logits.shape[1] == keys:
        return jnp.max(logits, axis=1, keepdims=True)
    first = lax.broadcasted_iota(jnp.int32, logits.shape, 1) < keys
    low = jnp.max(jnp.where(first, logits, -jnp.inf), axis=1, keepdims=True)
    high = jnp.max(jnp.where(first, -jnp.inf, logits), axis=1, keepdims=True)
    return jnp.where(first, low, high)


def encode_block(block, out_ref, first, req_ref, states_ref, fanout, span_len):
    scale = ENCODER_HEAD_DIM ** (-0.5)
    runs = encode_pairs(states_ref.shape[1])
    units = []
    for s in range(block.shape[0]):
        span = lax.div(req_ref[first + s], fanout)
        states = states_ref[pl.ds(pl.multiple_of(span * span_len, span_len), span_len), :]
        units += [(s, start, stop, spread(states, start, stop)) for start, stop in runs]
    logits = [dot_t(block[s, :, start:stop], keys) for s, start, stop, keys in units]
    tops = [softmax_top(part, span_len) for part in logits]
    weights = [jnp.exp((part - top) * scale).astype(BF16) for part, top in zip(logits, tops)]
    mixed = [dot(part, keys) for part, (_, _, _, keys) in zip(weights, units)]
    sums = []
    for part, (_, start, stop, keys) in zip(weights, units):
        ones = jnp.ones(keys.shape, BF16)
        if stop - start > ENCODER_HEAD_DIM:
            ones = jnp.where(own_cells(keys.shape, span_len), ones, jnp.zeros_like(ones))
        sums.append(dot(part, ones))
    for (s, start, stop, _), top, bottom in zip(units, mixed, sums):
        token = block[s, :, start:stop].astype(F32)
        out_ref[s, :, start:stop] = (token + top / bottom).astype(BF16)


def encode_kernel(first, fanout, span_len, req_ref, states_ref, *refs):
    blocks, out_ref = refs[:-1], refs[-1]
    at = 0
    for block in blocks:
        stop = at + block.shape[0]
        encode_block(block, out_ref.at[at:stop], first + at, req_ref, states_ref, fanout, span_len)
        at = stop


def encode(req, span_states, blocks, first, fanout, span_len, gflops):
    slots = sum(block.shape[0] for block in blocks)
    return pl.pallas_call(
        functools.partial(encode_kernel, first, fanout, span_len),
        out_shape=jax.ShapeDtypeStruct((slots,) + blocks[0].shape[1:], BF16),
        in_specs=[SMEM, VMEM] + [VMEM] * len(blocks),
        out_specs=VMEM,
        compiler_params=params(16),
        cost_estimate=cost(gflops),
        name="encode",
    )(req, span_states, *blocks)


def encode_local_kernel(fanout, span_len, req_ref, pick_ref, states_ref, store_ref, out_ref, tokens_ref):
    for s in range(out_ref.shape[0]):
        tokens_ref[s] = store_ref[pick_ref[s]]
    encode_block(tokens_ref, out_ref, 0, req_ref, states_ref, fanout, span_len)


def encode_local(req, pick, span_states, store, cap, fanout, span_len):
    block = (cap,) + store.shape[1:]
    return pl.pallas_call(
        functools.partial(encode_local_kernel, fanout, span_len),
        out_shape=jax.ShapeDtypeStruct(block, BF16),
        in_specs=[SMEM, SMEM, VMEM, VMEM],
        out_specs=VMEM,
        scratch_shapes=[pltpu.VMEM(block, BF16)],
        compiler_params=params(16),
        cost_estimate=cost(10),
        name="encode_local",
    )(req, pick, span_states, store)


def project_into(kv_ref, first, pieces, wk_ref, wv_ref):
    n, slots, tokens, width = pieces[0].shape
    rows = jnp.concatenate([piece[...].reshape(n * slots * tokens, width) for piece in pieces], axis=0)
    cols = wk_ref.shape[1]
    for side, weight in enumerate((wk_ref, wv_ref)):
        made = dot(rows, weight[...]).astype(BF16)
        for p in range(n * len(pieces)):
            part = made[p * slots * tokens : (p + 1) * slots * tokens]
            kv_ref[first : first + slots, p, :, side * cols : (side + 1) * cols] = part.reshape(
                slots, tokens, cols
            )


def project_kernel(n_pieces, *refs):
    pieces, (wk_ref, wv_ref, kv_ref) = refs[:n_pieces], refs[n_pieces:]
    project_into(kv_ref, 0, pieces, wk_ref, wv_ref)


def project(pieces, w_key, w_value):
    n, slots, tokens, _ = pieces[0].shape
    shape = (slots, n * len(pieces), tokens, 2 * w_key.shape[1])
    return pl.pallas_call(
        functools.partial(project_kernel, len(pieces)),
        out_shape=jax.ShapeDtypeStruct(shape, BF16),
        in_specs=[VMEM] * (len(pieces) + 2),
        out_specs=VMEM,
        compiler_params=params(32),
        cost_estimate=cost(10),
        name="project",
    )(*pieces, w_key, w_value)


def attend_kernel(firsts, n_heads, n_rep, targets, fanout, spans, n_rest, slot_ref, q_ref, *refs):
    ready, (own_ref, *refs) = refs[: len(firsts) - 1], refs[len(firsts) - 1 :]
    last = firsts[-1]
    if n_rest:
        pieces, (wk_ref, wv_ref, out_ref, rest_ref, kv_ref, sem) = refs[:n_rest], refs[n_rest:]
    else:
        rest_ref, out_ref, kv_ref, sem = refs
    heads_at, rep_at = lax.axis_index("heads"), lax.axis_index("rep")
    cols = q_ref.shape[1]
    span_len = q_ref.shape[0] // spans
    block = spans // (n_heads * n_rep)
    tokens = kv_ref.shape[1] * kv_ref.shape[2]
    mine = own_ref.shape[1]
    wanted = []
    for t, s in targets:
        owner = lax.rem(heads_at + t, n_heads) * n_rep + lax.rem(rep_at + s, n_rep)
        for i in range(block):
            wanted.append((owner * block + i, [slot_ref[(owner * block + i) * fanout + k] for k in range(fanout)]))
    held = [(at * fanout + k, slots[k]) for at, (_, slots) in enumerate(wanted) for k in range(fanout)]

    def whole(j, ref, index):
        return pltpu.make_async_copy(ref.at[index], kv_ref.at[j], sem.at[j])

    def part(j, index):
        return pltpu.make_async_copy(own_ref.at[index], kv_ref.at[j, :mine], sem.at[j])

    def other_part(j, index):
        return pltpu.make_async_copy(rest_ref.at[index], kv_ref.at[j, mine:], sem.at[len(held) + j])

    for j, slot in held:
        for ref, low, high in zip(ready, firsts, firsts[1:]):

            @pl.when(jnp.logical_and(slot >= low, slot < high))
            def _(j=j, slot=slot, ref=ref, low=low):
                whole(j, ref, slot - low).start()

        @pl.when(slot >= last)
        def _(j=j, slot=slot):
            part(j, slot - last).start()
            if not n_rest:
                other_part(j, slot - last).start()

    if n_rest:
        project_into(rest_ref, 0, pieces, wk_ref, wv_ref)
    for j, slot in held:

        @pl.when(slot >= last)
        def _(j=j, slot=slot):
            if n_rest:
                other_part(j, slot - last).start()
            part(j, slot - last).wait()
            other_part(j, slot - last).wait()

        @pl.when(slot < last)
        def _(j=j):
            whole(j, ready[0], 0).wait()

    heads = [slice(h * HD, (h + 1) * HD) for h in range(cols // HD)]
    for at, (span, _) in enumerate(wanted):
        rows = pl.ds(pl.multiple_of(span * span_len, span_len), span_len)

        def side(lanes):
            return kv_ref[at * fanout : (at + 1) * fanout, :, :, lanes].reshape(fanout * tokens, HD)

        logits = [dot_t(q_ref[rows, lanes], side(lanes)) for lanes in heads]
        tops = [jnp.max(part, axis=1, keepdims=True) for part in logits]
        weights = [jnp.exp((part - top) * HD ** (-0.5)) for part, top in zip(logits, tops)]
        scales = [1.0 / jnp.sum(part, axis=1, keepdims=True) for part in weights]
        mixed = [
            dot(part.astype(BF16), side(slice(cols + lanes.start, cols + lanes.stop)))
            for part, lanes in zip(weights, heads)
        ]
        into = slice(at % block * span_len, (at % block + 1) * span_len)
        for part, scale, lanes in zip(mixed, scales, heads):
            out_ref[at // block, into, lanes] = (part * scale).astype(BF16)


def attend(slot, queries, ready, own, rest, weights, n_heads, n_rep, targets, fanout, spans):
    firsts = [0]
    for kv in ready:
        firsts.append(firsts[-1] + kv.shape[0])
    cols = queries.shape[1]
    rows = queries.shape[0] // (n_heads * n_rep)
    todo = isinstance(rest, list)
    slots, mine, tokens, width = own.shape
    others = sum(piece.shape[0] for piece in rest) if todo else rest.shape[1]
    held = len(targets) * (spans // (n_heads * n_rep)) * fanout
    out_shape = [jax.ShapeDtypeStruct((len(targets), rows, cols), BF16)]
    if todo:
        out_shape.append(jax.ShapeDtypeStruct((slots, others, tokens, width), BF16))
    operands = [*rest, *weights] if todo else [rest]
    return pl.pallas_call(
        functools.partial(
            attend_kernel, firsts, n_heads, n_rep, targets, fanout, spans, len(rest) if todo else 0
        ),
        out_shape=out_shape,
        in_specs=[SMEM, VMEM] + [ANY] * (len(ready) + 1) + [VMEM if todo else ANY] * len(operands),
        out_specs=[VMEM] * len(out_shape),
        scratch_shapes=[
            pltpu.VMEM((held, mine + others, tokens, width), BF16),
            pltpu.SemaphoreType.DMA((2 * held,)),
        ],
        compiler_params=params(32),
        cost_estimate=cost(0.001),
        name="attend",
    )(slot, queries, *ready, own, *operands)


def out_kernel(n_rep, n_received, *refs):
    mixed, weights, received = refs[:n_rep], refs[n_rep : 2 * n_rep], refs[2 * n_rep : 2 * n_rep + n_received]
    total = sum(dot(a[0], w[...]) for a, w in zip(mixed, weights))
    for part in received:
        total = total + part[...].astype(F32)
    refs[-1][...] = total.astype(BF16)


def out_project(mixed, weights, t, start, stop, tile, gflops, received=(), out=None, final=False):
    _, rows, depth = mixed[0].shape
    width = weights[0].shape[1]
    base = start // tile
    n = len(mixed)
    operands = [*mixed, *weights, *received] + ([] if out is None else [out])
    return pl.pallas_call(
        functools.partial(out_kernel, n, len(received)),
        grid=((stop - start) // tile,),
        out_shape=jax.ShapeDtypeStruct((rows, width if final else stop - start), BF16),
        in_specs=[pl.BlockSpec((1, rows, depth), lambda j: (t, 0, 0))] * n
        + [pl.BlockSpec((depth, tile), lambda j: (0, base + j))] * n
        + [pl.BlockSpec((rows, tile), lambda j: (0, j))] * len(received)
        + [ANY] * (out is not None),
        out_specs=pl.BlockSpec((rows, tile), lambda j: (0, (base if final else 0) + j)),
        input_output_aliases={} if out is None else {len(operands) - 1: 0},
        compiler_params=params(16),
        cost_estimate=cost(gflops),
        name="out_final" if final else "out_project",
    )(*operands)


def after(values, *earlier):
    return lax.optimization_barrier((values, earlier))[0]


def shards(queries, span_states, store, entry_ids, owners, w_key, w_value, w_out):
    n_lanes, n_heads, n_rep = (lax.axis_size(name) for name in ("lanes", "heads", "rep"))
    spans, fanout = entry_ids.shape
    requests = spans * fanout
    cap = max(2, (requests + n_lanes - 1) // n_lanes)
    span_len = queries.shape[0] // spans

    def over_heads(array):
        return [array] + [lax.ppermute(array, "heads", shift_pairs(n_heads, s)) for s in range(1, n_heads)]

    def over_rep(array):
        return [array] + [lax.ppermute(array, "rep", shift_pairs(n_rep, s)) for s in range(1, n_rep)]

    order = list(range(n_lanes))
    items = []
    for d in order[1:]:
        cuts = (0, cap // 2, cap) if d == 1 else (0, cap)
        items += [(d, low, high) for low, high in zip(cuts, cuts[1:])]
    size = max(1, -(-(len(items) - 2) // LATER_GROUPS))
    cuts = [0] + list(range(2, len(items), size)) + [len(items)]
    parts = [range(low, high) for low, high in zip(cuts, cuts[1:])]

    own = jnp.concatenate([owners.T, entry_ids.T], axis=0)
    req, slot, pick = plan(own, order, cap)
    tables = tables_of_lanes(own, n_lanes, req)
    encoded = encode_local(req, pick, span_states, store, cap, fanout, span_len)
    blocks = fetch(after(tables, encoded), store, items, cap, fanout)

    def send(part, *earlier):
        ready = after([blocks[i] for i in part], *earlier)
        return [
            lax.ppermute(block, "lanes", lane_pairs(n_lanes, items[i][0], True))
            for block, i in zip(ready, part)
        ]

    crossed, pieces = [over_heads(encoded)], []
    arrived = [None] + [send(part) for part in parts[:2]]
    last = blocks
    for i, part in enumerate(parts, 1):
        if i + 2 <= len(parts):
            arrived.append(send(parts[i + 1], arrived[i], last))
        first = items[part[0]][0] * cap + items[part[0]][1]
        encoded = encode(
            req, span_states, after(arrived[i], last), first, fanout, span_len, ENCODE_COST[i]
        )
        crossed.append(over_heads(encoded))
        last = encoded
        while i > 1 and len(pieces) < i:
            last = jnp.stack(after(crossed[len(pieces)], last))
            pieces.append(over_rep(last))
    w_outs = over_rep(w_out)
    kvs, last = [], after(last, w_outs)
    while len(kvs) < len(pieces):
        last = project(after(pieces[len(kvs)], last), w_key, w_value)
        kvs.append(last)
    pieces = over_rep(jnp.stack(after(crossed[-1], kvs)))
    own_kv, rest = project(pieces[:1], w_key, w_value), pieces[1:]

    def mix(turns, q, rest):
        mixed = []
        for s in range(1, n_rep):
            given, *made = attend(
                slot, q, kvs, own_kv, rest, (w_key, w_value), n_heads, n_rep, [(t, s) for t in turns], fanout, spans
            )
            rest = made[0] if made else rest
            mixed.append(lax.ppermute(given, "rep", shift_pairs(n_rep, s)))
        kept = attend(
            slot, q, kvs, own_kv, rest, (w_key, w_value), n_heads, n_rep, [(t, 0) for t in turns], fanout, spans
        )
        return [kept[0]] + mixed, rest

    width = w_out.shape[1]
    tile = min(COL_TILE, width)
    cuts = [width // tile * part // 8 * tile for part in (0, 2, 4, 6, 7)] + [width]
    blocks = [(start, stop) for start, stop in zip(cuts, cuts[1:]) if stop > start]
    mixed, rest = mix(list(range(1, n_heads)), queries, rest)
    received, partials = [[] for _ in blocks], []
    for t in range(1, n_heads):
        for i, (start, stop) in enumerate(blocks):
            partial = out_project(mixed, w_outs, t - 1, start, stop, tile, 0.001)
            partial, mixed = lax.optimization_barrier((partial, mixed))
            partials.append(partial)
            received[i].append(lax.ppermute(partial, "heads", shift_pairs(n_heads, t)))
    mixed, rest = mix([0], after(queries, partials), rest)
    out = None
    for (start, stop), parts in zip(blocks, received):
        out = out_project(mixed, w_outs, 0, start, stop, tile, 0.2, parts, out, True)
    return out


def solution(mesh):
    return jax.shard_map(
        shards,
        mesh=mesh,
        in_specs=(
            P(("groups", "lanes"), ("heads", "rep")),
            P(("groups", "lanes"), None),
            P(("groups", "lanes"), ("heads", "rep"), None),
            P(("groups", "lanes"), None),
            P(("groups", "lanes"), None),
            P(None, ("heads", "rep")),
            P(None, ("heads", "rep")),
            P(("heads", "rep"), None),
        ),
        out_specs=P(("groups", "lanes", "heads", "rep"), None),
        check_vma=False,
    )
```

```python
import functools

import jax
import jax.numpy as jnp
from jax import lax
from jax.experimental import pallas as pl
from jax.experimental.pallas import tpu as pltpu
from jax.sharding import PartitionSpec as P

HD = 128
ENCODER_HEAD_DIM = 128
F32 = jnp.float32
BF16 = jnp.bfloat16
LATER_GROUPS = 2
COL_TILE = 512
ENCODE_COST = (None, 0.1, 10, 10)

VMEM = pl.BlockSpec(memory_space=pltpu.VMEM)
SMEM = pl.BlockSpec(memory_space=pltpu.SMEM)
ANY = pl.BlockSpec(memory_space=pl.ANY)


def params(mib):
    return pltpu.CompilerParams(vmem_limit_bytes=mib * 2**20)


def cost(gflops):
    return pl.CostEstimate(flops=int(gflops * 10**9), bytes_accessed=1024, transcendentals=0)


def apart(n, a, b):
    if n & (n - 1) == 0:
        return a ^ b
    return lax.rem(b - a + n, n)


def lane_pairs(n, d, reply):
    if n & (n - 1) == 0:
        return [(i, i ^ d) for i in range(n)]
    return [(i, (i - d if reply else i + d) % n) for i in range(n)]


def shift_pairs(n, s):
    return [(i, (i + s) % n) for i in range(n)]


def dot_t(a, b):
    return lax.dot_general(a, b, (((1,), (1,)), ((), ())), preferred_element_type=F32)


def dot(a, b):
    return jnp.dot(a, b, preferred_element_type=F32)


def plan_kernel(order, cap, own_ref, req_ref, slot_ref, pick_ref, next_ref):
    n_lanes = len(order)
    lane = lax.axis_index("lanes")
    fanout, spans = own_ref.shape[0] // 2, own_ref.shape[1]
    for i, d in enumerate(order):
        next_ref[d] = i * cap
    for i in range(n_lanes * cap):
        pick_ref[i] = 0
        req_ref[i] = 0
    for j in range(fanout * spans):
        span, k = j // fanout, j % fanout
        d = apart(n_lanes, lane, own_ref[k, span])
        slot = next_ref[d]
        next_ref[d] = slot + 1
        pick_ref[slot] = own_ref[fanout + k, span]
        req_ref[slot] = j
        slot_ref[j] = slot


def plan(own, order, cap):
    table = jax.ShapeDtypeStruct((len(order) * cap,), jnp.int32)
    return pl.pallas_call(
        functools.partial(plan_kernel, order, cap),
        out_shape=(table, jax.ShapeDtypeStruct((own.size // 2,), jnp.int32), table),
        in_specs=[SMEM],
        out_specs=(SMEM, SMEM, SMEM),
        scratch_shapes=[pltpu.SMEM((len(order),), jnp.int32)],
        compiler_params=params(16),
        cost_estimate=cost(10),
        name="plan",
    )(own)


def fetch_kernel(items, cap, *refs):
    others = max(d for d, _, _ in items)
    asked, store_ref, refs = refs[:others], refs[others], refs[others + 1 :]
    blocks, pick_ref = refs[:-1], refs[-1]
    lane = lax.axis_index("lanes")
    fanout, spans = asked[0].shape[0] // 2, asked[0].shape[1]
    for i in range(others * cap):
        pick_ref[i] = 0
    for d in range(others):
        place = d * cap
        for span in range(spans):
            for k in range(fanout):
                pick_ref[place] = asked[d][fanout + k, span]
                place = place + (asked[d][k, span] == lane).astype(jnp.int32)
    for block, (d, low, high) in zip(blocks, items):
        for s in range(low, high):
            block[s - low] = store_ref[pick_ref[(d - 1) * cap + s]]


def fetch(asked, store, items, cap):
    others = len(asked)
    return pl.pallas_call(
        functools.partial(fetch_kernel, items, cap),
        out_shape=[
            jax.ShapeDtypeStruct((high - low,) + store.shape[1:], store.dtype) for _, low, high in items
        ],
        in_specs=[SMEM] * others + [VMEM],
        out_specs=[VMEM] * len(items),
        scratch_shapes=[pltpu.SMEM((others * cap + 1,), jnp.int32)],
        compiler_params=params(16),
        cost_estimate=cost(10),
        name="fetch",
    )(*asked, store)


def encode_pairs(width):
    step = 2 * ENCODER_HEAD_DIM
    return [(start, min(start + step, width)) for start in range(0, width, step)]


def spread(states, start, stop):
    part = states[:, start:stop]
    heads = (stop - start) // ENCODER_HEAD_DIM
    if heads == 1:
        return part
    rows = jnp.concatenate([part] * heads, axis=0)
    return jnp.where(own_cells(rows.shape, part.shape[0]), rows, jnp.zeros_like(rows))


def own_cells(shape, keys):
    row = lax.broadcasted_iota(jnp.int32, shape, 0)
    col = lax.broadcasted_iota(jnp.int32, shape, 1)
    return (row >= keys) == (col >= ENCODER_HEAD_DIM)


def softmax_top(logits, keys):
    if logits.shape[1] == keys:
        return jnp.max(logits, axis=1, keepdims=True)
    first = lax.broadcasted_iota(jnp.int32, logits.shape, 1) < keys
    low = jnp.max(jnp.where(first, logits, -jnp.inf), axis=1, keepdims=True)
    high = jnp.max(jnp.where(first, -jnp.inf, logits), axis=1, keepdims=True)
    return jnp.where(first, low, high)


def encode_block(block, out_ref, first, req_ref, states_ref, fanout, span_len):
    scale = ENCODER_HEAD_DIM ** (-0.5)
    runs = encode_pairs(states_ref.shape[1])
    units = []
    for s in range(block.shape[0]):
        span = lax.div(req_ref[first + s], fanout)
        states = states_ref[pl.ds(pl.multiple_of(span * span_len, span_len), span_len), :]
        units += [(s, start, stop, spread(states, start, stop)) for start, stop in runs]
    logits = [dot_t(block[s, :, start:stop], keys) for s, start, stop, keys in units]
    tops = [softmax_top(part, span_len) for part in logits]
    weights = [jnp.exp((part - top) * scale).astype(BF16) for part, top in zip(logits, tops)]
    mixed = [dot(part, keys) for part, (_, _, _, keys) in zip(weights, units)]
    sums = []
    for part, (_, start, stop, keys) in zip(weights, units):
        ones = jnp.ones(keys.shape, BF16)
        if stop - start > ENCODER_HEAD_DIM:
            ones = jnp.where(own_cells(keys.shape, span_len), ones, jnp.zeros_like(ones))
        sums.append(dot(part, ones))
    for (s, start, stop, _), top, bottom in zip(units, mixed, sums):
        token = block[s, :, start:stop].astype(F32)
        out_ref[s, :, start:stop] = (token + top / bottom).astype(BF16)


def encode_kernel(first, fanout, span_len, req_ref, states_ref, *refs):
    blocks, out_ref = refs[:-1], refs[-1]
    at = 0
    for block in blocks:
        stop = at + block.shape[0]
        encode_block(block, out_ref.at[at:stop], first + at, req_ref, states_ref, fanout, span_len)
        at = stop


def encode(req, span_states, blocks, first, fanout, span_len, gflops):
    slots = sum(block.shape[0] for block in blocks)
    return pl.pallas_call(
        functools.partial(encode_kernel, first, fanout, span_len),
        out_shape=jax.ShapeDtypeStruct((slots,) + blocks[0].shape[1:], BF16),
        in_specs=[SMEM, VMEM] + [VMEM] * len(blocks),
        out_specs=VMEM,
        compiler_params=params(16),
        cost_estimate=cost(gflops),
        name="encode",
    )(req, span_states, *blocks)


def encode_local_kernel(fanout, span_len, req_ref, pick_ref, states_ref, store_ref, out_ref, tokens_ref):
    for s in range(out_ref.shape[0]):
        tokens_ref[s] = store_ref[pick_ref[s]]
    encode_block(tokens_ref, out_ref, 0, req_ref, states_ref, fanout, span_len)


def encode_local(req, pick, span_states, store, cap, fanout, span_len):
    block = (cap,) + store.shape[1:]
    return pl.pallas_call(
        functools.partial(encode_local_kernel, fanout, span_len),
        out_shape=jax.ShapeDtypeStruct(block, BF16),
        in_specs=[SMEM, SMEM, VMEM, VMEM],
        out_specs=VMEM,
        scratch_shapes=[pltpu.VMEM(block, BF16)],
        compiler_params=params(16),
        cost_estimate=cost(10),
        name="encode_local",
    )(req, pick, span_states, store)


def project_into(kv_ref, first, pieces, wk_ref, wv_ref):
    n, slots, tokens, width = pieces[0].shape
    rows = jnp.concatenate([piece[...].reshape(n * slots * tokens, width) for piece in pieces], axis=0)
    cols = wk_ref.shape[1]
    for side, weight in enumerate((wk_ref, wv_ref)):
        made = dot(rows, weight[...]).astype(BF16)
        for p in range(n * len(pieces)):
            part = made[p * slots * tokens : (p + 1) * slots * tokens]
            kv_ref[first : first + slots, p, :, side * cols : (side + 1) * cols] = part.reshape(
                slots, tokens, cols
            )


def project_kernel(n_pieces, *refs):
    pieces, (wk_ref, wv_ref, kv_ref) = refs[:n_pieces], refs[n_pieces:]
    project_into(kv_ref, 0, pieces, wk_ref, wv_ref)


def project(pieces, w_key, w_value):
    n, slots, tokens, _ = pieces[0].shape
    shape = (slots, n * len(pieces), tokens, 2 * w_key.shape[1])
    return pl.pallas_call(
        functools.partial(project_kernel, len(pieces)),
        out_shape=jax.ShapeDtypeStruct(shape, BF16),
        in_specs=[VMEM] * (len(pieces) + 2),
        out_specs=VMEM,
        compiler_params=params(32),
        cost_estimate=cost(10),
        name="project",
    )(*pieces, w_key, w_value)


def attend_kernel(firsts, n_heads, n_rep, targets, fanout, spans, n_rest, slot_ref, q_ref, *refs):
    ready, (own_ref, *refs) = refs[: len(firsts) - 1], refs[len(firsts) - 1 :]
    if n_rest:
        pieces, (wk_ref, wv_ref, out_ref, rest_ref) = refs[:n_rest], refs[n_rest:]
        project_into(rest_ref, 0, pieces, wk_ref, wv_ref)
    else:
        rest_ref, out_ref = refs
    heads_at, rep_at = lax.axis_index("heads"), lax.axis_index("rep")
    cols = q_ref.shape[1]
    span_len = q_ref.shape[0] // spans
    block = spans // (n_heads * n_rep)

    def place(slot, first, count):
        return jnp.clip(slot - first, 0, count - 1)

    def held(slot, lanes):
        at = place(slot, firsts[-1], own_ref.shape[0])
        value = jnp.concatenate([own_ref[at, :, :, lanes], rest_ref[at, :, :, lanes]], axis=0)
        for ref, first in reversed(list(zip(ready, firsts))):
            there = slot < first + ref.shape[0]
            value = jnp.where(there, ref[place(slot, first, ref.shape[0]), :, :, lanes], value)
        return value.reshape(-1, HD)

    heads = [slice(h * HD, (h + 1) * HD) for h in range(cols // HD)]
    for at, (t, s) in enumerate(targets):
        owner = lax.rem(heads_at + t, n_heads) * n_rep + lax.rem(rep_at + s, n_rep)
        for i in range(block):
            span = owner * block + i
            slots = [slot_ref[span * fanout + k] for k in range(fanout)]
            rows = pl.ds(pl.multiple_of(span * span_len, span_len), span_len)

            def side(lanes):
                return jnp.concatenate([held(slot, lanes) for slot in slots], axis=0)

            logits = [dot_t(q_ref[rows, lanes], side(lanes)) for lanes in heads]
            tops = [jnp.max(part, axis=1, keepdims=True) for part in logits]
            weights = [jnp.exp((part - top) * HD ** (-0.5)) for part, top in zip(logits, tops)]
            scales = [1.0 / jnp.sum(part, axis=1, keepdims=True) for part in weights]
            mixed = [
                dot(part.astype(BF16), side(slice(cols + lanes.start, cols + lanes.stop)))
                for part, lanes in zip(weights, heads)
            ]
            for part, scale, lanes in zip(mixed, scales, heads):
                out_ref[at, i * span_len : (i + 1) * span_len, lanes] = (part * scale).astype(BF16)


def attend(slot, queries, ready, own, rest, weights, n_heads, n_rep, targets, fanout, spans):
    firsts = [0]
    for kv in ready:
        firsts.append(firsts[-1] + kv.shape[0])
    cols = queries.shape[1]
    rows = queries.shape[0] // (n_heads * n_rep)
    todo = isinstance(rest, list)
    slots, _, tokens, width = own.shape
    out_shape = [jax.ShapeDtypeStruct((len(targets), rows, cols), BF16)]
    if todo:
        others = sum(piece.shape[0] for piece in rest)
        out_shape.append(jax.ShapeDtypeStruct((slots, others, tokens, width), BF16))
    operands = [*rest, *weights] if todo else [rest]
    return pl.pallas_call(
        functools.partial(
            attend_kernel, firsts, n_heads, n_rep, targets, fanout, spans, len(rest) if todo else 0
        ),
        out_shape=out_shape,
        in_specs=[SMEM] + [VMEM] * (len(ready) + 2 + len(operands)),
        out_specs=[VMEM] * len(out_shape),
        compiler_params=params(32),
        cost_estimate=cost(0.001),
        name="attend",
    )(slot, queries, *ready, own, *operands)


def out_kernel(n_rep, n_received, *refs):
    mixed, weights, received = refs[:n_rep], refs[n_rep : 2 * n_rep], refs[2 * n_rep : 2 * n_rep + n_received]
    total = sum(dot(a[0], w[...]) for a, w in zip(mixed, weights))
    for part in received:
        total = total + part[...].astype(F32)
    refs[-1][...] = total.astype(BF16)


def out_project(mixed, weights, t, start, stop, tile, gflops, received=(), out=None, final=False):
    _, rows, depth = mixed[0].shape
    width = weights[0].shape[1]
    base = start // tile
    n = len(mixed)
    operands = [*mixed, *weights, *received] + ([] if out is None else [out])
    return pl.pallas_call(
        functools.partial(out_kernel, n, len(received)),
        grid=((stop - start) // tile,),
        out_shape=jax.ShapeDtypeStruct((rows, width if final else stop - start), BF16),
        in_specs=[pl.BlockSpec((1, rows, depth), lambda j: (t, 0, 0))] * n
        + [pl.BlockSpec((depth, tile), lambda j: (0, base + j))] * n
        + [pl.BlockSpec((rows, tile), lambda j: (0, j))] * len(received)
        + [ANY] * (out is not None),
        out_specs=pl.BlockSpec((rows, tile), lambda j: (0, (base if final else 0) + j)),
        input_output_aliases={} if out is None else {len(operands) - 1: 0},
        compiler_params=params(16),
        cost_estimate=cost(gflops),
        name="out_final" if final else "out_project",
    )(*operands)


def after(values, *earlier):
    return lax.optimization_barrier((values, earlier))[0]


def shards(queries, span_states, store, entry_ids, owners, w_key, w_value, w_out):
    n_lanes, n_heads, n_rep = (lax.axis_size(name) for name in ("lanes", "heads", "rep"))
    spans, fanout = entry_ids.shape
    requests = spans * fanout
    cap = max(2, (requests + n_lanes - 1) // n_lanes)
    span_len = queries.shape[0] // spans

    def over_heads(array):
        return [array] + [lax.ppermute(array, "heads", shift_pairs(n_heads, s)) for s in range(1, n_heads)]

    def over_rep(array):
        return [array] + [lax.ppermute(array, "rep", shift_pairs(n_rep, s)) for s in range(1, n_rep)]

    order = list(range(n_lanes))
    items = []
    for d in order[1:]:
        cuts = (0, cap // 2, cap) if d == 1 else (0, cap)
        items += [(d, low, high) for low, high in zip(cuts, cuts[1:])]
    size = max(1, -(-(len(items) - 2) // LATER_GROUPS))
    cuts = [0] + list(range(2, len(items), size)) + [len(items)]
    parts = [range(low, high) for low, high in zip(cuts, cuts[1:])]

    own = jnp.concatenate([owners.T, entry_ids.T], axis=0)
    asked = [lax.ppermute(own, "lanes", lane_pairs(n_lanes, d, False)) for d in range(1, n_lanes)]
    req, slot, pick = plan(own, order, cap)
    encoded = encode_local(req, pick, span_states, store, cap, fanout, span_len)
    blocks = fetch(after(asked, encoded), store, items, cap)

    def send(part, *earlier):
        ready = after([blocks[i] for i in part], *earlier)
        return [
            lax.ppermute(block, "lanes", lane_pairs(n_lanes, items[i][0], True))
            for block, i in zip(ready, part)
        ]

    crossed, pieces = [over_heads(encoded)], []
    arrived = [None] + [send(part) for part in parts[:2]]
    last = blocks
    for i, part in enumerate(parts, 1):
        if i + 2 <= len(parts):
            arrived.append(send(parts[i + 1], arrived[i], last))
        first = items[part[0]][0] * cap + items[part[0]][1]
        encoded = encode(
            req, span_states, after(arrived[i], last), first, fanout, span_len, ENCODE_COST[i]
        )
        crossed.append(over_heads(encoded))
        last = encoded
        while i > 1 and len(pieces) < i:
            last = jnp.stack(after(crossed[len(pieces)], last))
            pieces.append(over_rep(last))
    w_outs = over_rep(w_out)
    kvs, last = [], after(last, w_outs)
    while len(kvs) < len(pieces):
        last = project(after(pieces[len(kvs)], last), w_key, w_value)
        kvs.append(last)
    pieces = over_rep(jnp.stack(after(crossed[-1], kvs)))
    own_kv, rest = project(pieces[:1], w_key, w_value), pieces[1:]

    def mix(turns, q, rest):
        mixed = []
        for s in range(1, n_rep):
            given, *made = attend(
                slot, q, kvs, own_kv, rest, (w_key, w_value), n_heads, n_rep, [(t, s) for t in turns], fanout, spans
            )
            rest = made[0] if made else rest
            mixed.append(lax.ppermute(given, "rep", shift_pairs(n_rep, s)))
        kept = attend(
            slot, q, kvs, own_kv, rest, (w_key, w_value), n_heads, n_rep, [(t, 0) for t in turns], fanout, spans
        )
        return [kept[0]] + mixed, rest

    width = w_out.shape[1]
    tile = min(COL_TILE, width)
    cuts = [width // tile * part // 8 * tile for part in (0, 2, 4, 6, 7)] + [width]
    blocks = [(start, stop) for start, stop in zip(cuts, cuts[1:]) if stop > start]
    mixed, rest = mix(list(range(1, n_heads)), queries, rest)
    received, partials = [[] for _ in blocks], []
    for t in range(1, n_heads):
        for i, (start, stop) in enumerate(blocks):
            partial = out_project(mixed, w_outs, t - 1, start, stop, tile, 0.001)
            partial, mixed = lax.optimization_barrier((partial, mixed))
            partials.append(partial)
            received[i].append(lax.ppermute(partial, "heads", shift_pairs(n_heads, t)))
    mixed, rest = mix([0], after(queries, partials), rest)
    out = None
    for (start, stop), parts in zip(blocks, received):
        out = out_project(mixed, w_outs, 0, start, stop, tile, 0.2, parts, out, True)
    return out


def solution(mesh):
    return jax.shard_map(
        shards,
        mesh=mesh,
        in_specs=(
            P(("groups", "lanes"), ("heads", "rep")),
            P(("groups", "lanes"), None),
            P(("groups", "lanes"), ("heads", "rep"), None),
            P(("groups", "lanes"), None),
            P(("groups", "lanes"), None),
            P(None, ("heads", "rep")),
            P(None, ("heads", "rep")),
            P(("heads", "rep"), None),
        ),
        out_specs=P(("groups", "lanes", "heads", "rep"), None),
        check_vma=False,
    )
```

```python
import functools

import jax
import jax.numpy as jnp
from jax import lax
from jax.experimental import pallas as pl
from jax.experimental.pallas import tpu as pltpu
from jax.sharding import PartitionSpec as P

HD = 128
ENCODER_HEAD_DIM = 128
F32 = jnp.float32
BF16 = jnp.bfloat16
COL_TILE = 512
ENCODE_COST = (None, 0.1, 0.1, 10, 10, 10)
SEND_AFTER = (None, 1, 3)
STACK_AFTER = {3: ((0,), (1, 2)), 4: ((3,),)}

VMEM = pl.BlockSpec(memory_space=pltpu.VMEM)
SMEM = pl.BlockSpec(memory_space=pltpu.SMEM)
ANY = pl.BlockSpec(memory_space=pl.ANY)


def params(mib):
    return pltpu.CompilerParams(vmem_limit_bytes=mib * 2**20)


def cost(gflops):
    return pl.CostEstimate(flops=int(gflops * 10**9), bytes_accessed=1024, transcendentals=0)


def apart(n, a, b):
    if n & (n - 1) == 0:
        return a ^ b
    return lax.rem(b - a + n, n)


def lane_pairs(n, d, reply):
    if n & (n - 1) == 0:
        return [(i, i ^ d) for i in range(n)]
    return [(i, (i - d if reply else i + d) % n) for i in range(n)]


def shift_pairs(n, s):
    return [(i, (i + s) % n) for i in range(n)]


def dot_t(a, b):
    return lax.dot_general(a, b, (((1,), (1,)), ((), ())), preferred_element_type=F32)


def dot(a, b):
    return jnp.dot(a, b, preferred_element_type=F32)


def plan_kernel(order, cap, own_ref, req_ref, slot_ref, pick_ref, next_ref):
    n_lanes = len(order)
    lane = lax.axis_index("lanes")
    fanout, spans = own_ref.shape[0] // 2, own_ref.shape[1]
    for i, d in enumerate(order):
        next_ref[d] = i * cap
    for i in range(n_lanes * cap):
        pick_ref[i] = 0
        req_ref[i] = 0
    for j in range(fanout * spans):
        span, k = j // fanout, j % fanout
        d = apart(n_lanes, lane, own_ref[k, span])
        slot = next_ref[d]
        next_ref[d] = slot + 1
        pick_ref[slot] = own_ref[fanout + k, span]
        req_ref[slot] = j
        slot_ref[j] = slot


def plan(own, order, cap):
    table = jax.ShapeDtypeStruct((len(order) * cap,), jnp.int32)
    return pl.pallas_call(
        functools.partial(plan_kernel, order, cap),
        out_shape=(table, jax.ShapeDtypeStruct((own.size // 2,), jnp.int32), table),
        in_specs=[SMEM],
        out_specs=(SMEM, SMEM, SMEM),
        scratch_shapes=[pltpu.SMEM((len(order),), jnp.int32)],
        compiler_params=params(16),
        cost_estimate=cost(10),
        name="plan",
    )(own)


def fetch_kernel(items, cap, *refs):
    others = max(d for d, _, _ in items)
    asked, store_ref, refs = refs[:others], refs[others], refs[others + 1 :]
    blocks, pick_ref = refs[:-1], refs[-1]
    lane = lax.axis_index("lanes")
    fanout, spans = asked[0].shape[0] // 2, asked[0].shape[1]
    for i in range(others * cap):
        pick_ref[i] = 0
    for d in range(others):
        place = d * cap
        for span in range(spans):
            for k in range(fanout):
                pick_ref[place] = asked[d][fanout + k, span]
                place = place + (asked[d][k, span] == lane).astype(jnp.int32)
    for block, (d, low, high) in zip(blocks, items):
        for s in range(low, high):
            block[s - low] = store_ref[pick_ref[(d - 1) * cap + s]]


def fetch(asked, store, items, cap):
    others = len(asked)
    return pl.pallas_call(
        functools.partial(fetch_kernel, items, cap),
        out_shape=[
            jax.ShapeDtypeStruct((high - low,) + store.shape[1:], store.dtype) for _, low, high in items
        ],
        in_specs=[SMEM] * others + [VMEM],
        out_specs=[VMEM] * len(items),
        scratch_shapes=[pltpu.SMEM((others * cap + 1,), jnp.int32)],
        compiler_params=params(16),
        cost_estimate=cost(10),
        name="fetch",
    )(*asked, store)


def encode_pairs(width):
    step = 2 * ENCODER_HEAD_DIM
    return [(start, min(start + step, width)) for start in range(0, width, step)]


def spread(states, start, stop):
    part = states[:, start:stop]
    heads = (stop - start) // ENCODER_HEAD_DIM
    if heads == 1:
        return part
    rows = jnp.concatenate([part] * heads, axis=0)
    return jnp.where(own_cells(rows.shape, part.shape[0]), rows, jnp.zeros_like(rows))


def own_cells(shape, keys):
    row = lax.broadcasted_iota(jnp.int32, shape, 0)
    col = lax.broadcasted_iota(jnp.int32, shape, 1)
    return (row >= keys) == (col >= ENCODER_HEAD_DIM)


def softmax_top(logits, keys):
    if logits.shape[1] == keys:
        return jnp.max(logits, axis=1, keepdims=True)
    first = lax.broadcasted_iota(jnp.int32, logits.shape, 1) < keys
    low = jnp.max(jnp.where(first, logits, -jnp.inf), axis=1, keepdims=True)
    high = jnp.max(jnp.where(first, -jnp.inf, logits), axis=1, keepdims=True)
    return jnp.where(first, low, high)


def encode_block(block, out_ref, first, req_ref, states_ref, fanout, span_len):
    scale = ENCODER_HEAD_DIM ** (-0.5)
    runs = encode_pairs(states_ref.shape[1])
    units = []
    for s in range(block.shape[0]):
        span = lax.div(req_ref[first + s], fanout)
        states = states_ref[pl.ds(pl.multiple_of(span * span_len, span_len), span_len), :]
        units += [(s, start, stop, spread(states, start, stop)) for start, stop in runs]
    logits = [dot_t(block[s, :, start:stop], keys) for s, start, stop, keys in units]
    tops = [softmax_top(part, span_len) for part in logits]
    weights = [jnp.exp((part - top) * scale).astype(BF16) for part, top in zip(logits, tops)]
    mixed = [dot(part, keys) for part, (_, _, _, keys) in zip(weights, units)]
    sums = []
    for part, (_, start, stop, keys) in zip(weights, units):
        ones = jnp.ones(keys.shape, BF16)
        if stop - start > ENCODER_HEAD_DIM:
            ones = jnp.where(own_cells(keys.shape, span_len), ones, jnp.zeros_like(ones))
        sums.append(dot(part, ones))
    for (s, start, stop, _), top, bottom in zip(units, mixed, sums):
        token = block[s, :, start:stop].astype(F32)
        out_ref[s, :, start:stop] = (token + top / bottom).astype(BF16)


def encode_kernel(first, fanout, span_len, req_ref, states_ref, *refs):
    blocks, out_ref = refs[:-1], refs[-1]
    at = 0
    for block in blocks:
        stop = at + block.shape[0]
        encode_block(block, out_ref.at[at:stop], first + at, req_ref, states_ref, fanout, span_len)
        at = stop


def encode(req, span_states, blocks, first, fanout, span_len, gflops):
    slots = sum(block.shape[0] for block in blocks)
    return pl.pallas_call(
        functools.partial(encode_kernel, first, fanout, span_len),
        out_shape=jax.ShapeDtypeStruct((slots,) + blocks[0].shape[1:], BF16),
        in_specs=[SMEM, VMEM] + [VMEM] * len(blocks),
        out_specs=VMEM,
        compiler_params=params(16),
        cost_estimate=cost(gflops),
        name="encode",
    )(req, span_states, *blocks)


def encode_local_kernel(fanout, span_len, req_ref, pick_ref, states_ref, store_ref, out_ref, tokens_ref):
    for s in range(out_ref.shape[0]):
        tokens_ref[s] = store_ref[pick_ref[s]]
    encode_block(tokens_ref, out_ref, 0, req_ref, states_ref, fanout, span_len)


def encode_local(req, pick, span_states, store, cap, fanout, span_len):
    block = (cap,) + store.shape[1:]
    return pl.pallas_call(
        functools.partial(encode_local_kernel, fanout, span_len),
        out_shape=jax.ShapeDtypeStruct(block, BF16),
        in_specs=[SMEM, SMEM, VMEM, VMEM],
        out_specs=VMEM,
        scratch_shapes=[pltpu.VMEM(block, BF16)],
        compiler_params=params(16),
        cost_estimate=cost(10),
        name="encode_local",
    )(req, pick, span_states, store)


def project_into(kv_ref, first, pieces, wk_ref, wv_ref):
    n, slots, tokens, width = pieces[0].shape
    rows = jnp.concatenate([piece[...].reshape(n * slots * tokens, width) for piece in pieces], axis=0)
    cols = wk_ref.shape[1]
    for side, weight in enumerate((wk_ref, wv_ref)):
        made = dot(rows, weight[...]).astype(BF16)
        for p in range(n * len(pieces)):
            part = made[p * slots * tokens : (p + 1) * slots * tokens]
            kv_ref[first : first + slots, p, :, side * cols : (side + 1) * cols] = part.reshape(
                slots, tokens, cols
            )


def project_kernel(n_pieces, *refs):
    pieces, (wk_ref, wv_ref, kv_ref) = refs[:n_pieces], refs[n_pieces:]
    project_into(kv_ref, 0, pieces, wk_ref, wv_ref)


def project(pieces, w_key, w_value):
    n, slots, tokens, _ = pieces[0].shape
    shape = (slots, n * len(pieces), tokens, 2 * w_key.shape[1])
    return pl.pallas_call(
        functools.partial(project_kernel, len(pieces)),
        out_shape=jax.ShapeDtypeStruct(shape, BF16),
        in_specs=[VMEM] * (len(pieces) + 2),
        out_specs=VMEM,
        compiler_params=params(32),
        cost_estimate=cost(10),
        name="project",
    )(*pieces, w_key, w_value)


def attend_kernel(firsts, n_heads, n_rep, targets, fanout, spans, n_rest, slot_ref, q_ref, *refs):
    ready, (own_ref, *refs) = refs[: len(firsts) - 1], refs[len(firsts) - 1 :]
    if n_rest:
        pieces, (wk_ref, wv_ref, out_ref, rest_ref) = refs[:n_rest], refs[n_rest:]
        project_into(rest_ref, 0, pieces, wk_ref, wv_ref)
    else:
        rest_ref, out_ref = refs
    heads_at, rep_at = lax.axis_index("heads"), lax.axis_index("rep")
    cols = q_ref.shape[1]
    span_len = q_ref.shape[0] // spans
    block = spans // (n_heads * n_rep)

    def place(slot, first, count):
        return jnp.clip(slot - first, 0, count - 1)

    def held(slot, lanes):
        at = place(slot, firsts[-1], own_ref.shape[0])
        value = jnp.concatenate([own_ref[at, :, :, lanes], rest_ref[at, :, :, lanes]], axis=0)
        for ref, first in reversed(list(zip(ready, firsts))):
            there = slot < first + ref.shape[0]
            value = jnp.where(there, ref[place(slot, first, ref.shape[0]), :, :, lanes], value)
        return value.reshape(-1, HD)

    heads = [slice(h * HD, (h + 1) * HD) for h in range(cols // HD)]
    for at, (t, s) in enumerate(targets):
        owner = lax.rem(heads_at + t, n_heads) * n_rep + lax.rem(rep_at + s, n_rep)
        for i in range(block):
            span = owner * block + i
            slots = [slot_ref[span * fanout + k] for k in range(fanout)]
            rows = pl.ds(pl.multiple_of(span * span_len, span_len), span_len)

            def side(lanes):
                return jnp.concatenate([held(slot, lanes) for slot in slots], axis=0)

            logits = [dot_t(q_ref[rows, lanes], side(lanes)) for lanes in heads]
            tops = [jnp.max(part, axis=1, keepdims=True) for part in logits]
            weights = [jnp.exp((part - top) * HD ** (-0.5)) for part, top in zip(logits, tops)]
            scales = [1.0 / jnp.sum(part, axis=1, keepdims=True) for part in weights]
            mixed = [
                dot(part.astype(BF16), side(slice(cols + lanes.start, cols + lanes.stop)))
                for part, lanes in zip(weights, heads)
            ]
            for part, scale, lanes in zip(mixed, scales, heads):
                out_ref[at, i * span_len : (i + 1) * span_len, lanes] = (part * scale).astype(BF16)


def attend(slot, queries, ready, own, rest, weights, n_heads, n_rep, targets, fanout, spans):
    firsts = [0]
    for kv in ready:
        firsts.append(firsts[-1] + kv.shape[0])
    cols = queries.shape[1]
    rows = queries.shape[0] // (n_heads * n_rep)
    todo = isinstance(rest, list)
    slots, _, tokens, width = own.shape
    out_shape = [jax.ShapeDtypeStruct((len(targets), rows, cols), BF16)]
    if todo:
        others = sum(piece.shape[0] for piece in rest)
        out_shape.append(jax.ShapeDtypeStruct((slots, others, tokens, width), BF16))
    operands = [*rest, *weights] if todo else [rest]
    return pl.pallas_call(
        functools.partial(
            attend_kernel, firsts, n_heads, n_rep, targets, fanout, spans, len(rest) if todo else 0
        ),
        out_shape=out_shape,
        in_specs=[SMEM] + [VMEM] * (len(ready) + 2 + len(operands)),
        out_specs=[VMEM] * len(out_shape),
        compiler_params=params(32),
        cost_estimate=cost(0.001),
        name="attend",
    )(slot, queries, *ready, own, *operands)


def out_kernel(n_rep, n_received, *refs):
    mixed, weights, received = refs[:n_rep], refs[n_rep : 2 * n_rep], refs[2 * n_rep : 2 * n_rep + n_received]
    total = sum(dot(a[0], w[...]) for a, w in zip(mixed, weights))
    for part in received:
        total = total + part[...].astype(F32)
    refs[-1][...] = total.astype(BF16)


def out_project(mixed, weights, t, start, stop, tile, gflops, received=(), out=None, final=False):
    _, rows, depth = mixed[0].shape
    width = weights[0].shape[1]
    base = start // tile
    n = len(mixed)
    operands = [*mixed, *weights, *received] + ([] if out is None else [out])
    return pl.pallas_call(
        functools.partial(out_kernel, n, len(received)),
        grid=((stop - start) // tile,),
        out_shape=jax.ShapeDtypeStruct((rows, width if final else stop - start), BF16),
        in_specs=[pl.BlockSpec((1, rows, depth), lambda j: (t, 0, 0))] * n
        + [pl.BlockSpec((depth, tile), lambda j: (0, base + j))] * n
        + [pl.BlockSpec((rows, tile), lambda j: (0, j))] * len(received)
        + [ANY] * (out is not None),
        out_specs=pl.BlockSpec((rows, tile), lambda j: (0, (base if final else 0) + j)),
        input_output_aliases={} if out is None else {len(operands) - 1: 0},
        compiler_params=params(16),
        cost_estimate=cost(gflops),
        name="out_final" if final else "out_project",
    )(*operands)


def after(values, *earlier):
    return lax.optimization_barrier((values, earlier))[0]


def shards(queries, span_states, store, entry_ids, owners, w_key, w_value, w_out):
    n_lanes, n_heads, n_rep = (lax.axis_size(name) for name in ("lanes", "heads", "rep"))
    spans, fanout = entry_ids.shape
    requests = spans * fanout
    cap = max(2, (requests + n_lanes - 1) // n_lanes)
    span_len = queries.shape[0] // spans

    def over_heads(array):
        return [array] + [lax.ppermute(array, "heads", shift_pairs(n_heads, s)) for s in range(1, n_heads)]

    def over_rep(array):
        return [array] + [lax.ppermute(array, "rep", shift_pairs(n_rep, s)) for s in range(1, n_rep)]

    order = list(range(n_lanes))
    items = []
    for d in order[1:]:
        cuts = (0, cap // 2, cap) if d in (1, n_lanes - 1) else (0, cap)
        items += [(d, low, high) for low, high in zip(cuts, cuts[1:])]
    middle = range(2, max(2, len(items) - 2))
    parts = [part for part in (range(0, 1), range(1, 2), middle, *(range(i, i + 1) for i in range(len(items))[-2:])) if part]
    groups = ((1, 2), (3,), (4, 5))

    own = jnp.concatenate([owners.T, entry_ids.T], axis=0)
    asked = [lax.ppermute(own, "lanes", lane_pairs(n_lanes, d, False)) for d in range(1, n_lanes)]
    req, slot, pick = plan(own, order, cap)
    encoded = encode_local(req, pick, span_states, store, cap, fanout, span_len)
    blocks = fetch(after(asked, encoded), store, items, cap)

    def send(part, *earlier):
        ready = after([blocks[i] for i in part], *earlier)
        return [
            lax.ppermute(block, "lanes", lane_pairs(n_lanes, items[i][0], True))
            for block, i in zip(ready, part)
        ]

    def stack(members, *earlier):
        ready = after([crossed[i] for i in members], *earlier)
        return jnp.stack([jnp.concatenate(piece, axis=0) for piece in zip(*ready)])

    crossed, pieces = [over_heads(encoded)], []
    arrived = [None] + [send(part) for part in parts[:3]]
    last = blocks
    for i, part in enumerate(parts, 1):
        if i + 3 <= len(parts):
            arrived.append(send(parts[i + 2], arrived[SEND_AFTER[i]], last))
        first = items[part[0]][0] * cap + items[part[0]][1]
        encoded = encode(
            req, span_states, after(arrived[i], last), first, fanout, span_len, ENCODE_COST[i]
        )
        crossed.append(over_heads(encoded))
        last = encoded
        for members in STACK_AFTER.get(i, ()):
            last = stack(members, last)
            pieces.append(over_rep(last))
    w_outs = over_rep(w_out)
    kvs, last = [], after(last, w_outs)
    while len(kvs) < len(pieces):
        last = project(after(pieces[len(kvs)], last), w_key, w_value)
        kvs.append(last)
    pieces = over_rep(stack(groups[-1], kvs))
    own_kv, rest = project(pieces[:1], w_key, w_value), pieces[1:]

    def mix(turns, q, rest):
        mixed = []
        for s in range(1, n_rep):
            given, *made = attend(
                slot, q, kvs, own_kv, rest, (w_key, w_value), n_heads, n_rep, [(t, s) for t in turns], fanout, spans
            )
            rest = made[0] if made else rest
            mixed.append(lax.ppermute(given, "rep", shift_pairs(n_rep, s)))
        kept = attend(
            slot, q, kvs, own_kv, rest, (w_key, w_value), n_heads, n_rep, [(t, 0) for t in turns], fanout, spans
        )
        return [kept[0]] + mixed, rest

    width = w_out.shape[1]
    tile = min(COL_TILE, width)
    cuts = [width // tile * part // 8 * tile for part in (0, 2, 4, 6, 7)] + [width]
    blocks = [(start, stop) for start, stop in zip(cuts, cuts[1:]) if stop > start]
    mixed, rest = mix(list(range(1, n_heads)), queries, rest)
    received, partials = [[] for _ in blocks], []
    for t in range(1, n_heads):
        for i, (start, stop) in enumerate(blocks):
            partial = out_project(mixed, w_outs, t - 1, start, stop, tile, 0.001)
            partial, mixed = lax.optimization_barrier((partial, mixed))
            partials.append(partial)
            received[i].append(lax.ppermute(partial, "heads", shift_pairs(n_heads, t)))
    mixed, rest = mix([0], after(queries, partials), rest)
    out = None
    for (start, stop), parts in zip(blocks, received):
        out = out_project(mixed, w_outs, 0, start, stop, tile, 0.2, parts, out, True)
    return out


def solution(mesh):
    return jax.shard_map(
        shards,
        mesh=mesh,
        in_specs=(
            P(("groups", "lanes"), ("heads", "rep")),
            P(("groups", "lanes"), None),
            P(("groups", "lanes"), ("heads", "rep"), None),
            P(("groups", "lanes"), None),
            P(("groups", "lanes"), None),
            P(None, ("heads", "rep")),
            P(None, ("heads", "rep")),
            P(("heads", "rep"), None),
        ),
        out_specs=P(("groups", "lanes", "heads", "rep"), None),
        check_vma=False,
    )
```

```python
import functools

import jax
import jax.numpy as jnp
from jax import lax
from jax.experimental import pallas as pl
from jax.experimental.pallas import tpu as pltpu
from jax.sharding import PartitionSpec as P

HD = 128
ENCODER_HEAD_DIM = 128
F32 = jnp.float32
BF16 = jnp.bfloat16
LATER_GROUPS = 2
COL_TILE = 512
ENCODE_COST = (None, 0.1, 10, 10)

VMEM = pl.BlockSpec(memory_space=pltpu.VMEM)
SMEM = pl.BlockSpec(memory_space=pltpu.SMEM)
ANY = pl.BlockSpec(memory_space=pl.ANY)


def params(mib):
    return pltpu.CompilerParams(vmem_limit_bytes=mib * 2**20)


def cost(gflops):
    return pl.CostEstimate(flops=int(gflops * 10**9), bytes_accessed=1024, transcendentals=0)


def apart(n, a, b):
    if n & (n - 1) == 0:
        return a ^ b
    return lax.rem(b - a + n, n)


def lane_pairs(n, d, reply):
    if n & (n - 1) == 0:
        return [(i, i ^ d) for i in range(n)]
    return [(i, (i - d if reply else i + d) % n) for i in range(n)]


def shift_pairs(n, s):
    return [(i, (i + s) % n) for i in range(n)]


def dot_t(a, b):
    return lax.dot_general(a, b, (((1,), (1,)), ((), ())), preferred_element_type=F32)


def dot(a, b):
    return jnp.dot(a, b, preferred_element_type=F32)


def plan_kernel(order, cap, own_ref, req_ref, slot_ref, pick_ref, next_ref):
    n_lanes = len(order)
    lane = lax.axis_index("lanes")
    fanout, spans = own_ref.shape[0] // 2, own_ref.shape[1]
    for i, d in enumerate(order):
        next_ref[d] = i * cap
    for i in range(n_lanes * cap):
        pick_ref[i] = 0
        req_ref[i] = 0
    for j in range(fanout * spans):
        span, k = j // fanout, j % fanout
        d = apart(n_lanes, lane, own_ref[k, span])
        slot = next_ref[d]
        next_ref[d] = slot + 1
        pick_ref[slot] = own_ref[fanout + k, span]
        req_ref[slot] = j
        slot_ref[j] = slot


def plan(own, order, cap):
    table = jax.ShapeDtypeStruct((len(order) * cap,), jnp.int32)
    return pl.pallas_call(
        functools.partial(plan_kernel, order, cap),
        out_shape=(table, jax.ShapeDtypeStruct((own.size // 2,), jnp.int32), table),
        in_specs=[SMEM],
        out_specs=(SMEM, SMEM, SMEM),
        scratch_shapes=[pltpu.SMEM((len(order),), jnp.int32)],
        compiler_params=params(16),
        cost_estimate=cost(10),
        name="plan",
    )(own)


def fetch_kernel(items, cap, *refs):
    others = max(d for d, _, _ in items)
    asked, store_ref, refs = refs[:others], refs[others], refs[others + 1 :]
    blocks, pick_ref = refs[:-1], refs[-1]
    lane = lax.axis_index("lanes")
    fanout, spans = asked[0].shape[0] // 2, asked[0].shape[1]
    for i in range(others * cap):
        pick_ref[i] = 0
    for d in range(others):
        place = d * cap
        for span in range(spans):
            for k in range(fanout):
                pick_ref[place] = asked[d][fanout + k, span]
                place = place + (asked[d][k, span] == lane).astype(jnp.int32)
    for block, (d, low, high) in zip(blocks, items):
        for s in range(low, high):
            block[s - low] = store_ref[pick_ref[(d - 1) * cap + s]]


def fetch(asked, store, items, cap):
    others = len(asked)
    return pl.pallas_call(
        functools.partial(fetch_kernel, items, cap),
        out_shape=[
            jax.ShapeDtypeStruct((high - low,) + store.shape[1:], store.dtype) for _, low, high in items
        ],
        in_specs=[SMEM] * others + [VMEM],
        out_specs=[VMEM] * len(items),
        scratch_shapes=[pltpu.SMEM((others * cap + 1,), jnp.int32)],
        compiler_params=params(16),
        cost_estimate=cost(10),
        name="fetch",
    )(*asked, store)


def encode_pairs(width):
    step = 2 * ENCODER_HEAD_DIM
    return [(start, min(start + step, width)) for start in range(0, width, step)]


def spread(states, start, stop):
    part = states[:, start:stop]
    heads = (stop - start) // ENCODER_HEAD_DIM
    if heads == 1:
        return part
    rows = jnp.concatenate([part] * heads, axis=0)
    return jnp.where(own_cells(rows.shape, part.shape[0]), rows, jnp.zeros_like(rows))


def own_cells(shape, keys):
    row = lax.broadcasted_iota(jnp.int32, shape, 0)
    col = lax.broadcasted_iota(jnp.int32, shape, 1)
    return (row >= keys) == (col >= ENCODER_HEAD_DIM)


def softmax_top(logits, keys):
    if logits.shape[1] == keys:
        return jnp.max(logits, axis=1, keepdims=True)
    first = lax.broadcasted_iota(jnp.int32, logits.shape, 1) < keys
    low = jnp.max(jnp.where(first, logits, -jnp.inf), axis=1, keepdims=True)
    high = jnp.max(jnp.where(first, -jnp.inf, logits), axis=1, keepdims=True)
    return jnp.where(first, low, high)


def encode_block(block, out_ref, first, req_ref, states_ref, fanout, span_len):
    scale = ENCODER_HEAD_DIM ** (-0.5)
    runs = encode_pairs(states_ref.shape[1])
    units = []
    for s in range(block.shape[0]):
        span = lax.div(req_ref[first + s], fanout)
        states = states_ref[pl.ds(pl.multiple_of(span * span_len, span_len), span_len), :]
        units += [(s, start, stop, spread(states, start, stop)) for start, stop in runs]
    logits = [dot_t(block[s, :, start:stop], keys) for s, start, stop, keys in units]
    tops = [softmax_top(part, span_len) for part in logits]
    weights = [jnp.exp((part - top) * scale).astype(BF16) for part, top in zip(logits, tops)]
    mixed = [dot(part, keys) for part, (_, _, _, keys) in zip(weights, units)]
    sums = []
    for part, (_, start, stop, keys) in zip(weights, units):
        ones = jnp.ones(keys.shape, BF16)
        if stop - start > ENCODER_HEAD_DIM:
            ones = jnp.where(own_cells(keys.shape, span_len), ones, jnp.zeros_like(ones))
        sums.append(dot(part, ones))
    for (s, start, stop, _), top, bottom in zip(units, mixed, sums):
        token = block[s, :, start:stop].astype(F32)
        out_ref[s, :, start:stop] = (token + top / bottom).astype(BF16)


def encode_kernel(first, fanout, span_len, req_ref, states_ref, *refs):
    blocks, out_ref = refs[:-1], refs[-1]
    at = 0
    for block in blocks:
        stop = at + block.shape[0]
        encode_block(block, out_ref.at[at:stop], first + at, req_ref, states_ref, fanout, span_len)
        at = stop


def encode(req, span_states, blocks, first, fanout, span_len, gflops):
    slots = sum(block.shape[0] for block in blocks)
    return pl.pallas_call(
        functools.partial(encode_kernel, first, fanout, span_len),
        out_shape=jax.ShapeDtypeStruct((slots,) + blocks[0].shape[1:], BF16),
        in_specs=[SMEM, VMEM] + [VMEM] * len(blocks),
        out_specs=VMEM,
        compiler_params=params(16),
        cost_estimate=cost(gflops),
        name="encode",
    )(req, span_states, *blocks)


def encode_local_kernel(fanout, span_len, req_ref, pick_ref, states_ref, store_ref, out_ref, tokens_ref):
    for s in range(out_ref.shape[0]):
        tokens_ref[s] = store_ref[pick_ref[s]]
    encode_block(tokens_ref, out_ref, 0, req_ref, states_ref, fanout, span_len)


def encode_local(req, pick, span_states, store, cap, fanout, span_len):
    block = (cap,) + store.shape[1:]
    return pl.pallas_call(
        functools.partial(encode_local_kernel, fanout, span_len),
        out_shape=jax.ShapeDtypeStruct(block, BF16),
        in_specs=[SMEM, SMEM, VMEM, VMEM],
        out_specs=VMEM,
        scratch_shapes=[pltpu.VMEM(block, BF16)],
        compiler_params=params(16),
        cost_estimate=cost(10),
        name="encode_local",
    )(req, pick, span_states, store)


def project_into(kv_ref, first, pieces, wk_ref, wv_ref):
    n, slots, tokens, width = pieces[0].shape
    rows = jnp.concatenate([piece[...].reshape(n * slots * tokens, width) for piece in pieces], axis=0)
    cols = wk_ref.shape[1]
    for side, weight in enumerate((wk_ref, wv_ref)):
        made = dot(rows, weight[...]).astype(BF16)
        for p in range(n * len(pieces)):
            part = made[p * slots * tokens : (p + 1) * slots * tokens]
            kv_ref[first : first + slots, p, :, side * cols : (side + 1) * cols] = part.reshape(
                slots, tokens, cols
            )


def project_kernel(n_pieces, *refs):
    pieces, (wk_ref, wv_ref, kv_ref) = refs[:n_pieces], refs[n_pieces:]
    project_into(kv_ref, 0, pieces, wk_ref, wv_ref)


def project(pieces, w_key, w_value):
    n, slots, tokens, _ = pieces[0].shape
    shape = (slots, n * len(pieces), tokens, 2 * w_key.shape[1])
    return pl.pallas_call(
        functools.partial(project_kernel, len(pieces)),
        out_shape=jax.ShapeDtypeStruct(shape, BF16),
        in_specs=[VMEM] * (len(pieces) + 2),
        out_specs=VMEM,
        compiler_params=params(32),
        cost_estimate=cost(10),
        name="project",
    )(*pieces, w_key, w_value)


def attend_kernel(firsts, n_own, n_heads, n_rep, targets, fanout, spans, n_rest, slot_ref, q_ref, *refs):
    ready, refs = refs[: len(firsts) - 1], refs[len(firsts) - 1 :]
    own, refs = refs[:n_own], refs[n_own:]
    if n_rest:
        pieces, (wk_ref, wv_ref, out_ref, rest_ref) = refs[:n_rest], refs[n_rest:]
        project_into(rest_ref, 0, pieces, wk_ref, wv_ref)
    else:
        rest_ref, out_ref = refs
    heads_at, rep_at = lax.axis_index("heads"), lax.axis_index("rep")
    cols = q_ref.shape[1]
    span_len = q_ref.shape[0] // spans
    block = spans // (n_heads * n_rep)

    def place(slot, first, count):
        return jnp.clip(slot - first, 0, count - 1)

    def held(slot, lanes):
        at = place(slot, firsts[-1], rest_ref.shape[0])
        value = jnp.concatenate([ref[at, :, :, lanes] for ref in (*own, rest_ref)], axis=0)
        for ref, first in reversed(list(zip(ready, firsts))):
            there = slot < first + ref.shape[0]
            value = jnp.where(there, ref[place(slot, first, ref.shape[0]), :, :, lanes], value)
        return value.reshape(-1, HD)

    heads = [slice(h * HD, (h + 1) * HD) for h in range(cols // HD)]
    for at, (t, s) in enumerate(targets):
        owner = lax.rem(heads_at + t, n_heads) * n_rep + lax.rem(rep_at + s, n_rep)
        for i in range(block):
            span = owner * block + i
            slots = [slot_ref[span * fanout + k] for k in range(fanout)]
            rows = pl.ds(pl.multiple_of(span * span_len, span_len), span_len)

            def side(lanes):
                return jnp.concatenate([held(slot, lanes) for slot in slots], axis=0)

            logits = [dot_t(q_ref[rows, lanes], side(lanes)) for lanes in heads]
            tops = [jnp.max(part, axis=1, keepdims=True) for part in logits]
            weights = [jnp.exp((part - top) * HD ** (-0.5)) for part, top in zip(logits, tops)]
            scales = [1.0 / jnp.sum(part, axis=1, keepdims=True) for part in weights]
            mixed = [
                dot(part.astype(BF16), side(slice(cols + lanes.start, cols + lanes.stop)))
                for part, lanes in zip(weights, heads)
            ]
            for part, scale, lanes in zip(mixed, scales, heads):
                out_ref[at, i * span_len : (i + 1) * span_len, lanes] = (part * scale).astype(BF16)


def attend(slot, queries, ready, own, rest, weights, n_heads, n_rep, targets, fanout, spans):
    firsts = [0]
    for kv in ready:
        firsts.append(firsts[-1] + kv.shape[0])
    cols = queries.shape[1]
    rows = queries.shape[0] // (n_heads * n_rep)
    todo = isinstance(rest, list)
    slots, _, tokens, width = own[0].shape
    out_shape = [jax.ShapeDtypeStruct((len(targets), rows, cols), BF16)]
    if todo:
        others = sum(piece.shape[0] for piece in rest)
        out_shape.append(jax.ShapeDtypeStruct((slots, others, tokens, width), BF16))
    operands = [*rest, *weights] if todo else [rest]
    return pl.pallas_call(
        functools.partial(
            attend_kernel, firsts, len(own), n_heads, n_rep, targets, fanout, spans, len(rest) if todo else 0
        ),
        out_shape=out_shape,
        in_specs=[SMEM] + [VMEM] * (len(ready) + 1 + len(own) + len(operands)),
        out_specs=[VMEM] * len(out_shape),
        compiler_params=params(32),
        cost_estimate=cost(0.001),
        name="attend",
    )(slot, queries, *ready, *own, *operands)


def out_kernel(n_rep, n_received, *refs):
    mixed, weights, received = refs[:n_rep], refs[n_rep : 2 * n_rep], refs[2 * n_rep : 2 * n_rep + n_received]
    parts = [dot(a[0], w[...]) for a, w in zip(mixed, weights)] + [part[...].astype(F32) for part in received]
    refs[-1][...] = sum(parts).astype(BF16)


def out_project(mixed, weights, t, start, stop, tile, gflops, received=(), out=None, final=False):
    rows = (mixed[0].shape[1:] if mixed else received[0].shape)[0]
    base = start // tile
    n = len(mixed)
    operands = [*mixed, *weights, *received] + ([] if out is None else [out])
    width = (weights[0] if mixed else out).shape[1]
    return pl.pallas_call(
        functools.partial(out_kernel, n, len(received)),
        grid=((stop - start) // tile,),
        out_shape=jax.ShapeDtypeStruct((rows, width if final else stop - start), BF16),
        in_specs=[pl.BlockSpec((1, *a.shape[1:]), lambda j: (t, 0, 0)) for a in mixed]
        + [pl.BlockSpec((w.shape[0], tile), lambda j: (0, base + j)) for w in weights]
        + [pl.BlockSpec((rows, tile), lambda j: (0, j))] * len(received)
        + [ANY] * (out is not None),
        out_specs=pl.BlockSpec((rows, tile), lambda j: (0, (base if final else 0) + j)),
        input_output_aliases={} if out is None else {len(operands) - 1: 0},
        compiler_params=params(16),
        cost_estimate=cost(gflops),
        name="out_final" if final else "out_project",
    )(*operands)


def after(values, *earlier):
    return lax.optimization_barrier((values, earlier))[0]


def shards(queries, span_states, store, entry_ids, owners, w_key, w_value, w_out):
    n_lanes, n_heads, n_rep = (lax.axis_size(name) for name in ("lanes", "heads", "rep"))
    spans, fanout = entry_ids.shape
    requests = spans * fanout
    cap = max(2, (requests + n_lanes - 1) // n_lanes)
    span_len = queries.shape[0] // spans

    def over_heads(array):
        return [array] + [lax.ppermute(array, "heads", shift_pairs(n_heads, s)) for s in range(1, n_heads)]

    def over_rep(array):
        return [array] + [lax.ppermute(array, "rep", shift_pairs(n_rep, s)) for s in range(1, n_rep)]

    order = list(range(n_lanes))
    items = []
    for d in order[1:]:
        cuts = (0, cap // 2, cap) if d == 1 else (0, cap)
        items += [(d, low, high) for low, high in zip(cuts, cuts[1:])]
    size = max(1, -(-(len(items) - 2) // LATER_GROUPS))
    cuts = [0] + list(range(2, len(items), size)) + [len(items)]
    parts = [range(low, high) for low, high in zip(cuts, cuts[1:])]

    own = jnp.concatenate([owners.T, entry_ids.T], axis=0)
    asked = [lax.ppermute(own, "lanes", lane_pairs(n_lanes, d, False)) for d in range(1, n_lanes)]
    req, slot, pick = plan(own, order, cap)
    encoded = encode_local(req, pick, span_states, store, cap, fanout, span_len)
    blocks = fetch(after(asked, encoded), store, items, cap)

    def send(part, *earlier):
        ready = after([blocks[i] for i in part], *earlier)
        return [
            lax.ppermute(block, "lanes", lane_pairs(n_lanes, items[i][0], True))
            for block, i in zip(ready, part)
        ]

    crossed, pieces = [over_heads(encoded)], []
    arrived = [None] + [send(part) for part in parts[:2]]
    last = blocks
    for i, part in enumerate(parts, 1):
        if i + 2 <= len(parts):
            arrived.append(send(parts[i + 1], arrived[i], last))
        first = items[part[0]][0] * cap + items[part[0]][1]
        encoded = encode(
            req, span_states, after(arrived[i], last), first, fanout, span_len, ENCODE_COST[i]
        )
        crossed.append(over_heads(encoded))
        last = encoded
        while i > 1 and len(pieces) < i:
            last = jnp.stack(after(crossed[len(pieces)], last))
            pieces.append(over_rep(last))
    w_outs = over_rep(w_out)
    kvs, last = [], after(last, w_outs)
    while len(kvs) < len(pieces):
        last = project(after(pieces[len(kvs)], last), w_key, w_value)
        kvs.append(last)
    local, *remote = crossed[-1]
    early = [piece[None] for piece in over_rep(after(local, kvs[0]))]
    last = project(after(early, last), w_key, w_value)
    own_kv = [last]
    remote = jnp.stack(after(remote, kvs, last))
    _, *rest = over_rep(remote)
    own_kv.append(project([remote], w_key, w_value))

    def mix(turns, q, rest):
        mixed = []
        for s in range(1, n_rep):
            given, *made = attend(
                slot, q, kvs, own_kv, rest, (w_key, w_value), n_heads, n_rep, [(t, s) for t in turns], fanout, spans
            )
            rest = made[0] if made else rest
            mixed.append(lax.ppermute(given, "rep", shift_pairs(n_rep, s)))
        kept = attend(
            slot, q, kvs, own_kv, rest, (w_key, w_value), n_heads, n_rep, [(t, 0) for t in turns], fanout, spans
        )
        return [kept[0]] + mixed, rest

    width = w_out.shape[1]
    tile = min(COL_TILE, width)
    cuts = [width // tile * part // 8 * tile for part in (0, 2, 4, 6, 7)] + [width]
    blocks = [(start, stop) for start, stop in zip(cuts, cuts[1:]) if stop > start]
    mixed, rest = mix(list(range(1, n_heads)), queries, rest)
    received, partials = [[] for _ in blocks], []
    for t in range(1, n_heads):
        for i, (start, stop) in enumerate(blocks):
            partial = out_project(mixed, w_outs, t - 1, start, stop, tile, 0.001)
            partial, mixed = lax.optimization_barrier((partial, mixed))
            partials.append(partial)
            received[i].append(lax.ppermute(partial, "heads", shift_pairs(n_heads, t)))
    mixed, rest = mix([0], after(queries, partials), rest)
    out, ahead = None, out_project(mixed, w_outs, 0, *blocks[-1], tile, 0.001)
    for i, ((start, stop), parts) in enumerate(zip(blocks, received)):
        if i + 1 < len(blocks):
            out = out_project(mixed, w_outs, 0, start, stop, tile, 0.2, parts, out, True)
        else:
            out = out_project([], [], 0, start, stop, tile, 0.2, [ahead, *parts], out, True)
    return out


def solution(mesh):
    return jax.shard_map(
        shards,
        mesh=mesh,
        in_specs=(
            P(("groups", "lanes"), ("heads", "rep")),
            P(("groups", "lanes"), None),
            P(("groups", "lanes"), ("heads", "rep"), None),
            P(("groups", "lanes"), None),
            P(("groups", "lanes"), None),
            P(None, ("heads", "rep")),
            P(None, ("heads", "rep")),
            P(("heads", "rep"), None),
        ),
        out_specs=P(("groups", "lanes", "heads", "rep"), None),
        check_vma=False,
    )
```

```python
import functools

import jax
import jax.numpy as jnp
from jax import lax
from jax.experimental import pallas as pl
from jax.experimental.pallas import tpu as pltpu
from jax.sharding import PartitionSpec as P

HD = 128
ENCODER_HEAD_DIM = 128
F32 = jnp.float32
BF16 = jnp.bfloat16
LATER_GROUPS = 2
COL_TILE = 512
ENCODE_COST = (None, 0.1, 10, 10)

VMEM = pl.BlockSpec(memory_space=pltpu.VMEM)
SMEM = pl.BlockSpec(memory_space=pltpu.SMEM)
ANY = pl.BlockSpec(memory_space=pl.ANY)


def params(mib):
    return pltpu.CompilerParams(vmem_limit_bytes=mib * 2**20)


def cost(gflops):
    return pl.CostEstimate(flops=int(gflops * 10**9), bytes_accessed=1024, transcendentals=0)


def apart(n, a, b):
    if n & (n - 1) == 0:
        return a ^ b
    return lax.rem(b - a + n, n)


def lane_pairs(n, d, reply):
    if n & (n - 1) == 0:
        return [(i, i ^ d) for i in range(n)]
    return [(i, (i - d if reply else i + d) % n) for i in range(n)]


def tables_of_lanes(own, n, meanwhile):
    if n & (n - 1):
        others = [lax.ppermute(own, "lanes", lane_pairs(n, d, False)) for d in range(1, n)]
        return jnp.concatenate([own] + others, axis=0)
    step, held = 1, own
    while step < n:
        other = lax.ppermute(held, "lanes", lane_pairs(n, step, False))
        held = jnp.concatenate(after([held, other], meanwhile if step == 1 else ()), axis=0)
        step *= 2
    return held


def shift_pairs(n, s):
    return [(i, (i + s) % n) for i in range(n)]


def dot_t(a, b):
    return lax.dot_general(a, b, (((1,), (1,)), ((), ())), preferred_element_type=F32)


def dot(a, b):
    return jnp.dot(a, b, preferred_element_type=F32)


def plan_kernel(order, cap, own_ref, req_ref, slot_ref, pick_ref, next_ref):
    n_lanes = len(order)
    lane = lax.axis_index("lanes")
    fanout, spans = own_ref.shape[0] // 2, own_ref.shape[1]
    for i, d in enumerate(order):
        next_ref[d] = i * cap
    for i in range(n_lanes * cap):
        pick_ref[i] = 0
        req_ref[i] = 0
    for j in range(fanout * spans):
        span, k = j // fanout, j % fanout
        d = apart(n_lanes, lane, own_ref[k, span])
        slot = next_ref[d]
        next_ref[d] = slot + 1
        pick_ref[slot] = own_ref[fanout + k, span]
        req_ref[slot] = j
        slot_ref[j] = slot


def plan(own, order, cap):
    table = jax.ShapeDtypeStruct((len(order) * cap,), jnp.int32)
    return pl.pallas_call(
        functools.partial(plan_kernel, order, cap),
        out_shape=(table, jax.ShapeDtypeStruct((own.size // 2,), jnp.int32), table),
        in_specs=[SMEM],
        out_specs=(SMEM, SMEM, SMEM),
        scratch_shapes=[pltpu.SMEM((len(order),), jnp.int32)],
        compiler_params=params(16),
        cost_estimate=cost(10),
        name="plan",
    )(own)


def fetch_kernel(items, cap, fanout, tables_ref, store_ref, *refs):
    blocks, pick_ref = refs[:-1], refs[-1]
    lane = lax.axis_index("lanes")
    spans = tables_ref.shape[1]
    others = tables_ref.shape[0] // (2 * fanout) - 1
    for i in range(others * cap):
        pick_ref[i] = 0
    for d in range(others):
        place, row = d * cap, (d + 1) * 2 * fanout
        for span in range(spans):
            for k in range(fanout):
                pick_ref[place] = tables_ref[row + fanout + k, span]
                place = place + (tables_ref[row + k, span] == lane).astype(jnp.int32)
    for block, (d, low, high) in zip(blocks, items):
        for s in range(low, high):
            block[s - low] = store_ref[pick_ref[(d - 1) * cap + s]]


def fetch(tables, store, items, cap, fanout):
    others = tables.shape[0] // (2 * fanout) - 1
    return pl.pallas_call(
        functools.partial(fetch_kernel, items, cap, fanout),
        out_shape=[
            jax.ShapeDtypeStruct((high - low,) + store.shape[1:], store.dtype) for _, low, high in items
        ],
        in_specs=[SMEM, VMEM],
        out_specs=[VMEM] * len(items),
        scratch_shapes=[pltpu.SMEM((others * cap + 1,), jnp.int32)],
        compiler_params=params(16),
        cost_estimate=cost(10),
        name="fetch",
    )(tables, store)


def encode_pairs(width):
    step = 2 * ENCODER_HEAD_DIM
    return [(start, min(start + step, width)) for start in range(0, width, step)]


def spread(states, start, stop):
    part = states[:, start:stop]
    heads = (stop - start) // ENCODER_HEAD_DIM
    if heads == 1:
        return part
    rows = jnp.concatenate([part] * heads, axis=0)
    return jnp.where(own_cells(rows.shape, part.shape[0]), rows, jnp.zeros_like(rows))


def own_cells(shape, keys):
    row = lax.broadcasted_iota(jnp.int32, shape, 0)
    col = lax.broadcasted_iota(jnp.int32, shape, 1)
    return (row >= keys) == (col >= ENCODER_HEAD_DIM)


def softmax_top(logits, keys):
    if logits.shape[1] == keys:
        return jnp.max(logits, axis=1, keepdims=True)
    first = lax.broadcasted_iota(jnp.int32, logits.shape, 1) < keys
    low = jnp.max(jnp.where(first, logits, -jnp.inf), axis=1, keepdims=True)
    high = jnp.max(jnp.where(first, -jnp.inf, logits), axis=1, keepdims=True)
    return jnp.where(first, low, high)


def encode_block(block, out_ref, first, req_ref, states_ref, fanout, span_len):
    scale = ENCODER_HEAD_DIM ** (-0.5)
    runs = encode_pairs(states_ref.shape[1])
    units = []
    for s in range(block.shape[0]):
        span = lax.div(req_ref[first + s], fanout)
        states = states_ref[pl.ds(pl.multiple_of(span * span_len, span_len), span_len), :]
        units += [(s, start, stop, spread(states, start, stop)) for start, stop in runs]
    logits = [dot_t(block[s, :, start:stop], keys) for s, start, stop, keys in units]
    tops = [softmax_top(part, span_len) for part in logits]
    weights = [jnp.exp((part - top) * scale).astype(BF16) for part, top in zip(logits, tops)]
    mixed = [dot(part, keys) for part, (_, _, _, keys) in zip(weights, units)]
    sums = []
    for part, (_, start, stop, keys) in zip(weights, units):
        ones = jnp.ones(keys.shape, BF16)
        if stop - start > ENCODER_HEAD_DIM:
            ones = jnp.where(own_cells(keys.shape, span_len), ones, jnp.zeros_like(ones))
        sums.append(dot(part, ones))
    for (s, start, stop, _), top, bottom in zip(units, mixed, sums):
        token = block[s, :, start:stop].astype(F32)
        out_ref[s, :, start:stop] = (token + top / bottom).astype(BF16)


def encode_kernel(first, fanout, span_len, req_ref, states_ref, *refs):
    blocks, out_ref = refs[:-1], refs[-1]
    at = 0
    for block in blocks:
        stop = at + block.shape[0]
        encode_block(block, out_ref.at[at:stop], first + at, req_ref, states_ref, fanout, span_len)
        at = stop


def encode(req, span_states, blocks, first, fanout, span_len, gflops):
    slots = sum(block.shape[0] for block in blocks)
    return pl.pallas_call(
        functools.partial(encode_kernel, first, fanout, span_len),
        out_shape=jax.ShapeDtypeStruct((slots,) + blocks[0].shape[1:], BF16),
        in_specs=[SMEM, VMEM] + [VMEM] * len(blocks),
        out_specs=VMEM,
        compiler_params=params(16),
        cost_estimate=cost(gflops),
        name="encode",
    )(req, span_states, *blocks)


def encode_local_kernel(fanout, span_len, req_ref, pick_ref, states_ref, store_ref, out_ref, tokens_ref):
    for s in range(out_ref.shape[0]):
        tokens_ref[s] = store_ref[pick_ref[s]]
    encode_block(tokens_ref, out_ref, 0, req_ref, states_ref, fanout, span_len)


def encode_local(req, pick, span_states, store, cap, fanout, span_len):
    block = (cap,) + store.shape[1:]
    return pl.pallas_call(
        functools.partial(encode_local_kernel, fanout, span_len),
        out_shape=jax.ShapeDtypeStruct(block, BF16),
        in_specs=[SMEM, SMEM, VMEM, VMEM],
        out_specs=VMEM,
        scratch_shapes=[pltpu.VMEM(block, BF16)],
        compiler_params=params(16),
        cost_estimate=cost(10),
        name="encode_local",
    )(req, pick, span_states, store)


def project_into(kv_ref, first, pieces, wk_ref, wv_ref):
    n, slots, tokens, width = pieces[0].shape
    rows = jnp.concatenate([piece[...].reshape(n * slots * tokens, width) for piece in pieces], axis=0)
    cols = wk_ref.shape[1]
    for side, weight in enumerate((wk_ref, wv_ref)):
        made = dot(rows, weight[...]).astype(BF16)
        for p in range(n * len(pieces)):
            part = made[p * slots * tokens : (p + 1) * slots * tokens]
            kv_ref[first : first + slots, p, :, side * cols : (side + 1) * cols] = part.reshape(
                slots, tokens, cols
            )


def project_kernel(n_pieces, *refs):
    pieces, (wk_ref, wv_ref, kv_ref) = refs[:n_pieces], refs[n_pieces:]
    project_into(kv_ref, 0, pieces, wk_ref, wv_ref)


def project(pieces, w_key, w_value):
    n, slots, tokens, _ = pieces[0].shape
    shape = (slots, n * len(pieces), tokens, 2 * w_key.shape[1])
    return pl.pallas_call(
        functools.partial(project_kernel, len(pieces)),
        out_shape=jax.ShapeDtypeStruct(shape, BF16),
        in_specs=[VMEM] * (len(pieces) + 2),
        out_specs=VMEM,
        compiler_params=params(32),
        cost_estimate=cost(10),
        name="project",
    )(*pieces, w_key, w_value)


def attend_kernel(firsts, n_own, n_heads, n_rep, targets, fanout, spans, n_rest, slot_ref, q_ref, *refs):
    ready, refs = refs[: len(firsts) - 1], refs[len(firsts) - 1 :]
    own, refs = refs[:n_own], refs[n_own:]
    if n_rest:
        pieces, (wk_ref, wv_ref, out_ref, rest_ref) = refs[:n_rest], refs[n_rest:]
        project_into(rest_ref, 0, pieces, wk_ref, wv_ref)
    else:
        rest_ref, out_ref = refs
    heads_at, rep_at = lax.axis_index("heads"), lax.axis_index("rep")
    cols = q_ref.shape[1]
    span_len = q_ref.shape[0] // spans
    block = spans // (n_heads * n_rep)

    def place(slot, first, count):
        return jnp.clip(slot - first, 0, count - 1)

    def held(slot, lanes):
        at = place(slot, firsts[-1], rest_ref.shape[0])
        value = jnp.concatenate([ref[at, :, :, lanes] for ref in (*own, rest_ref)], axis=0)
        for ref, first in reversed(list(zip(ready, firsts))):
            there = slot < first + ref.shape[0]
            value = jnp.where(there, ref[place(slot, first, ref.shape[0]), :, :, lanes], value)
        return value.reshape(-1, HD)

    heads = [slice(h * HD, (h + 1) * HD) for h in range(cols // HD)]
    for at, (t, s) in enumerate(targets):
        owner = lax.rem(heads_at + t, n_heads) * n_rep + lax.rem(rep_at + s, n_rep)
        for i in range(block):
            span = owner * block + i
            slots = [slot_ref[span * fanout + k] for k in range(fanout)]
            rows = pl.ds(pl.multiple_of(span * span_len, span_len), span_len)

            def side(lanes):
                return jnp.concatenate([held(slot, lanes) for slot in slots], axis=0)

            logits = [dot_t(q_ref[rows, lanes], side(lanes)) for lanes in heads]
            tops = [jnp.max(part, axis=1, keepdims=True) for part in logits]
            weights = [jnp.exp((part - top) * HD ** (-0.5)) for part, top in zip(logits, tops)]
            scales = [1.0 / jnp.sum(part, axis=1, keepdims=True) for part in weights]
            mixed = [
                dot(part.astype(BF16), side(slice(cols + lanes.start, cols + lanes.stop)))
                for part, lanes in zip(weights, heads)
            ]
            for part, scale, lanes in zip(mixed, scales, heads):
                out_ref[at, i * span_len : (i + 1) * span_len, lanes] = (part * scale).astype(BF16)


def attend(slot, queries, ready, own, rest, weights, n_heads, n_rep, targets, fanout, spans):
    firsts = [0]
    for kv in ready:
        firsts.append(firsts[-1] + kv.shape[0])
    cols = queries.shape[1]
    rows = queries.shape[0] // (n_heads * n_rep)
    todo = isinstance(rest, list)
    slots, _, tokens, width = own[0].shape
    out_shape = [jax.ShapeDtypeStruct((len(targets), rows, cols), BF16)]
    if todo:
        others = sum(piece.shape[0] for piece in rest)
        out_shape.append(jax.ShapeDtypeStruct((slots, others, tokens, width), BF16))
    operands = [*rest, *weights] if todo else [rest]
    return pl.pallas_call(
        functools.partial(
            attend_kernel, firsts, len(own), n_heads, n_rep, targets, fanout, spans, len(rest) if todo else 0
        ),
        out_shape=out_shape,
        in_specs=[SMEM] + [VMEM] * (len(ready) + 1 + len(own) + len(operands)),
        out_specs=[VMEM] * len(out_shape),
        compiler_params=params(32),
        cost_estimate=cost(0.001),
        name="attend",
    )(slot, queries, *ready, *own, *operands)


def out_kernel(n_rep, n_received, *refs):
    mixed, weights, received = refs[:n_rep], refs[n_rep : 2 * n_rep], refs[2 * n_rep : 2 * n_rep + n_received]
    parts = [dot(a[0], w[...]) for a, w in zip(mixed, weights)] + [part[...].astype(F32) for part in received]
    refs[-1][...] = sum(parts).astype(BF16)


def out_project(mixed, weights, t, start, stop, tile, gflops, received=(), out=None, final=False):
    rows = (mixed[0].shape[1:] if mixed else received[0].shape)[0]
    base = start // tile
    n = len(mixed)
    operands = [*mixed, *weights, *received] + ([] if out is None else [out])
    width = (weights[0] if mixed else out).shape[1]
    return pl.pallas_call(
        functools.partial(out_kernel, n, len(received)),
        grid=((stop - start) // tile,),
        out_shape=jax.ShapeDtypeStruct((rows, width if final else stop - start), BF16),
        in_specs=[pl.BlockSpec((1, *a.shape[1:]), lambda j: (t, 0, 0)) for a in mixed]
        + [pl.BlockSpec((w.shape[0], tile), lambda j: (0, base + j)) for w in weights]
        + [pl.BlockSpec((rows, tile), lambda j: (0, j))] * len(received)
        + [ANY] * (out is not None),
        out_specs=pl.BlockSpec((rows, tile), lambda j: (0, (base if final else 0) + j)),
        input_output_aliases={} if out is None else {len(operands) - 1: 0},
        compiler_params=params(16),
        cost_estimate=cost(gflops),
        name="out_final" if final else "out_project",
    )(*operands)


def after(values, *earlier):
    return lax.optimization_barrier((values, earlier))[0]


def shards(queries, span_states, store, entry_ids, owners, w_key, w_value, w_out):
    n_lanes, n_heads, n_rep = (lax.axis_size(name) for name in ("lanes", "heads", "rep"))
    spans, fanout = entry_ids.shape
    requests = spans * fanout
    cap = max(2, (requests + n_lanes - 1) // n_lanes)
    span_len = queries.shape[0] // spans

    def over_heads(array):
        return [array] + [lax.ppermute(array, "heads", shift_pairs(n_heads, s)) for s in range(1, n_heads)]

    def over_rep(array):
        return [array] + [lax.ppermute(array, "rep", shift_pairs(n_rep, s)) for s in range(1, n_rep)]

    order = list(range(n_lanes))
    items = []
    for d in order[1:]:
        cuts = (0, cap // 2, cap) if d == 1 else (0, cap)
        items += [(d, low, high) for low, high in zip(cuts, cuts[1:])]
    size = max(1, -(-(len(items) - 2) // LATER_GROUPS))
    cuts = [0] + list(range(2, len(items), size)) + [len(items)]
    parts = [range(low, high) for low, high in zip(cuts, cuts[1:])]

    own = jnp.concatenate([owners.T, entry_ids.T], axis=0)
    req, slot, pick = plan(own, order, cap)
    tables = tables_of_lanes(own, n_lanes, req)
    encoded = encode_local(req, pick, span_states, store, cap, fanout, span_len)
    blocks = fetch(after(tables, encoded), store, items, cap, fanout)

    def send(part, *earlier):
        ready = after([blocks[i] for i in part], *earlier)
        return [
            lax.ppermute(block, "lanes", lane_pairs(n_lanes, items[i][0], True))
            for block, i in zip(ready, part)
        ]

    crossed, pieces = [over_heads(encoded)], []
    arrived = [None] + [send(part) for part in parts[:2]]
    last = blocks
    for i, part in enumerate(parts, 1):
        if i + 2 <= len(parts):
            arrived.append(send(parts[i + 1], arrived[i], last))
        first = items[part[0]][0] * cap + items[part[0]][1]
        encoded = encode(
            req, span_states, after(arrived[i], last), first, fanout, span_len, ENCODE_COST[i]
        )
        crossed.append(over_heads(encoded))
        last = encoded
        while i > 1 and len(pieces) < i:
            last = jnp.stack(after(crossed[len(pieces)], last))
            pieces.append(over_rep(last))
    w_outs = over_rep(w_out)
    kvs, last = [], after(last, w_outs)
    while len(kvs) < len(pieces):
        last = project(after(pieces[len(kvs)], last), w_key, w_value)
        kvs.append(last)
    local, *remote = crossed[-1]
    early = [piece[None] for piece in over_rep(after(local, kvs[0]))]
    last = project(after(early, last), w_key, w_value)
    own_kv = [last]
    remote = jnp.stack(after(remote, kvs, last))
    _, *rest = over_rep(remote)
    own_kv.append(project([remote], w_key, w_value))

    def mix(turns, q, rest):
        mixed = []
        for s in range(1, n_rep):
            given, *made = attend(
                slot, q, kvs, own_kv, rest, (w_key, w_value), n_heads, n_rep, [(t, s) for t in turns], fanout, spans
            )
            rest = made[0] if made else rest
            mixed.append(lax.ppermute(given, "rep", shift_pairs(n_rep, s)))
        kept = attend(
            slot, q, kvs, own_kv, rest, (w_key, w_value), n_heads, n_rep, [(t, 0) for t in turns], fanout, spans
        )
        return [kept[0]] + mixed, rest

    width = w_out.shape[1]
    tile = min(COL_TILE, width)
    cuts = [width // tile * part // 8 * tile for part in (0, 2, 4, 6, 7)] + [width]
    blocks = [(start, stop) for start, stop in zip(cuts, cuts[1:]) if stop > start]
    mixed, rest = mix(list(range(1, n_heads)), queries, rest)
    received, partials = [[] for _ in blocks], []
    for t in range(1, n_heads):
        for i, (start, stop) in enumerate(blocks):
            partial = out_project(mixed, w_outs, t - 1, start, stop, tile, 0.001)
            partial, mixed = lax.optimization_barrier((partial, mixed))
            partials.append(partial)
            received[i].append(lax.ppermute(partial, "heads", shift_pairs(n_heads, t)))
    mixed, rest = mix([0], after(queries, partials), rest)
    out, ahead = None, out_project(mixed, w_outs, 0, *blocks[-1], tile, 0.001)
    for i, ((start, stop), parts) in enumerate(zip(blocks, received)):
        if i + 1 < len(blocks):
            out = out_project(mixed, w_outs, 0, start, stop, tile, 0.2, parts, out, True)
        else:
            out = out_project([], [], 0, start, stop, tile, 0.2, [ahead, *parts], out, True)
    return out


def solution(mesh):
    return jax.shard_map(
        shards,
        mesh=mesh,
        in_specs=(
            P(("groups", "lanes"), ("heads", "rep")),
            P(("groups", "lanes"), None),
            P(("groups", "lanes"), ("heads", "rep"), None),
            P(("groups", "lanes"), None),
            P(("groups", "lanes"), None),
            P(None, ("heads", "rep")),
            P(None, ("heads", "rep")),
            P(("heads", "rep"), None),
        ),
        out_specs=P(("groups", "lanes", "heads", "rep"), None),
        check_vma=False,
    )
```

```python
import functools

import jax
import jax.numpy as jnp
from jax import lax
from jax.experimental import pallas as pl
from jax.experimental.pallas import tpu as pltpu
from jax.sharding import PartitionSpec as P

HD = 128
ENCODER_HEAD_DIM = 128
F32 = jnp.float32
BF16 = jnp.bfloat16
LATER_GROUPS = 2
COL_TILE = 512
ENCODE_COST = (None, 0.1, 10, 10)

VMEM = pl.BlockSpec(memory_space=pltpu.VMEM)
SMEM = pl.BlockSpec(memory_space=pltpu.SMEM)
ANY = pl.BlockSpec(memory_space=pl.ANY)


def params(mib):
    return pltpu.CompilerParams(vmem_limit_bytes=mib * 2**20)


def cost(gflops):
    return pl.CostEstimate(flops=int(gflops * 10**9), bytes_accessed=1024, transcendentals=0)


def apart(n, a, b):
    if n & (n - 1) == 0:
        return a ^ b
    return lax.rem(b - a + n, n)


def lane_pairs(n, d, reply):
    if n & (n - 1) == 0:
        return [(i, i ^ d) for i in range(n)]
    return [(i, (i - d if reply else i + d) % n) for i in range(n)]


def tables_of_lanes(own, n, meanwhile):
    if n & (n - 1):
        others = [lax.ppermute(own, "lanes", lane_pairs(n, d, False)) for d in range(1, n)]
        return jnp.concatenate([own] + others, axis=0)
    step, held = 1, own
    while step < n:
        other = lax.ppermute(held, "lanes", lane_pairs(n, step, False))
        held = jnp.concatenate(after([held, other], meanwhile if step == 1 else ()), axis=0)
        step *= 2
    return held


def shift_pairs(n, s):
    return [(i, (i + s) % n) for i in range(n)]


def dot_t(a, b):
    return lax.dot_general(a, b, (((1,), (1,)), ((), ())), preferred_element_type=F32)


def dot(a, b):
    return jnp.dot(a, b, preferred_element_type=F32)


def plan_kernel(order, cap, own_ref, req_ref, slot_ref, pick_ref, next_ref):
    n_lanes = len(order)
    lane = lax.axis_index("lanes")
    fanout, spans = own_ref.shape[0] // 2, own_ref.shape[1]
    for i, d in enumerate(order):
        next_ref[d] = i * cap
    for i in range(n_lanes * cap):
        pick_ref[i] = 0
        req_ref[i] = 0
    for j in range(fanout * spans):
        span, k = j // fanout, j % fanout
        d = apart(n_lanes, lane, own_ref[k, span])
        slot = next_ref[d]
        next_ref[d] = slot + 1
        pick_ref[slot] = own_ref[fanout + k, span]
        req_ref[slot] = j
        slot_ref[j] = slot


def plan(own, order, cap):
    table = jax.ShapeDtypeStruct((len(order) * cap,), jnp.int32)
    return pl.pallas_call(
        functools.partial(plan_kernel, order, cap),
        out_shape=(table, jax.ShapeDtypeStruct((own.size // 2,), jnp.int32), table),
        in_specs=[SMEM],
        out_specs=(SMEM, SMEM, SMEM),
        scratch_shapes=[pltpu.SMEM((len(order),), jnp.int32)],
        compiler_params=params(16),
        cost_estimate=cost(10),
        name="plan",
    )(own)


def fetch_kernel(items, cap, fanout, tables_ref, store_ref, *refs):
    blocks, pick_ref = refs[:-1], refs[-1]
    lane = lax.axis_index("lanes")
    spans = tables_ref.shape[1]
    others = tables_ref.shape[0] // (2 * fanout) - 1
    for i in range(others * cap):
        pick_ref[i] = 0
    for d in range(others):
        place, row = d * cap, (d + 1) * 2 * fanout
        for span in range(spans):
            for k in range(fanout):
                pick_ref[place] = tables_ref[row + fanout + k, span]
                place = place + (tables_ref[row + k, span] == lane).astype(jnp.int32)
    for block, (d, low, high) in zip(blocks, items):
        for s in range(low, high):
            block[s - low] = store_ref[pick_ref[(d - 1) * cap + s]]


def fetch(tables, store, items, cap, fanout):
    others = tables.shape[0] // (2 * fanout) - 1
    return pl.pallas_call(
        functools.partial(fetch_kernel, items, cap, fanout),
        out_shape=[
            jax.ShapeDtypeStruct((high - low,) + store.shape[1:], store.dtype) for _, low, high in items
        ],
        in_specs=[SMEM, VMEM],
        out_specs=[VMEM] * len(items),
        scratch_shapes=[pltpu.SMEM((others * cap + 1,), jnp.int32)],
        compiler_params=params(16),
        cost_estimate=cost(10),
        name="fetch",
    )(tables, store)


def encode_pairs(width):
    step = 2 * ENCODER_HEAD_DIM
    return [(start, min(start + step, width)) for start in range(0, width, step)]


def spread(states, start, stop):
    part = states[:, start:stop]
    heads = (stop - start) // ENCODER_HEAD_DIM
    if heads == 1:
        return part
    rows = jnp.concatenate([part] * heads, axis=0)
    return jnp.where(own_cells(rows.shape, part.shape[0]), rows, jnp.zeros_like(rows))


def own_cells(shape, keys):
    row = lax.broadcasted_iota(jnp.int32, shape, 0)
    col = lax.broadcasted_iota(jnp.int32, shape, 1)
    return (row >= keys) == (col >= ENCODER_HEAD_DIM)


def softmax_top(logits, keys):
    if logits.shape[1] == keys:
        return jnp.max(logits, axis=1, keepdims=True)
    first = lax.broadcasted_iota(jnp.int32, logits.shape, 1) < keys
    low = jnp.max(jnp.where(first, logits, -jnp.inf), axis=1, keepdims=True)
    high = jnp.max(jnp.where(first, -jnp.inf, logits), axis=1, keepdims=True)
    return jnp.where(first, low, high)


def encode_block(block, out_ref, first, req_ref, states_ref, fanout, span_len):
    scale = ENCODER_HEAD_DIM ** (-0.5)
    runs = encode_pairs(states_ref.shape[1])
    units = []
    for s in range(block.shape[0]):
        span = lax.div(req_ref[first + s], fanout)
        states = states_ref[pl.ds(pl.multiple_of(span * span_len, span_len), span_len), :]
        units += [(s, start, stop, spread(states, start, stop)) for start, stop in runs]
    logits = [dot_t(block[s, :, start:stop], keys) for s, start, stop, keys in units]
    tops = [softmax_top(part, span_len) for part in logits]
    weights = [jnp.exp((part - top) * scale).astype(BF16) for part, top in zip(logits, tops)]
    mixed = [dot(part, keys) for part, (_, _, _, keys) in zip(weights, units)]
    sums = []
    for part, (_, start, stop, keys) in zip(weights, units):
        ones = jnp.ones(keys.shape, BF16)
        if stop - start > ENCODER_HEAD_DIM:
            ones = jnp.where(own_cells(keys.shape, span_len), ones, jnp.zeros_like(ones))
        sums.append(dot(part, ones))
    for (s, start, stop, _), top, bottom in zip(units, mixed, sums):
        token = block[s, :, start:stop].astype(F32)
        out_ref[s, :, start:stop] = (token + top / bottom).astype(BF16)


def encode_kernel(first, fanout, span_len, req_ref, states_ref, *refs):
    blocks, out_ref = refs[:-1], refs[-1]
    at = 0
    for block in blocks:
        stop = at + block.shape[0]
        encode_block(block, out_ref.at[at:stop], first + at, req_ref, states_ref, fanout, span_len)
        at = stop


def encode(req, span_states, blocks, first, fanout, span_len, gflops):
    slots = sum(block.shape[0] for block in blocks)
    return pl.pallas_call(
        functools.partial(encode_kernel, first, fanout, span_len),
        out_shape=jax.ShapeDtypeStruct((slots,) + blocks[0].shape[1:], BF16),
        in_specs=[SMEM, VMEM] + [VMEM] * len(blocks),
        out_specs=VMEM,
        compiler_params=params(16),
        cost_estimate=cost(gflops),
        name="encode",
    )(req, span_states, *blocks)


def encode_local_kernel(fanout, span_len, req_ref, pick_ref, states_ref, store_ref, out_ref, tokens_ref):
    for s in range(out_ref.shape[0]):
        tokens_ref[s] = store_ref[pick_ref[s]]
    encode_block(tokens_ref, out_ref, 0, req_ref, states_ref, fanout, span_len)


def encode_local(req, pick, span_states, store, cap, fanout, span_len):
    block = (cap,) + store.shape[1:]
    return pl.pallas_call(
        functools.partial(encode_local_kernel, fanout, span_len),
        out_shape=jax.ShapeDtypeStruct(block, BF16),
        in_specs=[SMEM, SMEM, VMEM, VMEM],
        out_specs=VMEM,
        scratch_shapes=[pltpu.VMEM(block, BF16)],
        compiler_params=params(16),
        cost_estimate=cost(10),
        name="encode_local",
    )(req, pick, span_states, store)


def project_into(kv_ref, first, pieces, wk_ref, wv_ref):
    n, slots, tokens, width = pieces[0].shape
    rows = jnp.concatenate([piece[...].reshape(n * slots * tokens, width) for piece in pieces], axis=0)
    cols = wk_ref.shape[1]
    for side, weight in enumerate((wk_ref, wv_ref)):
        made = dot(rows, weight[...]).astype(BF16)
        for p in range(n * len(pieces)):
            part = made[p * slots * tokens : (p + 1) * slots * tokens]
            kv_ref[first : first + slots, p, :, side * cols : (side + 1) * cols] = part.reshape(
                slots, tokens, cols
            )


def project_kernel(n_pieces, *refs):
    pieces, (wk_ref, wv_ref, kv_ref) = refs[:-3], refs[-3:]
    first = 0
    for at in range(0, len(pieces), n_pieces):
        project_into(kv_ref, first, pieces[at : at + n_pieces], wk_ref, wv_ref)
        first += pieces[at].shape[1]


def project(pieces, w_key, w_value, n_groups=1):
    n_pieces = len(pieces) // n_groups
    n, _, tokens, _ = pieces[0].shape
    slots = sum(piece.shape[1] for piece in pieces[::n_pieces])
    shape = (slots, n * n_pieces, tokens, 2 * w_key.shape[1])
    return pl.pallas_call(
        functools.partial(project_kernel, n_pieces),
        out_shape=jax.ShapeDtypeStruct(shape, BF16),
        in_specs=[VMEM] * (len(pieces) + 2),
        out_specs=VMEM,
        compiler_params=params(32),
        cost_estimate=cost(10),
        name="project",
    )(*pieces, w_key, w_value)


def attend_kernel(firsts, n_own, n_heads, n_rep, targets, fanout, spans, n_rest, slot_ref, q_ref, *refs):
    ready, refs = refs[: len(firsts) - 1], refs[len(firsts) - 1 :]
    own, refs = refs[:n_own], refs[n_own:]
    if n_rest:
        pieces, (wk_ref, wv_ref, out_ref, rest_ref) = refs[:n_rest], refs[n_rest:]
        project_into(rest_ref, 0, pieces, wk_ref, wv_ref)
    else:
        rest_ref, out_ref = refs
    heads_at, rep_at = lax.axis_index("heads"), lax.axis_index("rep")
    cols = q_ref.shape[1]
    span_len = q_ref.shape[0] // spans
    block = spans // (n_heads * n_rep)

    def place(slot, first, count):
        return jnp.clip(slot - first, 0, count - 1)

    def held(slot, lanes):
        at = place(slot, firsts[-1], rest_ref.shape[0])
        value = jnp.concatenate([ref[at, :, :, lanes] for ref in (*own, rest_ref)], axis=0)
        for ref, first in reversed(list(zip(ready, firsts))):
            there = slot < first + ref.shape[0]
            value = jnp.where(there, ref[place(slot, first, ref.shape[0]), :, :, lanes], value)
        return value.reshape(-1, HD)

    heads = [slice(h * HD, (h + 1) * HD) for h in range(cols // HD)]
    for at, (t, s) in enumerate(targets):
        owner = lax.rem(heads_at + t, n_heads) * n_rep + lax.rem(rep_at + s, n_rep)
        for i in range(block):
            span = owner * block + i
            slots = [slot_ref[span * fanout + k] for k in range(fanout)]
            rows = pl.ds(pl.multiple_of(span * span_len, span_len), span_len)

            def side(lanes):
                return jnp.concatenate([held(slot, lanes) for slot in slots], axis=0)

            logits = [dot_t(q_ref[rows, lanes], side(lanes)) for lanes in heads]
            tops = [jnp.max(part, axis=1, keepdims=True) for part in logits]
            weights = [jnp.exp((part - top) * HD ** (-0.5)) for part, top in zip(logits, tops)]
            scales = [1.0 / jnp.sum(part, axis=1, keepdims=True) for part in weights]
            mixed = [
                dot(part.astype(BF16), side(slice(cols + lanes.start, cols + lanes.stop)))
                for part, lanes in zip(weights, heads)
            ]
            for part, scale, lanes in zip(mixed, scales, heads):
                out_ref[at, i * span_len : (i + 1) * span_len, lanes] = (part * scale).astype(BF16)


def attend(slot, queries, ready, own, rest, weights, n_heads, n_rep, targets, fanout, spans):
    firsts = [0]
    for kv in ready:
        firsts.append(firsts[-1] + kv.shape[0])
    cols = queries.shape[1]
    rows = queries.shape[0] // (n_heads * n_rep)
    todo = isinstance(rest, list)
    slots, _, tokens, width = own[0].shape
    out_shape = [jax.ShapeDtypeStruct((len(targets), rows, cols), BF16)]
    if todo:
        others = sum(piece.shape[0] for piece in rest)
        out_shape.append(jax.ShapeDtypeStruct((slots, others, tokens, width), BF16))
    operands = [*rest, *weights] if todo else [rest]
    return pl.pallas_call(
        functools.partial(
            attend_kernel, firsts, len(own), n_heads, n_rep, targets, fanout, spans, len(rest) if todo else 0
        ),
        out_shape=out_shape,
        in_specs=[SMEM] + [VMEM] * (len(ready) + 1 + len(own) + len(operands)),
        out_specs=[VMEM] * len(out_shape),
        compiler_params=params(32),
        cost_estimate=cost(0.001),
        name="attend",
    )(slot, queries, *ready, *own, *operands)


def out_kernel(n_rep, n_received, *refs):
    mixed, weights, received = refs[:n_rep], refs[n_rep : 2 * n_rep], refs[2 * n_rep : 2 * n_rep + n_received]
    parts = [dot(a[0], w[...]) for a, w in zip(mixed, weights)] + [part[...].astype(F32) for part in received]
    refs[-1][...] = sum(parts).astype(BF16)


def out_project(mixed, weights, t, start, stop, tile, gflops, received=(), out=None, final=False):
    rows = (mixed[0].shape[1:] if mixed else received[0].shape)[0]
    base = start // tile
    n = len(mixed)
    operands = [*mixed, *weights, *received] + ([] if out is None else [out])
    width = (weights[0] if mixed else out).shape[1]
    return pl.pallas_call(
        functools.partial(out_kernel, n, len(received)),
        grid=((stop - start) // tile,),
        out_shape=jax.ShapeDtypeStruct((rows, width if final else stop - start), BF16),
        in_specs=[pl.BlockSpec((1, *a.shape[1:]), lambda j: (t, 0, 0)) for a in mixed]
        + [pl.BlockSpec((w.shape[0], tile), lambda j: (0, base + j)) for w in weights]
        + [pl.BlockSpec((rows, tile), lambda j: (0, j))] * len(received)
        + [ANY] * (out is not None),
        out_specs=pl.BlockSpec((rows, tile), lambda j: (0, (base if final else 0) + j)),
        input_output_aliases={} if out is None else {len(operands) - 1: 0},
        compiler_params=params(16),
        cost_estimate=cost(gflops),
        name="out_final" if final else "out_project",
    )(*operands)


def after(values, *earlier):
    return lax.optimization_barrier((values, earlier))[0]


def shards(queries, span_states, store, entry_ids, owners, w_key, w_value, w_out):
    n_lanes, n_heads, n_rep = (lax.axis_size(name) for name in ("lanes", "heads", "rep"))
    spans, fanout = entry_ids.shape
    requests = spans * fanout
    cap = max(2, (requests + n_lanes - 1) // n_lanes)
    span_len = queries.shape[0] // spans

    def over_heads(array):
        return [array] + [lax.ppermute(array, "heads", shift_pairs(n_heads, s)) for s in range(1, n_heads)]

    def over_rep(array):
        return [array] + [lax.ppermute(array, "rep", shift_pairs(n_rep, s)) for s in range(1, n_rep)]

    order = list(range(n_lanes))
    items = []
    for d in order[1:]:
        cuts = (0, cap // 2, cap) if d == 1 else (0, cap)
        items += [(d, low, high) for low, high in zip(cuts, cuts[1:])]
    size = max(1, -(-(len(items) - 2) // LATER_GROUPS))
    cuts = [0] + list(range(2, len(items), size)) + [len(items)]
    parts = [range(low, high) for low, high in zip(cuts, cuts[1:])]

    own = jnp.concatenate([owners.T, entry_ids.T], axis=0)
    req, slot, pick = plan(own, order, cap)
    tables = tables_of_lanes(own, n_lanes, req)
    encoded = encode_local(req, pick, span_states, store, cap, fanout, span_len)
    blocks = fetch(after(tables, encoded), store, items, cap, fanout)

    def send(part, *earlier):
        ready = after([blocks[i] for i in part], *earlier)
        return [
            lax.ppermute(block, "lanes", lane_pairs(n_lanes, items[i][0], True))
            for block, i in zip(ready, part)
        ]

    crossed, pieces = [over_heads(encoded)], []
    arrived = [None] + [send(part) for part in parts[:2]]
    last = blocks
    for i, part in enumerate(parts, 1):
        if i + 2 <= len(parts):
            arrived.append(send(parts[i + 1], arrived[i], last))
        first = items[part[0]][0] * cap + items[part[0]][1]
        encoded = encode(
            req, span_states, after(arrived[i], last), first, fanout, span_len, ENCODE_COST[i]
        )
        crossed.append(over_heads(encoded))
        last = encoded
        while i > 1 and len(pieces) < i:
            last = jnp.stack(after(crossed[len(pieces)], last))
            pieces.append(over_rep(last))
    w_outs = over_rep(w_out)
    kvs, last = [], after(last, w_outs)
    for some in (pieces[:2], pieces[2:]):
        if some:
            last = project(after(sum(some, []), last), w_key, w_value, len(some))
            kvs.append(last)
    local, *remote = crossed[-1]
    early = [piece[None] for piece in over_rep(after(local, kvs[0]))]
    last = project(after(early, last), w_key, w_value)
    own_kv = [last]
    remote = jnp.stack(after(remote, kvs, last))
    _, *rest = over_rep(remote)
    own_kv.append(project([remote], w_key, w_value))

    def mix(turns, q, rest):
        mixed = []
        for s in range(1, n_rep):
            given, *made = attend(
                slot, q, kvs, own_kv, rest, (w_key, w_value), n_heads, n_rep, [(t, s) for t in turns], fanout, spans
            )
            rest = made[0] if made else rest
            mixed.append(lax.ppermute(given, "rep", shift_pairs(n_rep, s)))
        kept = attend(
            slot, q, kvs, own_kv, rest, (w_key, w_value), n_heads, n_rep, [(t, 0) for t in turns], fanout, spans
        )
        return [kept[0]] + mixed, rest

    width = w_out.shape[1]
    tile = min(COL_TILE, width)
    cuts = [width // tile * part // 8 * tile for part in (0, 2, 4, 6, 7)] + [width]
    blocks = [(start, stop) for start, stop in zip(cuts, cuts[1:]) if stop > start]
    mixed, rest = mix(list(range(1, n_heads)), queries, rest)
    received, partials = [[] for _ in blocks], []
    for t in range(1, n_heads):
        for i, (start, stop) in enumerate(blocks):
            partial = out_project(mixed, w_outs, t - 1, start, stop, tile, 0.001)
            partial, mixed = lax.optimization_barrier((partial, mixed))
            partials.append(partial)
            received[i].append(lax.ppermute(partial, "heads", shift_pairs(n_heads, t)))
    mixed, rest = mix([0], after(queries, partials), rest)
    out, ahead = None, out_project(mixed, w_outs, 0, *blocks[-1], tile, 0.001)
    for i, ((start, stop), parts) in enumerate(zip(blocks, received)):
        if i + 1 < len(blocks):
            out = out_project(mixed, w_outs, 0, start, stop, tile, 0.2, parts, out, True)
        else:
            out = out_project([], [], 0, start, stop, tile, 0.2, [ahead, *parts], out, True)
    return out


def solution(mesh):
    return jax.shard_map(
        shards,
        mesh=mesh,
        in_specs=(
            P(("groups", "lanes"), ("heads", "rep")),
            P(("groups", "lanes"), None),
            P(("groups", "lanes"), ("heads", "rep"), None),
            P(("groups", "lanes"), None),
            P(("groups", "lanes"), None),
            P(None, ("heads", "rep")),
            P(None, ("heads", "rep")),
            P(("heads", "rep"), None),
        ),
        out_specs=P(("groups", "lanes", "heads", "rep"), None),
        check_vma=False,
    )
```
